32 devices in a mesh: depth: 8 (over z, y), rows: 4 (over x, core).
Axes of the slice: x: 2, y: 2, z: 4, core: 2. Of those that a mesh axis runs over, the one named last changes fastest.
Arguments:
- density: float32 [16, 512, 512], P('depth', 'rows'), may hold values from 0 to 6
- transfer_table: float32 [4, 16], replicated, may hold values from 0.2 to 1
Outputs:
- picture: float32 [4, 512, 512], P(None, ('rows', 'depth'))
The draws below stay inside these ranges and needn't reach their ends.
All inputs are finite; a program needn't handle non-finite values.
Results may differ from the reference program's by a relative error of at most 0.000021.
Values sent between devices are 32-bit elements; how exact they have to be, the bound alone decides.
A program may use at most 64 MiB of HBM per device.

```python
import jax
import jax.numpy as jnp
from jax import lax

NX = 512
PASSES = 3
KNOTS = 16
NZ = 16
NY = 512


def draw_density(key, part):
    normals = jax.random.normal(key, (NZ, NY, NX), jnp.float32)
    values = jnp.exp(0.5 * normals)
    return jnp.clip(values, 0.05, 5.9)


def setup_inputs(seed: int = 0) -> dict:
    splits = jax.random.split(jax.random.key(seed), 3)
    density = draw_density(jax.random.fold_in(splits[2], 71), 0)
    transfer_table = jnp.clip(jax.random.uniform(splits[1], (4, KNOTS), jnp.float32, 0.2, 1.0), 0.2, 1.0)
    return {"density": density, "transfer_table": transfer_table}


TIME_STEP = 0.15
OPTICAL_DEPTH = 3.0
UPPER_DENSITY = 6.0
AMBIENT = 0.35

def diffusion_flux(center, neighbours):
    summed = jnp.zeros_like(center)
    for other in neighbours:
        change = other - center
        summed = summed + change / (1.0 + change * change)
    return center + TIME_STEP * summed

def appearance(center, neighbours, transfer_table, depth_count):
    deeper, nearer, next_row, prev_row, next_col, prev_col = neighbours
    grad_depth = (deeper - nearer) * 0.5
    grad_row = (next_row - prev_row) * 0.5
    grad_col = (next_col - prev_col) * 0.5
    shading = AMBIENT + (1.0 - AMBIENT) * jnp.abs(0.64 * grad_depth + 0.6 * grad_row + 0.48 * grad_col) / jnp.sqrt(grad_depth * grad_depth + grad_row * grad_row + grad_col * grad_col + 0.25)
    position = center * ((KNOTS - 1) / UPPER_DENSITY)
    mixed = [jnp.zeros_like(center) for channel in range(4)]
    for knot in range(KNOTS):
        hat_weight = jnp.maximum(0.0, 1.0 - jnp.abs(position - knot))
        mixed = [mixed[channel] + transfer_table[channel, knot] * hat_weight for channel in range(4)]
    opacity = 1.0 - jnp.exp(-mixed[3] * (OPTICAL_DEPTH / depth_count))
    colors = jnp.stack([mixed[0] * shading, mixed[1] * shading, mixed[2] * shading])
    return (colors, opacity)

def plane_sides(window):
    center = window[1]
    rows_pad = jnp.pad(center, ((1, 1), (0, 0)), mode='edge')
    cols_pad = jnp.pad(center, ((0, 0), (1, 1)), mode='edge')
    return (window[2], window[0], rows_pad[2:], rows_pad[:-2], cols_pad[:, 2:], cols_pad[:, :-2])

def reference(density, transfer_table):
    field = density
    planes = jnp.arange(NZ, dtype=jnp.int32)
    for sweep in range(PASSES):
        padded = jnp.pad(field, ((1, 1), (0, 0), (0, 0)), mode='edge')

        def one_plane(index):
            window = lax.dynamic_slice_in_dim(padded, index, 3, 0)
            return diffusion_flux(window[1], plane_sides(window))
        field = lax.map(one_plane, planes)
    padded = jnp.pad(field, ((1, 1), (0, 0), (0, 0)), mode='edge')

    def advance(carry, index):
        color_sum, remaining = carry
        window = lax.dynamic_slice_in_dim(padded, index, 3, 0)
        colors, opacity = appearance(window[1], plane_sides(window), transfer_table, NZ)
        color_sum = color_sum + remaining * opacity * colors
        remaining = remaining * (1.0 - opacity)
        return ((color_sum, remaining), None)
    start = (jnp.zeros((3, NY, NX), jnp.float32), jnp.ones((NY, NX), jnp.float32))
    (color_sum, remaining), unused = lax.scan(advance, start, planes)
    return jnp.concatenate([color_sum, (1.0 - remaining)[None]], axis=0)
```

```python
import functools

import jax
import jax.numpy as jnp
from jax import lax
from jax.experimental import pallas as pl
from jax.experimental.pallas import tpu as pltpu
from jax.sharding import PartitionSpec as P

PASSES = 3
KNOTS = 16


TIME_STEP = 0.15
OPTICAL_DEPTH = 3.0
UPPER_DENSITY = 6.0
AMBIENT = 0.35


def extended(cells, sides, width):
    for axis, dim in sides:
        count = lax.axis_size(axis)
        ends = count - 1
        head = lax.slice_in_dim(cells, 0, width, axis=dim)
        tail = lax.slice_in_dim(cells, cells.shape[dim] - width, cells.shape[dim], axis=dim)
        cells = jnp.concatenate(
            [
                lax.ppermute(tail, axis, [(i, (i + 1) % count) for i in range(ends)]),
                cells,
                lax.ppermute(head, axis, [((i + 1) % count, i) for i in range(ends)]),
            ],
            axis=dim,
        )
    return cells


def partner(value, axis, stride):
    mask = 2**stride
    pairs = [(source, source ^ mask) for source in range(lax.axis_size(axis))]
    return lax.ppermute(value, axis, pairs)


def diffusion_flux(center, neighbours):
    summed = jnp.zeros_like(center)
    for other in neighbours:
        change = other - center
        summed = summed + change / (1.0 + change * change)
    return center + TIME_STEP * summed


def appearance(center, neighbours, transfer_table, depth_count):
    deeper, nearer, next_row, prev_row, next_col, prev_col = neighbours
    grad_depth = (deeper - nearer) * 0.5
    grad_row = (next_row - prev_row) * 0.5
    grad_col = (next_col - prev_col) * 0.5
    shading = AMBIENT + (1.0 - AMBIENT) * jnp.abs(
        0.64 * grad_depth + 0.6 * grad_row + 0.48 * grad_col
    ) / jnp.sqrt(grad_depth * grad_depth + grad_row * grad_row + grad_col * grad_col + 0.25)
    position = center * ((KNOTS - 1) / UPPER_DENSITY)
    mixed = [jnp.zeros_like(center) for channel in range(4)]
    for knot in range(KNOTS):
        hat_weight = jnp.maximum(0.0, 1.0 - jnp.abs(position - knot))
        mixed = [
            mixed[channel] + transfer_table[channel, knot] * hat_weight for channel in range(4)
        ]
    opacity = 1.0 - jnp.exp(-mixed[3] * (OPTICAL_DEPTH / depth_count))
    colors = jnp.stack([mixed[0] * shading, mixed[1] * shading, mixed[2] * shading])
    return (colors, opacity)


def neighbour_fields(field):
    padded = extended(field, (("depth", 0), ("rows", 1)), 1)
    depth_index = lax.axis_index("depth")
    depth_count = lax.axis_size("depth")
    rows_index = lax.axis_index("rows")
    rows_count = lax.axis_size("rows")
    above = jnp.where(depth_index == 0, field[:1], padded[:1, 1:-1])
    below = jnp.where(depth_index == depth_count - 1, field[-1:], padded[-1:, 1:-1])
    first_row = jnp.where(rows_index == 0, field[:, :1], padded[1:-1, :1])
    last_row = jnp.where(rows_index == rows_count - 1, field[:, -1:], padded[1:-1, -1:])
    deeper = jnp.concatenate([field[1:], below], axis=0)
    nearer = jnp.concatenate([above, field[:-1]], axis=0)
    next_row = jnp.concatenate([field[:, 1:], last_row], axis=1)
    prev_row = jnp.concatenate([first_row, field[:, :-1]], axis=1)
    next_col = jnp.concatenate([field[:, :, 1:], field[:, :, -1:]], axis=2)
    prev_col = jnp.concatenate([field[:, :, :1], field[:, :, :-1]], axis=2)
    return (deeper, nearer, next_row, prev_row, next_col, prev_col)


def composite(front_part, back_part):
    return front_part + (1.0 - front_part[3:4]) * back_part


def per_device(density, transfer_table):
    planes_here = density.shape[0]
    band_rows = density.shape[1]
    columns = density.shape[2]
    depth_count = lax.axis_size("depth")
    depth_index = lax.axis_index("depth")
    total_planes = planes_here * depth_count
    field = density
    for sweep in range(PASSES):
        field = diffusion_flux(field, neighbour_fields(field))
    colors, opacity = appearance(field, neighbour_fields(field), transfer_table, total_planes)
    color_sum = jnp.zeros((3, band_rows, columns), jnp.float32)
    remaining = jnp.ones((band_rows, columns), jnp.float32)
    for plane in range(planes_here):
        color_sum = color_sum + remaining * opacity[plane] * colors[:, plane]
        remaining = remaining * (1.0 - opacity[plane])
    partial_value = jnp.concatenate([color_sum, (1.0 - remaining)[None]], axis=0)
    strip_rows = band_rows // depth_count
    current = partial_value.reshape(4, depth_count, strip_rows, columns)
    levels = depth_count.bit_length() - 1
    for bit in range(levels):
        blocks = current.shape[1]
        paired = current.reshape(4, blocks // 2, 2, strip_rows, columns)
        own_bit = depth_index // 2**bit % 2
        kept_half = jnp.where(own_bit == 0, paired[:, :, 0], paired[:, :, 1])
        sent_half = jnp.where(own_bit == 0, paired[:, :, 1], paired[:, :, 0])
        received = partner(sent_half, "depth", bit)
        front_part = jnp.where(own_bit == 0, kept_half, received)
        back_part = jnp.where(own_bit == 0, received, kept_half)
        current = composite(front_part, back_part)
    return current.reshape(4, strip_rows, columns)


HALO = PASSES + 1
TILE = 8


def flux(change):
    denominator = 1.0 + change * change
    guess = pl.reciprocal(denominator, approx=True)
    return change * (guess * (2.0 - denominator * guess))


def roll(cells, shift, axis):
    return pltpu.roll(cells, shift % cells.shape[axis], axis)


def volume_kernel(
    depth_count,
    rows_count,
    density,
    table,
    picture,
    local,
    field,
    halo,
    edges,
    load_sem,
    send,
    recv,
    halo_send,
    halo_recv,
    edge_send,
    edge_recv,
):
    planes, band, columns = local.shape
    strip = band // depth_count
    total_planes = planes * depth_count
    tall = strip + TILE
    d = lax.axis_index("depth")
    r = lax.axis_index("rows")
    next_rows = lax.rem(r + 1, rows_count)
    prev_rows = lax.rem(r + rows_count - 1, rows_count)

    load = pltpu.make_async_copy(density, local, load_sem)
    load.start()

    barrier = pltpu.get_barrier_semaphore()

    def greet(depth, rows):
        pl.semaphore_signal(
            barrier, inc=1, device_id=(depth, rows), device_id_type=pl.DeviceIdType.MESH
        )

    for k in range(1, depth_count):
        greet(lax.rem(d + k, depth_count), r)

    @pl.when(d == 0)
    def _():
        for s in range(depth_count):
            greet(s, prev_rows)

    @pl.when(d == depth_count - 1)
    def _():
        for s in range(depth_count):
            greet(s, next_rows)

    load.wait()
    for p in range(planes):
        first = local[p, :TILE, :]
        final = local[p, band - TILE :, :]
        edges[depth_count, p] = jnp.concatenate([first[:HALO], final[HALO:]], axis=0)
        for s in range(depth_count):
            if s == 0:
                before = jnp.concatenate(
                    [first[HALO - 1 - i : HALO - i] for i in range(HALO)], axis=0
                )
            else:
                before = local[p, s * strip - TILE : s * strip, :][HALO:]
            if s == depth_count - 1:
                after = jnp.concatenate(
                    [final[TILE - 1 - i : TILE - i] for i in range(HALO)], axis=0
                )
            else:
                after = local[p, (s + 1) * strip : (s + 1) * strip + TILE, :][:HALO]
            halo[s, p] = jnp.concatenate([after, before], axis=0)

    def main_copy(peer, slot):
        return pltpu.make_async_remote_copy(
            src_ref=local.at[:, pl.ds(pl.multiple_of(peer * strip, TILE), strip), :],
            dst_ref=field.at[pl.ds(d * planes, planes), pl.ds(0, strip), :],
            send_sem=send.at[slot],
            recv_sem=recv.at[d],
            device_id=(peer, r),
            device_id_type=pl.DeviceIdType.MESH,
        )

    def halo_copy(peer, slot):
        return pltpu.make_async_remote_copy(
            src_ref=halo.at[peer],
            dst_ref=field.at[pl.ds(d * planes, planes), pl.ds(strip, TILE), :],
            send_sem=halo_send.at[slot],
            recv_sem=halo_recv.at[d],
            device_id=(peer, r),
            device_id_type=pl.DeviceIdType.MESH,
        )

    def edge_copy(depth, rows, slot):
        return pltpu.make_async_remote_copy(
            src_ref=edges.at[depth_count],
            dst_ref=edges.at[d],
            send_sem=edge_send.at[slot],
            recv_sem=edge_recv.at[d],
            device_id=(depth, rows),
            device_id_type=pl.DeviceIdType.MESH,
        )

    def edge_copies():
        return (
            edge_copy(depth_count - 1, prev_rows, 0),
            edge_copy(0, next_rows, 1),
        )

    def landing(ref, sem):
        return pltpu.make_async_copy(ref, ref, sem)

    pl.semaphore_wait(barrier, depth_count + 1)
    order = sorted(range(1, depth_count), key=lambda k: abs(k - depth_count // 2))

    for copy in edge_copies():
        copy.start()

    for k in order:
        peer = lax.rem(d + k, depth_count)
        main_copy(peer, k).start()
        halo_copy(peer, k).start()

    own = pl.multiple_of(d * strip, TILE)
    for p in range(planes):
        field[d * planes + p, 0:strip, :] = local[p, pl.ds(own, strip), :]
        field[d * planes + p, strip:, :] = halo[d, p]

    for k in order:
        source = lax.rem(d + k, depth_count)
        here = pl.ds(source * planes, planes)
        landing(field.at[here, pl.ds(0, strip), :], recv.at[source]).wait()
        landing(field.at[here, pl.ds(strip, TILE), :], halo_recv.at[source]).wait()

    upper = lax.broadcasted_iota(jnp.int32, (TILE, columns), 0) < HALO

    def merge(replaced):
        for s in range(depth_count):
            landing(edges.at[s], edge_recv.at[s]).wait()
            for p in range(planes):
                z = s * planes + p
                field[z, strip:, :] = jnp.where(replaced, edges[s, p], field[z, strip:, :])

    @pl.when(d == 0)
    def _():
        merge(jnp.logical_and(jnp.logical_not(upper), r > 0))

    @pl.when(d == depth_count - 1)
    def _():
        merge(jnp.logical_and(upper, r < rows_count - 1))

    column = lax.broadcasted_iota(jnp.int32, (tall, columns), 1)
    inner = column < columns - 1

    last = total_planes - 1

    for sweep in range(PASSES):

        def plane(z, carry):
            here, above = carry
            deeper = here if z is last else field[z + 1]
            below = flux(deeper - here)
            down = flux(roll(here, -1, 0) - here)
            right = jnp.where(inner, flux(roll(here, -1, 1) - here), 0.0)
            summed = below - above + (down - roll(down, 1, 0)) + (right - roll(right, 1, 1))
            field[z] = here + TIME_STEP * summed
            return deeper, below

        dark = jnp.zeros((tall, columns), jnp.float32)
        plane(last, lax.fori_loop(0, last, plane, (field[0], dark)))

    inner_strip = lax.broadcasted_iota(jnp.int32, (strip, columns), 1) < columns - 1

    picture[...] = jnp.zeros_like(picture)
    picture[3] = jnp.ones((strip, columns), jnp.float32)

    def shade(z, carry):
        nearer, tile = carry
        here = tile[:strip]
        below = tile if z is last else field[z + 1]
        deeper = below[:strip]
        step_row = roll(tile, -1, 0) - tile
        both_rows = (step_row + roll(step_row, 1, 0))[:strip]
        step_col = jnp.where(inner_strip, roll(here, -1, 1) - here, 0.0)
        grad_depth = (deeper - nearer) * 0.5
        grad_row = both_rows * 0.5
        grad_col = (step_col + roll(step_col, 1, 1)) * 0.5
        shading = AMBIENT + (1.0 - AMBIENT) * jnp.abs(
            0.64 * grad_depth + 0.6 * grad_row + 0.48 * grad_col
        ) * lax.rsqrt(grad_depth * grad_depth + grad_row * grad_row + grad_col * grad_col + 0.25)
        mixed = transfer(here * ((KNOTS - 1) / UPPER_DENSITY), table)
        through = jnp.exp(mixed[3] * (-OPTICAL_DEPTH / total_planes))
        remaining = picture[3]
        weight = remaining * (1.0 - through) * shading
        for channel in range(3):
            picture[channel] += weight * mixed[channel]
        picture[3] = remaining * through
        return here, below

    shade(last, lax.fori_loop(0, last, shade, (field[0, :strip, :], field[0])))
    picture[3] = 1.0 - picture[3]

    for k in order:
        peer = lax.rem(d + k, depth_count)
        main_copy(peer, k).wait_send()
        halo_copy(peer, k).wait_send()

    for copy in edge_copies():
        copy.wait_send()


def transfer(position, table):
    mixed = [jnp.zeros_like(position) for channel in range(4)]
    for knot in range(KNOTS):
        hat_weight = jnp.maximum(0.0, 1.0 - jnp.abs(position - knot))
        mixed = [mixed[channel] + table[channel, knot] * hat_weight for channel in range(4)]
    return mixed


def in_one_kernel(depth_count, rows_count, density, transfer_table):
    planes, band, columns = density.shape
    strip = band // depth_count
    total_planes = planes * depth_count
    tall = strip + TILE
    return pl.pallas_call(
        functools.partial(volume_kernel, depth_count, rows_count),
        out_shape=jax.ShapeDtypeStruct((4, strip, columns), jnp.float32),
        in_specs=[
            pl.BlockSpec(memory_space=pl.ANY),
            pl.BlockSpec(memory_space=pltpu.SMEM),
        ],
        out_specs=pl.BlockSpec(memory_space=pltpu.VMEM),
        scratch_shapes=[
            pltpu.VMEM((planes, band, columns), jnp.float32),
            pltpu.VMEM((total_planes, tall, columns), jnp.float32),
            pltpu.VMEM((depth_count, planes, TILE, columns), jnp.float32),
            pltpu.VMEM((depth_count + 1, planes, TILE, columns), jnp.float32),
            pltpu.SemaphoreType.DMA,
            *[pltpu.SemaphoreType.DMA((depth_count,)) for _ in range(6)],
        ],
        compiler_params=pltpu.CompilerParams(
            collective_id=0, has_side_effects=True, vmem_limit_bytes=32 * 2**20
        ),
    )(density, transfer_table)


def fits_one_kernel(depth_count, rows_count, density):
    planes, band, columns = density.shape
    strip = band // depth_count
    held = 4 * planes * columns * (band + depth_count * (strip + 3 * TILE))
    return (
        depth_count > 1
        and rows_count > 1
        and band % depth_count == 0
        and strip % TILE == 0
        and HALO * 2 == TILE
        and columns % 128 == 0
        and held < 2**23
    )


def choose(density, transfer_table):
    depth_count = lax.axis_size("depth")
    rows_count = lax.axis_size("rows")
    if fits_one_kernel(depth_count, rows_count, density):
        return in_one_kernel(depth_count, rows_count, density, transfer_table)
    return per_device(density, transfer_table)


def solution(mesh):
    placed = (P("depth", "rows", None), P())
    return jax.shard_map(
        choose,
        mesh=mesh,
        in_specs=placed,
        out_specs=P(None, ("rows", "depth"), None),
        check_vma=False,
    )
```

```python
import functools

import jax
import jax.numpy as jnp
from jax import lax
from jax.experimental import pallas as pl
from jax.experimental.pallas import tpu as pltpu
from jax.sharding import PartitionSpec as P

PASSES = 3
KNOTS = 16


TIME_STEP = 0.15
OPTICAL_DEPTH = 3.0
UPPER_DENSITY = 6.0
AMBIENT = 0.35


def extended(cells, sides, width):
    for axis, dim in sides:
        count = lax.axis_size(axis)
        ends = count - 1
        head = lax.slice_in_dim(cells, 0, width, axis=dim)
        tail = lax.slice_in_dim(cells, cells.shape[dim] - width, cells.shape[dim], axis=dim)
        cells = jnp.concatenate(
            [
                lax.ppermute(tail, axis, [(i, (i + 1) % count) for i in range(ends)]),
                cells,
                lax.ppermute(head, axis, [((i + 1) % count, i) for i in range(ends)]),
            ],
            axis=dim,
        )
    return cells


def partner(value, axis, stride):
    mask = 2**stride
    pairs = [(source, source ^ mask) for source in range(lax.axis_size(axis))]
    return lax.ppermute(value, axis, pairs)


def diffusion_flux(center, neighbours):
    summed = jnp.zeros_like(center)
    for other in neighbours:
        change = other - center
        summed = summed + change / (1.0 + change * change)
    return center + TIME_STEP * summed


def appearance(center, neighbours, transfer_table, depth_count):
    deeper, nearer, next_row, prev_row, next_col, prev_col = neighbours
    grad_depth = (deeper - nearer) * 0.5
    grad_row = (next_row - prev_row) * 0.5
    grad_col = (next_col - prev_col) * 0.5
    shading = AMBIENT + (1.0 - AMBIENT) * jnp.abs(
        0.64 * grad_depth + 0.6 * grad_row + 0.48 * grad_col
    ) / jnp.sqrt(grad_depth * grad_depth + grad_row * grad_row + grad_col * grad_col + 0.25)
    position = center * ((KNOTS - 1) / UPPER_DENSITY)
    mixed = [jnp.zeros_like(center) for channel in range(4)]
    for knot in range(KNOTS):
        hat_weight = jnp.maximum(0.0, 1.0 - jnp.abs(position - knot))
        mixed = [
            mixed[channel] + transfer_table[channel, knot] * hat_weight for channel in range(4)
        ]
    opacity = 1.0 - jnp.exp(-mixed[3] * (OPTICAL_DEPTH / depth_count))
    colors = jnp.stack([mixed[0] * shading, mixed[1] * shading, mixed[2] * shading])
    return (colors, opacity)


def neighbour_fields(field):
    padded = extended(field, (("depth", 0), ("rows", 1)), 1)
    depth_index = lax.axis_index("depth")
    depth_count = lax.axis_size("depth")
    rows_index = lax.axis_index("rows")
    rows_count = lax.axis_size("rows")
    above = jnp.where(depth_index == 0, field[:1], padded[:1, 1:-1])
    below = jnp.where(depth_index == depth_count - 1, field[-1:], padded[-1:, 1:-1])
    first_row = jnp.where(rows_index == 0, field[:, :1], padded[1:-1, :1])
    last_row = jnp.where(rows_index == rows_count - 1, field[:, -1:], padded[1:-1, -1:])
    deeper = jnp.concatenate([field[1:], below], axis=0)
    nearer = jnp.concatenate([above, field[:-1]], axis=0)
    next_row = jnp.concatenate([field[:, 1:], last_row], axis=1)
    prev_row = jnp.concatenate([first_row, field[:, :-1]], axis=1)
    next_col = jnp.concatenate([field[:, :, 1:], field[:, :, -1:]], axis=2)
    prev_col = jnp.concatenate([field[:, :, :1], field[:, :, :-1]], axis=2)
    return (deeper, nearer, next_row, prev_row, next_col, prev_col)


def composite(front_part, back_part):
    return front_part + (1.0 - front_part[3:4]) * back_part


def per_device(density, transfer_table):
    planes_here = density.shape[0]
    band_rows = density.shape[1]
    columns = density.shape[2]
    depth_count = lax.axis_size("depth")
    depth_index = lax.axis_index("depth")
    total_planes = planes_here * depth_count
    field = density
    for sweep in range(PASSES):
        field = diffusion_flux(field, neighbour_fields(field))
    colors, opacity = appearance(field, neighbour_fields(field), transfer_table, total_planes)
    color_sum = jnp.zeros((3, band_rows, columns), jnp.float32)
    remaining = jnp.ones((band_rows, columns), jnp.float32)
    for plane in range(planes_here):
        color_sum = color_sum + remaining * opacity[plane] * colors[:, plane]
        remaining = remaining * (1.0 - opacity[plane])
    partial_value = jnp.concatenate([color_sum, (1.0 - remaining)[None]], axis=0)
    strip_rows = band_rows // depth_count
    current = partial_value.reshape(4, depth_count, strip_rows, columns)
    levels = depth_count.bit_length() - 1
    for bit in range(levels):
        blocks = current.shape[1]
        paired = current.reshape(4, blocks // 2, 2, strip_rows, columns)
        own_bit = depth_index // 2**bit % 2
        kept_half = jnp.where(own_bit == 0, paired[:, :, 0], paired[:, :, 1])
        sent_half = jnp.where(own_bit == 0, paired[:, :, 1], paired[:, :, 0])
        received = partner(sent_half, "depth", bit)
        front_part = jnp.where(own_bit == 0, kept_half, received)
        back_part = jnp.where(own_bit == 0, received, kept_half)
        current = composite(front_part, back_part)
    return current.reshape(4, strip_rows, columns)


HALO = PASSES + 1
TILE = 8
LANES = 128
UNROLL = 4


def flux(change):
    denominator = 1.0 + change * change
    guess = pl.reciprocal(denominator, approx=True)
    return change * (guess * (2.0 - denominator * guess))


def roll(cells, shift, axis):
    return pltpu.roll(cells, shift % cells.shape[axis], axis)


def lookup(entries, index):
    return jnp.take_along_axis(entries, index, axis=1)


def volume_kernel(
    depth_count,
    rows_count,
    density,
    transfer_table,
    picture,
    local,
    table,
    parcels,
    edges,
    field,
    later,
    rolled,
    side,
    knots,
    shifted,
    load_sem,
    table_sem,
    send,
    recv,
    edge_send,
    edge_recv,
):
    planes, band, columns = local.shape
    strip = band // depth_count
    chunks = columns // LANES
    total_planes = planes * depth_count
    tall = strip + TILE
    d = lax.axis_index("depth")
    r = lax.axis_index("rows")
    next_rows = lax.rem(r + 1, rows_count)
    prev_rows = lax.rem(r + rows_count - 1, rows_count)
    order = sorted(range(1, depth_count), key=lambda k: abs(k - depth_count // 2))

    load = pltpu.make_async_copy(density, local, load_sem)
    load.start()
    load_table = pltpu.make_async_copy(transfer_table, table, table_sem)
    load_table.start()

    barrier = pltpu.get_barrier_semaphore()

    def greet(depth, rows):
        pl.semaphore_signal(
            barrier, inc=1, device_id=(depth, rows), device_id_type=pl.DeviceIdType.MESH
        )

    for k in order:
        greet(lax.rem(d + k, depth_count), r)

    @pl.when(d == 0)
    def _():
        for s in range(depth_count):
            greet(s, prev_rows)

    @pl.when(d == depth_count - 1)
    def _():
        for s in range(depth_count):
            greet(s, next_rows)

    def flipped(rows, first):
        return jnp.concatenate([rows[first - i : first - i + 1] for i in range(HALO)], axis=0)

    load.wait()
    for c in range(chunks):
        lanes = slice(c * LANES, (c + 1) * LANES)
        for p in range(planes):
            first = local[p, :TILE, lanes]
            final = local[p, band - TILE :, lanes]
            edges[depth_count, p, c] = jnp.concatenate([first[:HALO], final[HALO:]], axis=0)
            for s in range(depth_count):
                parcels[s, c, p, :strip, :] = local[p, s * strip : (s + 1) * strip, lanes]
                if s == 0:
                    before = flipped(first, HALO - 1)
                else:
                    before = local[p, s * strip - TILE : s * strip, lanes][HALO:]
                if s == depth_count - 1:
                    after = flipped(final, TILE - 1)
                else:
                    after = local[p, (s + 1) * strip : (s + 1) * strip + TILE, lanes][:HALO]
                parcels[s, c, p, strip:, :] = jnp.concatenate([after, before], axis=0)

    def parcel(peer, c, slot):
        return pltpu.make_async_remote_copy(
            src_ref=parcels.at[peer, c],
            dst_ref=field.at[c, pl.ds(d * planes, planes)],
            send_sem=send.at[slot, c],
            recv_sem=recv.at[d, c],
            device_id=(peer, r),
            device_id_type=pl.DeviceIdType.MESH,
        )

    def edge_copies():
        return [
            pltpu.make_async_remote_copy(
                src_ref=edges.at[depth_count],
                dst_ref=edges.at[d],
                send_sem=edge_send.at[slot],
                recv_sem=edge_recv.at[d],
                device_id=(depth, rows),
                device_id_type=pl.DeviceIdType.MESH,
            )
            for slot, depth, rows in ((0, depth_count - 1, prev_rows), (1, 0, next_rows))
        ]

    def landing(ref, sem):
        return pltpu.make_async_copy(ref, ref, sem)

    pl.semaphore_wait(barrier, depth_count + 1)
    for copy in edge_copies():
        copy.start()
    for c in range(chunks):
        for k in order:
            parcel(lax.rem(d + k, depth_count), c, k).start()

    for c in range(chunks):
        for p in range(planes):
            field[c, d * planes + p] = parcels[d, c, p]
    dark = jnp.zeros((tall, LANES), jnp.float32)

    @pl.loop(0, total_planes + 1)
    def _(z):
        field[chunks, z] = dark
        for p in range(PASSES + 1):
            rolled[p, z] = dark
            side[p, z] = dark

    load_table.wait()
    entry = lax.broadcasted_iota(jnp.int32, (TILE, LANES), 1)
    for channel in range(4):
        value = jnp.zeros((TILE, LANES), jnp.float32)
        slope = jnp.zeros((TILE, LANES), jnp.float32)
        for knot in range(KNOTS - 1):
            start = table[channel, knot]
            value = jnp.where(entry == knot, start, value)
            slope = jnp.where(entry == knot, table[channel, knot + 1] - start, slope)
        knots[channel] = value
        knots[4 + channel] = slope

    lane = lax.broadcasted_iota(jnp.int32, (tall, LANES), 1)
    lane_zero = lane == 0
    upper = lax.broadcasted_iota(jnp.int32, (TILE, LANES), 0) < HALO

    def merge(c, replaced):
        for s in range(depth_count):
            for p in range(planes):
                z = s * planes + p
                field[c, z, strip:, :] = jnp.where(
                    replaced, edges[s, p, c], field[c, z, strip:, :]
                )

    @pl.when((d == 0) | (d == depth_count - 1))
    def _():
        for s in range(depth_count):
            landing(edges.at[s], edge_recv.at[s]).wait()

    def stage(c, p):
        low = jnp.where(c == 0, p, -1)
        high = jnp.where(c == chunks, p, LANES)
        inner = (lane > low) & (lane < high)

        def cells(z):
            here = field[c, z] if p == 0 else later[p - 1, z]
            moved = roll(here, 1, 1)
            center = jnp.where(lane_zero, rolled[p, z], moved)
            rolled[p, z] = moved
            return here, center

        def sides(z, value):
            value = jnp.where(inner, value, 0.0)
            moved = roll(value, 1, 1)
            before = jnp.where(lane_zero, side[p, z], moved)
            side[p, z] = moved
            return value, before

        return cells, sides

    def diffuse(c, p):
        cells, sides = stage(c, p)

        def plane(z, carry):
            here, center, above = carry
            here_below, center_below = cells(z + 1)
            below = flux(center_below - center)
            down = flux(roll(center, -1, 0) - center)
            right, left = sides(z, flux(here - center))
            summed = (below - above) + (down - roll(down, 1, 0)) + (right - left)
            result = center + TIME_STEP * summed
            later[p, z] = result
            return (here_below, center_below, below), result

        def step(block, carry):
            for u in range(UNROLL):
                carry, result = plane(block * UNROLL + u, carry)

            @pl.when(block == total_planes // UNROLL - 1)
            def _():
                later[p, total_planes] = result

            return carry

        here, center = cells(0)
        lax.fori_loop(0, total_planes // UNROLL, step, (here, center, dark))

    def shade(c):
        cells, sides = stage(c, PASSES)

        def plane(z, carry):
            here, center, nearer, remaining, colors = carry
            here_below, center_below = cells(z + 1)
            down = roll(center, -1, 0) - center
            right, left = sides(z, here - center)
            middle = center[:strip]
            grad_depth = (center_below[:strip] - nearer) * 0.5
            grad_row = (down + roll(down, 1, 0))[:strip] * 0.5
            grad_col = (right + left)[:strip] * 0.5
            shading = AMBIENT + (1.0 - AMBIENT) * jnp.abs(
                0.64 * grad_depth + 0.6 * grad_row + 0.48 * grad_col
            ) * lax.rsqrt(
                grad_depth * grad_depth + grad_row * grad_row + grad_col * grad_col + 0.25
            )
            position = middle * ((KNOTS - 1) / UPPER_DENSITY)
            index = jnp.clip(position.astype(jnp.int32), 0, KNOTS - 2)
            part = position - index.astype(jnp.float32)
            tiles = [index[i : i + TILE] for i in range(0, strip, TILE)]
            mixed = [
                jnp.concatenate([lookup(knots[channel], tile) for tile in tiles], axis=0)
                + part
                * jnp.concatenate([lookup(knots[4 + channel], tile) for tile in tiles], axis=0)
                for channel in range(4)
            ]
            through = jnp.exp(mixed[3] * (-OPTICAL_DEPTH / total_planes))
            kept = remaining * through
            weight = (remaining - kept) * shading
            colors = tuple(colors[i] + weight * mixed[i] for i in range(3))
            return here_below, center_below, middle, kept, colors

        def step(block, carry):
            for u in range(UNROLL):
                carry = plane(block * UNROLL + u, carry)
            return carry

        here, center = cells(0)
        flat = jnp.zeros((strip, LANES), jnp.float32)
        carry = (here, center, center[:strip], jnp.ones_like(flat), (flat,) * 3)
        carry = lax.fori_loop(0, total_planes // UNROLL, step, carry)
        for channel in range(3):
            shifted[c, channel] = carry[4][channel]
        shifted[c, 3] = 1.0 - carry[3]

    @pl.loop(0, chunks + 1)
    def _(c):
        @pl.when(c < chunks)
        def _():
            for k in order:
                source = lax.rem(d + k, depth_count)
                landing(
                    field.at[c, pl.ds(source * planes, planes)], recv.at[source, c]
                ).wait()

            @pl.when(d == 0)
            def _():
                merge(c, jnp.logical_and(jnp.logical_not(upper), r > 0))

            @pl.when(d == depth_count - 1)
            def _():
                merge(c, jnp.logical_and(upper, r < rows_count - 1))

            field[c, total_planes] = field[c, total_planes - 1]

        for p in range(PASSES):
            diffuse(c, p)
        shade(c)

    early = lax.broadcasted_iota(jnp.int32, (strip, LANES), 1) < LANES - HALO
    for c in range(chunks):
        for channel in range(4):
            picture[channel, :, c * LANES : (c + 1) * LANES] = jnp.where(
                early,
                roll(shifted[c, channel], -HALO, 1),
                roll(shifted[c + 1, channel], -HALO, 1),
            )

    for c in range(chunks):
        for k in order:
            parcel(lax.rem(d + k, depth_count), c, k).wait_send()
    for copy in edge_copies():
        copy.wait_send()


def in_one_kernel(depth_count, rows_count, density, transfer_table):
    planes, band, columns = density.shape
    strip = band // depth_count
    chunks = columns // LANES
    total_planes = planes * depth_count
    tall = strip + TILE
    return pl.pallas_call(
        functools.partial(volume_kernel, depth_count, rows_count),
        out_shape=jax.ShapeDtypeStruct((4, strip, columns), jnp.float32),
        in_specs=[pl.BlockSpec(memory_space=pl.ANY)] * 2,
        out_specs=pl.BlockSpec(memory_space=pltpu.VMEM),
        scratch_shapes=[
            pltpu.VMEM((planes, band, columns), jnp.float32),
            pltpu.SMEM(transfer_table.shape, jnp.float32),
            pltpu.VMEM((depth_count, chunks, planes, tall, LANES), jnp.float32),
            pltpu.VMEM((depth_count + 1, planes, chunks, TILE, LANES), jnp.float32),
            pltpu.VMEM((chunks + 1, total_planes + 1, tall, LANES), jnp.float32),
            pltpu.VMEM((PASSES, total_planes + 1, tall, LANES), jnp.float32),
            pltpu.VMEM((PASSES + 1, total_planes + 1, tall, LANES), jnp.float32),
            pltpu.VMEM((PASSES + 1, total_planes + 1, tall, LANES), jnp.float32),
            pltpu.VMEM((8, TILE, LANES), jnp.float32),
            pltpu.VMEM((chunks + 1, 4, strip, LANES), jnp.float32),
            pltpu.SemaphoreType.DMA,
            pltpu.SemaphoreType.DMA,
            pltpu.SemaphoreType.DMA((depth_count, chunks)),
            pltpu.SemaphoreType.DMA((depth_count, chunks)),
            pltpu.SemaphoreType.DMA((2,)),
            pltpu.SemaphoreType.DMA((depth_count,)),
        ],
        compiler_params=pltpu.CompilerParams(
            collective_id=0, has_side_effects=True, vmem_limit_bytes=56 * 2**20
        ),
    )(density, transfer_table)


def fits_one_kernel(depth_count, rows_count, density):
    planes, band, columns = density.shape
    strip = band // depth_count
    total_planes = planes * depth_count
    return (
        depth_count > 1
        and rows_count > 1
        and band % depth_count == 0
        and strip % TILE == 0
        and HALO * 2 == TILE
        and columns % LANES == 0
        and total_planes % UNROLL == 0
        and planes * columns * band + 24 * (total_planes + 1) * (strip + TILE) * LANES < 2**22
    )


def choose(density, transfer_table):
    depth_count = lax.axis_size("depth")
    rows_count = lax.axis_size("rows")
    if fits_one_kernel(depth_count, rows_count, density):
        return in_one_kernel(depth_count, rows_count, density, transfer_table)
    return per_device(density, transfer_table)


def solution(mesh):
    placed = (P("depth", "rows", None), P())
    return jax.shard_map(
        choose,
        mesh=mesh,
        in_specs=placed,
        out_specs=P(None, ("rows", "depth"), None),
        check_vma=False,
    )
```

```python
import functools

import jax
import jax.numpy as jnp
from jax import lax
from jax.experimental import pallas as pl
from jax.experimental.pallas import tpu as pltpu
from jax.sharding import PartitionSpec as P

PASSES = 3
KNOTS = 16


TIME_STEP = 0.15
OPTICAL_DEPTH = 3.0
UPPER_DENSITY = 6.0
AMBIENT = 0.35


def extended(cells, sides, width):
    for axis, dim in sides:
        count = lax.axis_size(axis)
        ends = count - 1
        head = lax.slice_in_dim(cells, 0, width, axis=dim)
        tail = lax.slice_in_dim(cells, cells.shape[dim] - width, cells.shape[dim], axis=dim)
        cells = jnp.concatenate(
            [
                lax.ppermute(tail, axis, [(i, (i + 1) % count) for i in range(ends)]),
                cells,
                lax.ppermute(head, axis, [((i + 1) % count, i) for i in range(ends)]),
            ],
            axis=dim,
        )
    return cells


def partner(value, axis, stride):
    mask = 2**stride
    pairs = [(source, source ^ mask) for source in range(lax.axis_size(axis))]
    return lax.ppermute(value, axis, pairs)


def diffusion_flux(center, neighbours):
    summed = jnp.zeros_like(center)
    for other in neighbours:
        change = other - center
        summed = summed + change / (1.0 + change * change)
    return center + TIME_STEP * summed


def appearance(center, neighbours, transfer_table, depth_count):
    deeper, nearer, next_row, prev_row, next_col, prev_col = neighbours
    grad_depth = (deeper - nearer) * 0.5
    grad_row = (next_row - prev_row) * 0.5
    grad_col = (next_col - prev_col) * 0.5
    shading = AMBIENT + (1.0 - AMBIENT) * jnp.abs(
        0.64 * grad_depth + 0.6 * grad_row + 0.48 * grad_col
    ) / jnp.sqrt(grad_depth * grad_depth + grad_row * grad_row + grad_col * grad_col + 0.25)
    position = center * ((KNOTS - 1) / UPPER_DENSITY)
    mixed = [jnp.zeros_like(center) for channel in range(4)]
    for knot in range(KNOTS):
        hat_weight = jnp.maximum(0.0, 1.0 - jnp.abs(position - knot))
        mixed = [
            mixed[channel] + transfer_table[channel, knot] * hat_weight for channel in range(4)
        ]
    opacity = 1.0 - jnp.exp(-mixed[3] * (OPTICAL_DEPTH / depth_count))
    colors = jnp.stack([mixed[0] * shading, mixed[1] * shading, mixed[2] * shading])
    return (colors, opacity)


def neighbour_fields(field):
    padded = extended(field, (("depth", 0), ("rows", 1)), 1)
    depth_index = lax.axis_index("depth")
    depth_count = lax.axis_size("depth")
    rows_index = lax.axis_index("rows")
    rows_count = lax.axis_size("rows")
    above = jnp.where(depth_index == 0, field[:1], padded[:1, 1:-1])
    below = jnp.where(depth_index == depth_count - 1, field[-1:], padded[-1:, 1:-1])
    first_row = jnp.where(rows_index == 0, field[:, :1], padded[1:-1, :1])
    last_row = jnp.where(rows_index == rows_count - 1, field[:, -1:], padded[1:-1, -1:])
    deeper = jnp.concatenate([field[1:], below], axis=0)
    nearer = jnp.concatenate([above, field[:-1]], axis=0)
    next_row = jnp.concatenate([field[:, 1:], last_row], axis=1)
    prev_row = jnp.concatenate([first_row, field[:, :-1]], axis=1)
    next_col = jnp.concatenate([field[:, :, 1:], field[:, :, -1:]], axis=2)
    prev_col = jnp.concatenate([field[:, :, :1], field[:, :, :-1]], axis=2)
    return (deeper, nearer, next_row, prev_row, next_col, prev_col)


def composite(front_part, back_part):
    return front_part + (1.0 - front_part[3:4]) * back_part


def per_device(density, transfer_table):
    planes_here = density.shape[0]
    band_rows = density.shape[1]
    columns = density.shape[2]
    depth_count = lax.axis_size("depth")
    depth_index = lax.axis_index("depth")
    total_planes = planes_here * depth_count
    field = density
    for sweep in range(PASSES):
        field = diffusion_flux(field, neighbour_fields(field))
    colors, opacity = appearance(field, neighbour_fields(field), transfer_table, total_planes)
    color_sum = jnp.zeros((3, band_rows, columns), jnp.float32)
    remaining = jnp.ones((band_rows, columns), jnp.float32)
    for plane in range(planes_here):
        color_sum = color_sum + remaining * opacity[plane] * colors[:, plane]
        remaining = remaining * (1.0 - opacity[plane])
    partial_value = jnp.concatenate([color_sum, (1.0 - remaining)[None]], axis=0)
    strip_rows = band_rows // depth_count
    current = partial_value.reshape(4, depth_count, strip_rows, columns)
    levels = depth_count.bit_length() - 1
    for bit in range(levels):
        blocks = current.shape[1]
        paired = current.reshape(4, blocks // 2, 2, strip_rows, columns)
        own_bit = depth_index // 2**bit % 2
        kept_half = jnp.where(own_bit == 0, paired[:, :, 0], paired[:, :, 1])
        sent_half = jnp.where(own_bit == 0, paired[:, :, 1], paired[:, :, 0])
        received = partner(sent_half, "depth", bit)
        front_part = jnp.where(own_bit == 0, kept_half, received)
        back_part = jnp.where(own_bit == 0, received, kept_half)
        current = composite(front_part, back_part)
    return current.reshape(4, strip_rows, columns)


HALO = PASSES + 1
TILE = 8
LANES = 128
UNROLL = 16


def flux(change):
    denominator = 1.0 + change * change
    guess = pl.reciprocal(denominator, approx=True)
    return change * (guess * (2.0 - denominator * guess))


def roll(cells, shift, axis):
    return pltpu.roll(cells, shift % cells.shape[axis], axis)


def lookup(entries, index):
    return jnp.take_along_axis(entries, index, axis=1)


def volume_kernel(
    depth_count,
    rows_count,
    density,
    transfer_table,
    picture,
    local,
    table,
    parcels,
    edges,
    field,
    later,
    rolled,
    side,
    knots,
    shifted,
    load_sem,
    table_sem,
    send,
    recv,
    edge_send,
    edge_recv,
):
    planes, band, columns = local.shape
    strip = band // depth_count
    chunks = columns // LANES
    total_planes = planes * depth_count
    tall = strip + TILE
    d = lax.axis_index("depth")
    r = lax.axis_index("rows")
    next_rows = lax.rem(r + 1, rows_count)
    prev_rows = lax.rem(r + rows_count - 1, rows_count)
    order = sorted(range(1, depth_count), key=lambda k: abs(k - depth_count // 2))

    load = pltpu.make_async_copy(density, local, load_sem)
    load.start()
    load_table = pltpu.make_async_copy(transfer_table, table, table_sem)
    load_table.start()

    barrier = pltpu.get_barrier_semaphore()

    def greet(depth, rows):
        pl.semaphore_signal(
            barrier, inc=1, device_id=(depth, rows), device_id_type=pl.DeviceIdType.MESH
        )

    for k in order:
        greet(lax.rem(d + k, depth_count), r)

    @pl.when(d == 0)
    def _():
        for s in range(depth_count):
            greet(s, prev_rows)

    @pl.when(d == depth_count - 1)
    def _():
        for s in range(depth_count):
            greet(s, next_rows)

    def flipped(rows, first):
        return jnp.concatenate([rows[first - i : first - i + 1] for i in range(HALO)], axis=0)

    load.wait()
    for c in range(chunks):
        lanes = slice(c * LANES, (c + 1) * LANES)
        for p in range(planes):
            first = local[p, :TILE, lanes]
            final = local[p, band - TILE :, lanes]
            edges[depth_count, p, c] = jnp.concatenate([first[:HALO], final[HALO:]], axis=0)
            for s in range(depth_count):
                parcels[s, c, p, :strip, :] = local[p, s * strip : (s + 1) * strip, lanes]
                if s == 0:
                    before = flipped(first, HALO - 1)
                else:
                    before = local[p, s * strip - TILE : s * strip, lanes][HALO:]
                if s == depth_count - 1:
                    after = flipped(final, TILE - 1)
                else:
                    after = local[p, (s + 1) * strip : (s + 1) * strip + TILE, lanes][:HALO]
                parcels[s, c, p, strip:, :] = jnp.concatenate([after, before], axis=0)

    def parcel(peer, c, slot):
        return pltpu.make_async_remote_copy(
            src_ref=parcels.at[peer, c],
            dst_ref=field.at[c, pl.ds(d * planes, planes)],
            send_sem=send.at[slot, c],
            recv_sem=recv.at[d, c],
            device_id=(peer, r),
            device_id_type=pl.DeviceIdType.MESH,
        )

    def edge_copies():
        return [
            pltpu.make_async_remote_copy(
                src_ref=edges.at[depth_count],
                dst_ref=edges.at[d],
                send_sem=edge_send.at[slot],
                recv_sem=edge_recv.at[d],
                device_id=(depth, rows),
                device_id_type=pl.DeviceIdType.MESH,
            )
            for slot, depth, rows in ((0, depth_count - 1, prev_rows), (1, 0, next_rows))
        ]

    def landing(ref, sem):
        return pltpu.make_async_copy(ref, ref, sem)

    pl.semaphore_wait(barrier, depth_count + 1)
    for copy in edge_copies():
        copy.start()
    for c in range(chunks):
        for k in order:
            parcel(lax.rem(d + k, depth_count), c, k).start()

    for c in range(chunks):
        for p in range(planes):
            field[c, d * planes + p] = parcels[d, c, p]
    dark = jnp.zeros((tall, LANES), jnp.float32)

    @pl.loop(0, total_planes + 1)
    def _(z):
        field[chunks, z] = dark
        for p in range(PASSES + 1):
            rolled[p, z] = dark
            side[p, z] = dark

    load_table.wait()
    entry = lax.broadcasted_iota(jnp.int32, (TILE, LANES), 1)
    for channel in range(4):
        value = jnp.zeros((TILE, LANES), jnp.float32)
        slope = jnp.zeros((TILE, LANES), jnp.float32)
        for knot in range(KNOTS - 1):
            start = table[channel, knot]
            value = jnp.where(entry == knot, start, value)
            slope = jnp.where(entry == knot, table[channel, knot + 1] - start, slope)
        knots[channel] = value
        knots[4 + channel] = slope

    lane = lax.broadcasted_iota(jnp.int32, (tall, LANES), 1)
    lane_zero = lane == 0
    upper = lax.broadcasted_iota(jnp.int32, (TILE, LANES), 0) < HALO

    def merge(c, replaced):
        for s in range(depth_count):
            for p in range(planes):
                z = s * planes + p
                field[c, z, strip:, :] = jnp.where(
                    replaced, edges[s, p, c], field[c, z, strip:, :]
                )

    @pl.when((d == 0) | (d == depth_count - 1))
    def _():
        for s in range(depth_count):
            landing(edges.at[s], edge_recv.at[s]).wait()

    def stage(c, p):
        low = jnp.where(c == 0, p, -1)
        high = jnp.where(c == chunks, p, LANES)
        inner = (lane > low) & (lane < high)

        def cells(z):
            here = field[c, z] if p == 0 else later[p - 1, z]
            moved = roll(here, 1, 1)
            center = jnp.where(lane_zero, rolled[p, z], moved)
            rolled[p, z] = moved
            return here, center

        def sides(z, value):
            value = jnp.where(inner, value, 0.0)
            moved = roll(value, 1, 1)
            before = jnp.where(lane_zero, side[p, z], moved)
            side[p, z] = moved
            return value, before

        return cells, sides

    def diffuse(c, p):
        cells, sides = stage(c, p)

        def plane(z, carry):
            here, center, above = carry
            here_below, center_below = cells(z + 1)
            below = flux(center_below - center)
            down = flux(roll(center, -1, 0) - center)
            right, left = sides(z, flux(here - center))
            summed = (below - above) + (down - roll(down, 1, 0)) + (right - left)
            result = center + TIME_STEP * summed
            later[p, z] = result
            return (here_below, center_below, below), result

        def step(block, carry):
            for u in range(UNROLL):
                carry, result = plane(block * UNROLL + u, carry)

            later[p, total_planes] = result
            return carry

        here, center = cells(0)
        lax.fori_loop(0, total_planes // UNROLL, step, (here, center, dark))

    def shade(c):
        cells, sides = stage(c, PASSES)

        def plane(z, carry):
            here, center, nearer, remaining, colors = carry
            here_below, center_below = cells(z + 1)
            down = roll(center, -1, 0) - center
            right, left = sides(z, here - center)
            middle = center[:strip]
            grad_depth = (center_below[:strip] - nearer) * 0.5
            grad_row = (down + roll(down, 1, 0))[:strip] * 0.5
            grad_col = (right + left)[:strip] * 0.5
            shading = AMBIENT + (1.0 - AMBIENT) * jnp.abs(
                0.64 * grad_depth + 0.6 * grad_row + 0.48 * grad_col
            ) * lax.rsqrt(
                grad_depth * grad_depth + grad_row * grad_row + grad_col * grad_col + 0.25
            )
            position = middle * ((KNOTS - 1) / UPPER_DENSITY)
            index = jnp.clip(position.astype(jnp.int32), 0, KNOTS - 2)
            part = position - index.astype(jnp.float32)
            tiles = [index[i : i + TILE] for i in range(0, strip, TILE)]
            mixed = [
                jnp.concatenate([lookup(knots[channel], tile) for tile in tiles], axis=0)
                + part
                * jnp.concatenate([lookup(knots[4 + channel], tile) for tile in tiles], axis=0)
                for channel in range(4)
            ]
            through = jnp.exp(mixed[3] * (-OPTICAL_DEPTH / total_planes))
            kept = remaining * through
            weight = (remaining - kept) * shading
            colors = tuple(colors[i] + weight * mixed[i] for i in range(3))
            return here_below, center_below, middle, kept, colors

        def step(block, carry):
            for u in range(UNROLL):
                carry = plane(block * UNROLL + u, carry)
            return carry

        here, center = cells(0)
        flat = jnp.zeros((strip, LANES), jnp.float32)
        carry = (here, center, center[:strip], jnp.ones_like(flat), (flat,) * 3)
        carry = lax.fori_loop(0, total_planes // UNROLL, step, carry)
        for channel in range(3):
            shifted[c, channel] = carry[4][channel]
        shifted[c, 3] = 1.0 - carry[3]

    @pl.loop(0, chunks + 1)
    def _(c):
        @pl.when(c < chunks)
        def _():
            for k in order:
                source = lax.rem(d + k, depth_count)
                landing(
                    field.at[c, pl.ds(source * planes, planes)], recv.at[source, c]
                ).wait()

            @pl.when(d == 0)
            def _():
                merge(c, jnp.logical_and(jnp.logical_not(upper), r > 0))

            @pl.when(d == depth_count - 1)
            def _():
                merge(c, jnp.logical_and(upper, r < rows_count - 1))

            field[c, total_planes] = field[c, total_planes - 1]

        for p in range(PASSES):
            diffuse(c, p)
        shade(c)

    early = lax.broadcasted_iota(jnp.int32, (strip, LANES), 1) < LANES - HALO
    for c in range(chunks):
        for channel in range(4):
            picture[channel, :, c * LANES : (c + 1) * LANES] = jnp.where(
                early,
                roll(shifted[c, channel], -HALO, 1),
                roll(shifted[c + 1, channel], -HALO, 1),
            )

    for c in range(chunks):
        for k in order:
            parcel(lax.rem(d + k, depth_count), c, k).wait_send()
    for copy in edge_copies():
        copy.wait_send()


def in_one_kernel(depth_count, rows_count, density, transfer_table):
    planes, band, columns = density.shape
    strip = band // depth_count
    chunks = columns // LANES
    total_planes = planes * depth_count
    tall = strip + TILE
    return pl.pallas_call(
        functools.partial(volume_kernel, depth_count, rows_count),
        out_shape=jax.ShapeDtypeStruct((4, strip, columns), jnp.float32),
        in_specs=[pl.BlockSpec(memory_space=pltpu.HBM)] * 2,
        out_specs=pl.BlockSpec(memory_space=pltpu.VMEM),
        scratch_shapes=[
            pltpu.VMEM((planes, band, columns), jnp.float32),
            pltpu.SMEM(transfer_table.shape, jnp.float32),
            pltpu.VMEM((depth_count, chunks, planes, tall, LANES), jnp.float32),
            pltpu.VMEM((depth_count + 1, planes, chunks, TILE, LANES), jnp.float32),
            pltpu.VMEM((chunks + 1, total_planes + 1, tall, LANES), jnp.float32),
            pltpu.VMEM((PASSES, total_planes + 1, tall, LANES), jnp.float32),
            pltpu.VMEM((PASSES + 1, total_planes + 1, tall, LANES), jnp.float32),
            pltpu.VMEM((PASSES + 1, total_planes + 1, tall, LANES), jnp.float32),
            pltpu.VMEM((8, TILE, LANES), jnp.float32),
            pltpu.VMEM((chunks + 1, 4, strip, LANES), jnp.float32),
            pltpu.SemaphoreType.DMA,
            pltpu.SemaphoreType.DMA,
            pltpu.SemaphoreType.DMA((depth_count, chunks)),
            pltpu.SemaphoreType.DMA((depth_count, chunks)),
            pltpu.SemaphoreType.DMA((2,)),
            pltpu.SemaphoreType.DMA((depth_count,)),
        ],
        compiler_params=pltpu.CompilerParams(
            collective_id=0, has_side_effects=True, vmem_limit_bytes=24 * 2**20
        ),
    )(density, transfer_table)


def fits_one_kernel(depth_count, rows_count, density):
    planes, band, columns = density.shape
    strip = band // depth_count
    total_planes = planes * depth_count
    return (
        depth_count > 1
        and rows_count > 1
        and band % depth_count == 0
        and strip % TILE == 0
        and HALO * 2 == TILE
        and columns % LANES == 0
        and total_planes % UNROLL == 0
        and planes * columns * band + 24 * (total_planes + 1) * (strip + TILE) * LANES < 2**22
    )


def choose(density, transfer_table):
    depth_count = lax.axis_size("depth")
    rows_count = lax.axis_size("rows")
    if fits_one_kernel(depth_count, rows_count, density):
        return in_one_kernel(depth_count, rows_count, density, transfer_table)
    return per_device(density, transfer_table)


def solution(mesh):
    placed = (P("depth", "rows", None), P())
    return jax.shard_map(
        choose,
        mesh=mesh,
        in_specs=placed,
        out_specs=P(None, ("rows", "depth"), None),
        check_vma=False,
    )
```

```python
import functools

import jax
import jax.numpy as jnp
from jax import lax
from jax.experimental import pallas as pl
from jax.experimental.pallas import tpu as pltpu
from jax.sharding import PartitionSpec as P

PASSES = 3
KNOTS = 16


TIME_STEP = 0.15
OPTICAL_DEPTH = 3.0
UPPER_DENSITY = 6.0
AMBIENT = 0.35


def extended(cells, sides, width):
    for axis, dim in sides:
        count = lax.axis_size(axis)
        ends = count - 1
        head = lax.slice_in_dim(cells, 0, width, axis=dim)
        tail = lax.slice_in_dim(cells, cells.shape[dim] - width, cells.shape[dim], axis=dim)
        cells = jnp.concatenate(
            [
                lax.ppermute(tail, axis, [(i, (i + 1) % count) for i in range(ends)]),
                cells,
                lax.ppermute(head, axis, [((i + 1) % count, i) for i in range(ends)]),
            ],
            axis=dim,
        )
    return cells


def partner(value, axis, stride):
    mask = 2**stride
    pairs = [(source, source ^ mask) for source in range(lax.axis_size(axis))]
    return lax.ppermute(value, axis, pairs)


def diffusion_flux(center, neighbours):
    summed = jnp.zeros_like(center)
    for other in neighbours:
        change = other - center
        summed = summed + change / (1.0 + change * change)
    return center + TIME_STEP * summed


def appearance(center, neighbours, transfer_table, depth_count):
    deeper, nearer, next_row, prev_row, next_col, prev_col = neighbours
    grad_depth = (deeper - nearer) * 0.5
    grad_row = (next_row - prev_row) * 0.5
    grad_col = (next_col - prev_col) * 0.5
    shading = AMBIENT + (1.0 - AMBIENT) * jnp.abs(
        0.64 * grad_depth + 0.6 * grad_row + 0.48 * grad_col
    ) / jnp.sqrt(grad_depth * grad_depth + grad_row * grad_row + grad_col * grad_col + 0.25)
    position = center * ((KNOTS - 1) / UPPER_DENSITY)
    mixed = [jnp.zeros_like(center) for channel in range(4)]
    for knot in range(KNOTS):
        hat_weight = jnp.maximum(0.0, 1.0 - jnp.abs(position - knot))
        mixed = [
            mixed[channel] + transfer_table[channel, knot] * hat_weight for channel in range(4)
        ]
    opacity = 1.0 - jnp.exp(-mixed[3] * (OPTICAL_DEPTH / depth_count))
    colors = jnp.stack([mixed[0] * shading, mixed[1] * shading, mixed[2] * shading])
    return (colors, opacity)


def neighbour_fields(field):
    padded = extended(field, (("depth", 0), ("rows", 1)), 1)
    depth_index = lax.axis_index("depth")
    depth_count = lax.axis_size("depth")
    rows_index = lax.axis_index("rows")
    rows_count = lax.axis_size("rows")
    above = jnp.where(depth_index == 0, field[:1], padded[:1, 1:-1])
    below = jnp.where(depth_index == depth_count - 1, field[-1:], padded[-1:, 1:-1])
    first_row = jnp.where(rows_index == 0, field[:, :1], padded[1:-1, :1])
    last_row = jnp.where(rows_index == rows_count - 1, field[:, -1:], padded[1:-1, -1:])
    deeper = jnp.concatenate([field[1:], below], axis=0)
    nearer = jnp.concatenate([above, field[:-1]], axis=0)
    next_row = jnp.concatenate([field[:, 1:], last_row], axis=1)
    prev_row = jnp.concatenate([first_row, field[:, :-1]], axis=1)
    next_col = jnp.concatenate([field[:, :, 1:], field[:, :, -1:]], axis=2)
    prev_col = jnp.concatenate([field[:, :, :1], field[:, :, :-1]], axis=2)
    return (deeper, nearer, next_row, prev_row, next_col, prev_col)


def composite(front_part, back_part):
    return front_part + (1.0 - front_part[3:4]) * back_part


def per_device(density, transfer_table):
    planes_here = density.shape[0]
    band_rows = density.shape[1]
    columns = density.shape[2]
    depth_count = lax.axis_size("depth")
    depth_index = lax.axis_index("depth")
    total_planes = planes_here * depth_count
    field = density
    for sweep in range(PASSES):
        field = diffusion_flux(field, neighbour_fields(field))
    colors, opacity = appearance(field, neighbour_fields(field), transfer_table, total_planes)
    color_sum = jnp.zeros((3, band_rows, columns), jnp.float32)
    remaining = jnp.ones((band_rows, columns), jnp.float32)
    for plane in range(planes_here):
        color_sum = color_sum + remaining * opacity[plane] * colors[:, plane]
        remaining = remaining * (1.0 - opacity[plane])
    partial_value = jnp.concatenate([color_sum, (1.0 - remaining)[None]], axis=0)
    strip_rows = band_rows // depth_count
    current = partial_value.reshape(4, depth_count, strip_rows, columns)
    levels = depth_count.bit_length() - 1
    for bit in range(levels):
        blocks = current.shape[1]
        paired = current.reshape(4, blocks // 2, 2, strip_rows, columns)
        own_bit = depth_index // 2**bit % 2
        kept_half = jnp.where(own_bit == 0, paired[:, :, 0], paired[:, :, 1])
        sent_half = jnp.where(own_bit == 0, paired[:, :, 1], paired[:, :, 0])
        received = partner(sent_half, "depth", bit)
        front_part = jnp.where(own_bit == 0, kept_half, received)
        back_part = jnp.where(own_bit == 0, received, kept_half)
        current = composite(front_part, back_part)
    return current.reshape(4, strip_rows, columns)


HALO = PASSES + 1
TILE = 8
LANES = 128
UNROLL = 16


def flux(change):
    denominator = 1.0 + change * change
    guess = pl.reciprocal(denominator, approx=True)
    return change * (guess * (2.0 - denominator * guess))


def roll(cells, shift, axis):
    return pltpu.roll(cells, shift % cells.shape[axis], axis)


def lookup(entries, index):
    return jnp.take_along_axis(entries, index, axis=1)


def volume_kernel(
    depth_count,
    rows_count,
    density,
    transfer_table,
    picture,
    local,
    table,
    parcels,
    edges,
    field,
    later,
    rolled,
    side,
    knots,
    shifted,
    load_sem,
    table_sem,
    send,
    recv,
    edge_send,
    edge_recv,
):
    planes, band, columns = local.shape
    strip = band // depth_count
    chunks = columns // LANES
    total_planes = planes * depth_count
    tall = strip + TILE
    d = lax.axis_index("depth")
    r = lax.axis_index("rows")
    next_rows = lax.rem(r + 1, rows_count)
    prev_rows = lax.rem(r + rows_count - 1, rows_count)
    order = sorted(range(1, depth_count), key=lambda k: abs(k - depth_count // 2))

    load = pltpu.make_async_copy(density, local, load_sem)
    load.start()
    load_table = pltpu.make_async_copy(transfer_table, table, table_sem)
    load_table.start()

    barrier = pltpu.get_barrier_semaphore()

    def greet(depth, rows):
        pl.semaphore_signal(
            barrier, inc=1, device_id=(depth, rows), device_id_type=pl.DeviceIdType.MESH
        )

    for k in order:
        greet(lax.rem(d + k, depth_count), r)

    @pl.when(d == 0)
    def _():
        for s in range(depth_count):
            greet(s, prev_rows)

    @pl.when(d == depth_count - 1)
    def _():
        for s in range(depth_count):
            greet(s, next_rows)

    def flipped(rows, first):
        return jnp.concatenate([rows[first - i : first - i + 1] for i in range(HALO)], axis=0)

    load.wait()
    for c in range(chunks):
        lanes = slice(c * LANES, (c + 1) * LANES)
        for p in range(planes):
            first = local[p, :TILE, lanes]
            final = local[p, band - TILE :, lanes]
            edges[depth_count, p, c] = jnp.concatenate([first[:HALO], final[HALO:]], axis=0)
            for s in range(depth_count):
                parcels[s, c, p, :strip, :] = local[p, s * strip : (s + 1) * strip, lanes]
                if s == 0:
                    before = flipped(first, HALO - 1)
                else:
                    before = local[p, s * strip - TILE : s * strip, lanes][HALO:]
                if s == depth_count - 1:
                    after = flipped(final, TILE - 1)
                else:
                    after = local[p, (s + 1) * strip : (s + 1) * strip + TILE, lanes][:HALO]
                parcels[s, c, p, strip:, :] = jnp.concatenate([after, before], axis=0)

    def parcel(peer, c, slot):
        return pltpu.make_async_remote_copy(
            src_ref=parcels.at[peer, c],
            dst_ref=field.at[c, pl.ds(d * planes, planes)],
            send_sem=send.at[slot, c],
            recv_sem=recv.at[d, c],
            device_id=(peer, r),
            device_id_type=pl.DeviceIdType.MESH,
        )

    def edge_copies():
        return [
            pltpu.make_async_remote_copy(
                src_ref=edges.at[depth_count],
                dst_ref=edges.at[d],
                send_sem=edge_send.at[slot],
                recv_sem=edge_recv.at[d],
                device_id=(depth, rows),
                device_id_type=pl.DeviceIdType.MESH,
            )
            for slot, depth, rows in ((0, depth_count - 1, prev_rows), (1, 0, next_rows))
        ]

    def landing(ref, sem):
        return pltpu.make_async_copy(ref, ref, sem)

    pl.semaphore_wait(barrier, depth_count + 1)
    for copy in edge_copies():
        copy.start()
    for c in range(chunks):
        for k in order:
            parcel(lax.rem(d + k, depth_count), c, k).start()

    for c in range(chunks):
        for p in range(planes):
            field[c, d * planes + p] = parcels[d, c, p]
    dark = jnp.zeros((tall, LANES), jnp.float32)

    @pl.loop(0, total_planes + 1)
    def _(z):
        for p in range(PASSES + 1):
            rolled[p, z] = dark
            side[p, z] = dark

    load_table.wait()
    entry = lax.broadcasted_iota(jnp.int32, (TILE, LANES), 1)
    for channel in range(4):
        value = jnp.zeros((TILE, LANES), jnp.float32)
        slope = jnp.zeros((TILE, LANES), jnp.float32)
        for knot in range(KNOTS - 1):
            start = table[channel, knot]
            value = jnp.where(entry == knot, start, value)
            slope = jnp.where(entry == knot, table[channel, knot + 1] - start, slope)
        knots[channel] = value
        knots[4 + channel] = slope

    lane = lax.broadcasted_iota(jnp.int32, (tall, LANES), 1)
    lane_zero = lane == 0
    upper = lax.broadcasted_iota(jnp.int32, (TILE, LANES), 0) < HALO

    def merge(c, replaced):
        for s in range(depth_count):
            for p in range(planes):
                z = s * planes + p
                field[c, z, strip:, :] = jnp.where(
                    replaced, edges[s, p, c], field[c, z, strip:, :]
                )

    @pl.when((d == 0) | (d == depth_count - 1))
    def _():
        for s in range(depth_count):
            landing(edges.at[s], edge_recv.at[s]).wait()

    def stage(c, p):
        inner = lane > jnp.where(c == 0, p, -1)

        def cells(z):
            here = field[c, z] if p == 0 else later[p - 1, z]
            moved = roll(here, 1, 1)
            center = jnp.where(lane_zero, rolled[p, z], moved)
            rolled[p, z] = moved
            return here, center

        def sides(z, value):
            value = jnp.where(inner, value, 0.0)
            moved = roll(value, 1, 1)
            before = jnp.where(lane_zero, side[p, z], moved)
            side[p, z] = moved
            return value, before

        return cells, sides

    def diffuse(c, p):
        cells, sides = stage(c, p)

        def plane(z, carry):
            here, center, above = carry
            here_below, center_below = cells(z + 1)
            below = flux(center_below - center)
            down = flux(roll(center, -1, 0) - center)
            right, left = sides(z, flux(here - center))
            summed = (below - above) + (down - roll(down, 1, 0)) + (right - left)
            result = center + TIME_STEP * summed
            later[p, z] = result
            return (here_below, center_below, below), result

        def step(block, carry):
            for u in range(UNROLL):
                carry, result = plane(block * UNROLL + u, carry)

            later[p, total_planes] = result
            return carry

        here, center = cells(0)
        lax.fori_loop(0, total_planes // UNROLL, step, (here, center, dark))

    def transfer(cells):
        position = cells * ((KNOTS - 1) / UPPER_DENSITY)
        index = jnp.clip(position.astype(jnp.int32), 0, KNOTS - 2)
        part = position - index.astype(jnp.float32)
        tiles = [index[i : i + TILE] for i in range(0, strip, TILE)]
        mixed = []
        for channel in range(4):
            value = jnp.concatenate([lookup(knots[channel], tile) for tile in tiles], axis=0)
            slope = jnp.concatenate([lookup(knots[4 + channel], tile) for tile in tiles], axis=0)
            mixed.append(value + part * slope)
        return mixed

    def shading_of(grad_depth, grad_row, grad_col):
        return AMBIENT + (1.0 - AMBIENT) * jnp.abs(
            0.64 * grad_depth + 0.6 * grad_row + 0.48 * grad_col
        ) * lax.rsqrt(
            grad_depth * grad_depth + grad_row * grad_row + grad_col * grad_col + 0.25
        )

    def last_columns():
        group = LANES // total_planes
        first_lane = lane < group
        deepest = lane >= LANES - group
        rightmost = lane % group == group - 1
        cells = field[chunks - 1, total_planes - 1]
        for z in range(total_planes - 1):
            other = roll(field[chunks - 1, z], (z + 1) * group, 1)
            cells = jnp.where((lane >= z * group) & (lane < (z + 1) * group), other, cells)

        def changes(cells):
            return (
                roll(cells, -group, 1) - cells,
                roll(cells, -1, 0) - cells,
                roll(cells, -1, 1) - cells,
            )

        for sweep in range(PASSES):
            below, down, right = changes(cells)
            below = jnp.where(deepest, 0.0, flux(below))
            down = flux(down)
            right = jnp.where(rightmost, 0.0, flux(right))
            summed = (
                (below - roll(below, group, 1))
                + (down - roll(down, 1, 0))
                + (right - roll(right, 1, 1))
            )
            cells = cells + TIME_STEP * summed
        below, down, right = changes(cells)
        below = jnp.where(deepest, 0.0, below)
        right = jnp.where(rightmost, 0.0, right)
        shading = shading_of(
            (below + roll(below, group, 1))[:strip] * 0.5,
            (down + roll(down, 1, 0))[:strip] * 0.5,
            (right + roll(right, 1, 1))[:strip] * 0.5,
        )
        mixed = transfer(cells[:strip])
        through = jnp.exp(mixed[3] * (-OPTICAL_DEPTH / total_planes))
        ahead = [group * 2**i for i in range((total_planes - 1).bit_length())]
        for shift in ahead:
            through = through * jnp.where(lane[:strip] < shift, 1.0, roll(through, shift, 1))
        remaining = jnp.where(first_lane[:strip], 1.0, roll(through, group, 1))
        weight = (remaining - through) * shading
        result = []
        for channel in range(3):
            color = weight * mixed[channel]
            for shift in ahead:
                color = color + roll(color, shift, 1)
            result.append(color)
        return result + [through]

    def shade(c):
        cells, sides = stage(c, PASSES)

        def plane(z, carry):
            here, center, nearer, remaining, colors = carry
            here_below, center_below = cells(z + 1)
            down = roll(center, -1, 0) - center
            right, left = sides(z, here - center)
            middle = center[:strip]
            grad_depth = (center_below[:strip] - nearer) * 0.5
            grad_row = (down + roll(down, 1, 0))[:strip] * 0.5
            grad_col = (right + left)[:strip] * 0.5
            shading = shading_of(grad_depth, grad_row, grad_col)
            mixed = transfer(middle)
            through = jnp.exp(mixed[3] * (-OPTICAL_DEPTH / total_planes))
            kept = remaining * through
            weight = (remaining - kept) * shading
            colors = tuple(colors[i] + weight * mixed[i] for i in range(3))
            return here_below, center_below, middle, kept, colors

        def step(block, carry):
            for u in range(UNROLL):
                carry = plane(block * UNROLL + u, carry)
            return carry

        here, center = cells(0)
        flat = jnp.zeros((strip, LANES), jnp.float32)
        carry = (here, center, center[:strip], jnp.ones_like(flat), (flat,) * 3)
        carry = lax.fori_loop(0, total_planes // UNROLL, step, carry)
        for channel in range(3):
            shifted[c, channel] = carry[4][channel]
        shifted[c, 3] = carry[3]

    @pl.loop(0, chunks)
    def _(c):
        for k in order:
            source = lax.rem(d + k, depth_count)
            landing(field.at[c, pl.ds(source * planes, planes)], recv.at[source, c]).wait()

        @pl.when(d == 0)
        def _():
            merge(c, jnp.logical_and(jnp.logical_not(upper), r > 0))

        @pl.when(d == depth_count - 1)
        def _():
            merge(c, jnp.logical_and(upper, r < rows_count - 1))

        field[c, total_planes] = field[c, total_planes - 1]
        for p in range(PASSES):
            diffuse(c, p)
        shade(c)

    ending = last_columns()
    early = lane[:strip] < LANES - HALO
    for c in range(chunks):
        for channel in range(4):
            beyond = roll(shifted[c + 1, channel], -HALO, 1) if c < chunks - 1 else ending[channel]
            picture[channel, :, c * LANES : (c + 1) * LANES] = jnp.where(
                early, roll(shifted[c, channel], -HALO, 1), beyond
            )

    for c in range(chunks):
        for k in order:
            parcel(lax.rem(d + k, depth_count), c, k).wait_send()
    for copy in edge_copies():
        copy.wait_send()


def in_one_kernel(depth_count, rows_count, density, transfer_table):
    planes, band, columns = density.shape
    strip = band // depth_count
    chunks = columns // LANES
    total_planes = planes * depth_count
    tall = strip + TILE
    return pl.pallas_call(
        functools.partial(volume_kernel, depth_count, rows_count),
        out_shape=jax.ShapeDtypeStruct((4, strip, columns), jnp.float32),
        in_specs=[pl.BlockSpec(memory_space=pltpu.HBM)] * 2,
        out_specs=pl.BlockSpec(memory_space=pltpu.VMEM),
        scratch_shapes=[
            pltpu.VMEM((planes, band, columns), jnp.float32),
            pltpu.SMEM(transfer_table.shape, jnp.float32),
            pltpu.VMEM((depth_count, chunks, planes, tall, LANES), jnp.float32),
            pltpu.VMEM((depth_count + 1, planes, chunks, TILE, LANES), jnp.float32),
            pltpu.VMEM((chunks, total_planes + 1, tall, LANES), jnp.float32),
            pltpu.VMEM((PASSES, total_planes + 1, tall, LANES), jnp.float32),
            pltpu.VMEM((PASSES + 1, total_planes + 1, tall, LANES), jnp.float32),
            pltpu.VMEM((PASSES + 1, total_planes + 1, tall, LANES), jnp.float32),
            pltpu.VMEM((8, TILE, LANES), jnp.float32),
            pltpu.VMEM((chunks, 4, strip, LANES), jnp.float32),
            pltpu.SemaphoreType.DMA,
            pltpu.SemaphoreType.DMA,
            pltpu.SemaphoreType.DMA((depth_count, chunks)),
            pltpu.SemaphoreType.DMA((depth_count, chunks)),
            pltpu.SemaphoreType.DMA((2,)),
            pltpu.SemaphoreType.DMA((depth_count,)),
        ],
        compiler_params=pltpu.CompilerParams(
            collective_id=0, has_side_effects=True, vmem_limit_bytes=56 * 2**20
        ),
    )(density, transfer_table)


def fits_one_kernel(depth_count, rows_count, density):
    planes, band, columns = density.shape
    strip = band // depth_count
    total_planes = planes * depth_count
    return (
        depth_count > 1
        and rows_count > 1
        and band % depth_count == 0
        and strip % TILE == 0
        and HALO * 2 == TILE
        and columns % LANES == 0
        and total_planes % UNROLL == 0
        and total_planes * 2 * HALO == LANES
        and planes * columns * band + 24 * (total_planes + 1) * (strip + TILE) * LANES < 2**22
    )


def choose(density, transfer_table):
    depth_count = lax.axis_size("depth")
    rows_count = lax.axis_size("rows")
    if fits_one_kernel(depth_count, rows_count, density):
        result = in_one_kernel(depth_count, rows_count, density, transfer_table)
        last = lax.broadcasted_iota(jnp.int32, result.shape, 0) == 3
        return jnp.where(last, 1.0 - result, result)
    return per_device(density, transfer_table)


def solution(mesh):
    placed = (P("depth", "rows", None), P())
    return jax.shard_map(
        choose,
        mesh=mesh,
        in_specs=placed,
        out_specs=P(None, ("rows", "depth"), None),
        check_vma=False,
    )
```

```python
import functools

import jax
import jax.numpy as jnp
from jax import lax
from jax.experimental import pallas as pl
from jax.experimental.pallas import tpu as pltpu
from jax.sharding import PartitionSpec as P

PASSES = 3
KNOTS = 16


TIME_STEP = 0.15
OPTICAL_DEPTH = 3.0
UPPER_DENSITY = 6.0
AMBIENT = 0.35


def extended(cells, sides, width):
    for axis, dim in sides:
        count = lax.axis_size(axis)
        ends = count - 1
        head = lax.slice_in_dim(cells, 0, width, axis=dim)
        tail = lax.slice_in_dim(cells, cells.shape[dim] - width, cells.shape[dim], axis=dim)
        cells = jnp.concatenate(
            [
                lax.ppermute(tail, axis, [(i, (i + 1) % count) for i in range(ends)]),
                cells,
                lax.ppermute(head, axis, [((i + 1) % count, i) for i in range(ends)]),
            ],
            axis=dim,
        )
    return cells


def partner(value, axis, stride):
    mask = 2**stride
    pairs = [(source, source ^ mask) for source in range(lax.axis_size(axis))]
    return lax.ppermute(value, axis, pairs)


def diffusion_flux(center, neighbours):
    summed = jnp.zeros_like(center)
    for other in neighbours:
        change = other - center
        summed = summed + change / (1.0 + change * change)
    return center + TIME_STEP * summed


def appearance(center, neighbours, transfer_table, depth_count):
    deeper, nearer, next_row, prev_row, next_col, prev_col = neighbours
    grad_depth = (deeper - nearer) * 0.5
    grad_row = (next_row - prev_row) * 0.5
    grad_col = (next_col - prev_col) * 0.5
    shading = AMBIENT + (1.0 - AMBIENT) * jnp.abs(
        0.64 * grad_depth + 0.6 * grad_row + 0.48 * grad_col
    ) / jnp.sqrt(grad_depth * grad_depth + grad_row * grad_row + grad_col * grad_col + 0.25)
    position = center * ((KNOTS - 1) / UPPER_DENSITY)
    mixed = [jnp.zeros_like(center) for channel in range(4)]
    for knot in range(KNOTS):
        hat_weight = jnp.maximum(0.0, 1.0 - jnp.abs(position - knot))
        mixed = [
            mixed[channel] + transfer_table[channel, knot] * hat_weight for channel in range(4)
        ]
    opacity = 1.0 - jnp.exp(-mixed[3] * (OPTICAL_DEPTH / depth_count))
    colors = jnp.stack([mixed[0] * shading, mixed[1] * shading, mixed[2] * shading])
    return (colors, opacity)


def neighbour_fields(field):
    padded = extended(field, (("depth", 0), ("rows", 1)), 1)
    depth_index = lax.axis_index("depth")
    depth_count = lax.axis_size("depth")
    rows_index = lax.axis_index("rows")
    rows_count = lax.axis_size("rows")
    above = jnp.where(depth_index == 0, field[:1], padded[:1, 1:-1])
    below = jnp.where(depth_index == depth_count - 1, field[-1:], padded[-1:, 1:-1])
    first_row = jnp.where(rows_index == 0, field[:, :1], padded[1:-1, :1])
    last_row = jnp.where(rows_index == rows_count - 1, field[:, -1:], padded[1:-1, -1:])
    deeper = jnp.concatenate([field[1:], below], axis=0)
    nearer = jnp.concatenate([above, field[:-1]], axis=0)
    next_row = jnp.concatenate([field[:, 1:], last_row], axis=1)
    prev_row = jnp.concatenate([first_row, field[:, :-1]], axis=1)
    next_col = jnp.concatenate([field[:, :, 1:], field[:, :, -1:]], axis=2)
    prev_col = jnp.concatenate([field[:, :, :1], field[:, :, :-1]], axis=2)
    return (deeper, nearer, next_row, prev_row, next_col, prev_col)


def composite(front_part, back_part):
    return front_part + (1.0 - front_part[3:4]) * back_part


def per_device(density, transfer_table):
    planes_here = density.shape[0]
    band_rows = density.shape[1]
    columns = density.shape[2]
    depth_count = lax.axis_size("depth")
    depth_index = lax.axis_index("depth")
    total_planes = planes_here * depth_count
    field = density
    for sweep in range(PASSES):
        field = diffusion_flux(field, neighbour_fields(field))
    colors, opacity = appearance(field, neighbour_fields(field), transfer_table, total_planes)
    color_sum = jnp.zeros((3, band_rows, columns), jnp.float32)
    remaining = jnp.ones((band_rows, columns), jnp.float32)
    for plane in range(planes_here):
        color_sum = color_sum + remaining * opacity[plane] * colors[:, plane]
        remaining = remaining * (1.0 - opacity[plane])
    partial_value = jnp.concatenate([color_sum, (1.0 - remaining)[None]], axis=0)
    strip_rows = band_rows // depth_count
    current = partial_value.reshape(4, depth_count, strip_rows, columns)
    levels = depth_count.bit_length() - 1
    for bit in range(levels):
        blocks = current.shape[1]
        paired = current.reshape(4, blocks // 2, 2, strip_rows, columns)
        own_bit = depth_index // 2**bit % 2
        kept_half = jnp.where(own_bit == 0, paired[:, :, 0], paired[:, :, 1])
        sent_half = jnp.where(own_bit == 0, paired[:, :, 1], paired[:, :, 0])
        received = partner(sent_half, "depth", bit)
        front_part = jnp.where(own_bit == 0, kept_half, received)
        back_part = jnp.where(own_bit == 0, received, kept_half)
        current = composite(front_part, back_part)
    return current.reshape(4, strip_rows, columns)


HALO = PASSES + 1
TILE = 8
LANES = 128
UNROLL = 16


def flux(change):
    denominator = 1.0 + change * change
    guess = pl.reciprocal(denominator, approx=True)
    return change * (guess * (2.0 - denominator * guess))


def roll(cells, shift, axis):
    return pltpu.roll(cells, shift % cells.shape[axis], axis)


def lookup(entries, index):
    return jnp.take_along_axis(entries, index, axis=1)


def volume_kernel(
    depth_count,
    rows_count,
    density,
    transfer_table,
    picture,
    local,
    table,
    parcels,
    edges,
    field,
    later,
    rolled,
    side,
    knots,
    shifted,
    load_sem,
    table_sem,
    send,
    recv,
    edge_send,
    edge_recv,
):
    planes, band, columns = local.shape
    strip = band // depth_count
    chunks = columns // LANES
    total_planes = planes * depth_count
    tall = strip + TILE
    d = lax.axis_index("depth")
    r = lax.axis_index("rows")
    next_rows = lax.rem(r + 1, rows_count)
    prev_rows = lax.rem(r + rows_count - 1, rows_count)
    order = sorted(range(1, depth_count), key=lambda k: abs(k - depth_count // 2))
    odd = lax.rem(d, 2)

    def peer_of(k):
        return lax.rem(d + k + odd * (depth_count - 2 * k), depth_count)

    load = pltpu.make_async_copy(density, local, load_sem)
    load.start()
    load_table = pltpu.make_async_copy(transfer_table, table, table_sem)
    load_table.start()

    barrier = pltpu.get_barrier_semaphore()

    def greet(depth, rows):
        pl.semaphore_signal(
            barrier, inc=1, device_id=(depth, rows), device_id_type=pl.DeviceIdType.MESH
        )

    for k in order:
        greet(peer_of(k), r)

    @pl.when(d == 0)
    def _():
        for s in range(depth_count):
            greet(s, prev_rows)

    @pl.when(d == depth_count - 1)
    def _():
        for s in range(depth_count):
            greet(s, next_rows)

    def flipped(rows, first):
        return jnp.concatenate([rows[first - i : first - i + 1] for i in range(HALO)], axis=0)

    load.wait()
    for c in range(chunks):
        lanes = slice(c * LANES, (c + 1) * LANES)
        for p in range(planes):
            first = local[p, :TILE, lanes]
            final = local[p, band - TILE :, lanes]
            edges[depth_count, p, c] = jnp.concatenate([first[:HALO], final[HALO:]], axis=0)
            for s in range(depth_count):
                parcels[s, c, p, :strip, :] = local[p, s * strip : (s + 1) * strip, lanes]
                if s == 0:
                    before = flipped(first, HALO - 1)
                else:
                    before = local[p, s * strip - TILE : s * strip, lanes][HALO:]
                if s == depth_count - 1:
                    after = flipped(final, TILE - 1)
                else:
                    after = local[p, (s + 1) * strip : (s + 1) * strip + TILE, lanes][:HALO]
                parcels[s, c, p, strip:, :] = jnp.concatenate([after, before], axis=0)

    def parcel(peer, c, slot):
        return pltpu.make_async_remote_copy(
            src_ref=parcels.at[peer, c],
            dst_ref=field.at[c, pl.ds(d * planes, planes)],
            send_sem=send.at[slot, c],
            recv_sem=recv.at[d, c],
            device_id=(peer, r),
            device_id_type=pl.DeviceIdType.MESH,
        )

    def edge_copies():
        return [
            pltpu.make_async_remote_copy(
                src_ref=edges.at[depth_count],
                dst_ref=edges.at[d],
                send_sem=edge_send.at[slot],
                recv_sem=edge_recv.at[d],
                device_id=(depth, rows),
                device_id_type=pl.DeviceIdType.MESH,
            )
            for slot, depth, rows in ((0, depth_count - 1, prev_rows), (1, 0, next_rows))
        ]

    def landing(ref, sem):
        return pltpu.make_async_copy(ref, ref, sem)

    pl.semaphore_wait(barrier, depth_count + 1)
    for copy in edge_copies():
        copy.start()
    for c in range(chunks):
        for k in order:
            parcel(peer_of(k), c, k).start()

    for c in range(chunks):
        for p in range(planes):
            field[c, d * planes + p] = parcels[d, c, p]
    dark = jnp.zeros((tall, LANES), jnp.float32)

    @pl.loop(0, total_planes + 1)
    def _(z):
        for p in range(PASSES + 1):
            rolled[p, z] = dark
            side[p, z] = dark

    load_table.wait()
    entry = lax.broadcasted_iota(jnp.int32, (TILE, LANES), 1)
    for channel in range(4):
        value = jnp.zeros((TILE, LANES), jnp.float32)
        slope = jnp.zeros((TILE, LANES), jnp.float32)
        for knot in range(KNOTS - 1):
            start = table[channel, knot]
            value = jnp.where(entry == knot, start, value)
            slope = jnp.where(entry == knot, table[channel, knot + 1] - start, slope)
        knots[channel] = value
        knots[4 + channel] = slope

    lane = lax.broadcasted_iota(jnp.int32, (tall, LANES), 1)
    lane_zero = lane == 0
    upper = lax.broadcasted_iota(jnp.int32, (TILE, LANES), 0) < HALO

    def merge(c, replaced):
        for s in range(depth_count):
            for p in range(planes):
                z = s * planes + p
                field[c, z, strip:, :] = jnp.where(
                    replaced, edges[s, p, c], field[c, z, strip:, :]
                )

    @pl.when((d == 0) | (d == depth_count - 1))
    def _():
        for s in range(depth_count):
            landing(edges.at[s], edge_recv.at[s]).wait()

    def stage(c, p):
        inner = lane > jnp.where(c == 0, p, -1)

        def cells(z):
            here = field[c, z] if p == 0 else later[p - 1, z]
            moved = roll(here, 1, 1)
            center = jnp.where(lane_zero, rolled[p, z], moved)
            rolled[p, z] = moved
            return here, center

        def sides(z, value):
            value = jnp.where(inner, value, 0.0)
            moved = roll(value, 1, 1)
            before = jnp.where(lane_zero, side[p, z], moved)
            side[p, z] = moved
            return value, before

        return cells, sides

    def diffuse(c, p):
        cells, sides = stage(c, p)

        def plane(z, carry):
            here, center, above = carry
            here_below, center_below = cells(z + 1)
            below = flux(center_below - center)
            down = flux(roll(center, -1, 0) - center)
            right, left = sides(z, flux(here - center))
            summed = (below - above) + (down - roll(down, 1, 0)) + (right - left)
            result = center + TIME_STEP * summed
            later[p, z] = result
            return (here_below, center_below, below), result

        def step(block, carry):
            for u in range(UNROLL):
                carry, result = plane(block * UNROLL + u, carry)

            later[p, total_planes] = result
            return carry

        here, center = cells(0)
        lax.fori_loop(0, total_planes // UNROLL, step, (here, center, dark))

    def transfer(cells):
        position = cells * ((KNOTS - 1) / UPPER_DENSITY)
        index = jnp.clip(position.astype(jnp.int32), 0, KNOTS - 2)
        part = position - index.astype(jnp.float32)
        tiles = [index[i : i + TILE] for i in range(0, strip, TILE)]
        mixed = []
        for channel in range(4):
            value = jnp.concatenate([lookup(knots[channel], tile) for tile in tiles], axis=0)
            slope = jnp.concatenate([lookup(knots[4 + channel], tile) for tile in tiles], axis=0)
            mixed.append(value + part * slope)
        return mixed

    def shading_of(grad_depth, grad_row, grad_col):
        return AMBIENT + (1.0 - AMBIENT) * jnp.abs(
            0.64 * grad_depth + 0.6 * grad_row + 0.48 * grad_col
        ) * lax.rsqrt(
            grad_depth * grad_depth + grad_row * grad_row + grad_col * grad_col + 0.25
        )

    def last_columns():
        group = LANES // total_planes
        first_lane = lane < group
        deepest = lane >= LANES - group
        rightmost = lane % group == group - 1
        cells = field[chunks - 1, total_planes - 1]
        for z in range(total_planes - 1):
            other = roll(field[chunks - 1, z], (z + 1) * group, 1)
            cells = jnp.where((lane >= z * group) & (lane < (z + 1) * group), other, cells)

        def changes(cells):
            return (
                roll(cells, -group, 1) - cells,
                roll(cells, -1, 0) - cells,
                roll(cells, -1, 1) - cells,
            )

        for sweep in range(PASSES):
            below, down, right = changes(cells)
            below = jnp.where(deepest, 0.0, flux(below))
            down = flux(down)
            right = jnp.where(rightmost, 0.0, flux(right))
            summed = (
                (below - roll(below, group, 1))
                + (down - roll(down, 1, 0))
                + (right - roll(right, 1, 1))
            )
            cells = cells + TIME_STEP * summed
        below, down, right = changes(cells)
        below = jnp.where(deepest, 0.0, below)
        right = jnp.where(rightmost, 0.0, right)
        shading = shading_of(
            (below + roll(below, group, 1))[:strip] * 0.5,
            (down + roll(down, 1, 0))[:strip] * 0.5,
            (right + roll(right, 1, 1))[:strip] * 0.5,
        )
        mixed = transfer(cells[:strip])
        through = jnp.exp(mixed[3] * (-OPTICAL_DEPTH / total_planes))
        ahead = [group * 2**i for i in range((total_planes - 1).bit_length())]
        for shift in ahead:
            through = through * jnp.where(lane[:strip] < shift, 1.0, roll(through, shift, 1))
        remaining = jnp.where(first_lane[:strip], 1.0, roll(through, group, 1))
        weight = (remaining - through) * shading
        result = []
        for channel in range(3):
            color = weight * mixed[channel]
            for shift in ahead:
                color = color + roll(color, shift, 1)
            result.append(color)
        return result + [1.0 - through]

    def shade(c):
        cells, sides = stage(c, PASSES)

        def plane(z, carry):
            here, center, nearer, remaining, colors = carry
            here_below, center_below = cells(z + 1)
            down = roll(center, -1, 0) - center
            right, left = sides(z, here - center)
            middle = center[:strip]
            grad_depth = (center_below[:strip] - nearer) * 0.5
            grad_row = (down + roll(down, 1, 0))[:strip] * 0.5
            grad_col = (right + left)[:strip] * 0.5
            shading = shading_of(grad_depth, grad_row, grad_col)
            mixed = transfer(middle)
            through = jnp.exp(mixed[3] * (-OPTICAL_DEPTH / total_planes))
            kept = remaining * through
            weight = (remaining - kept) * shading
            colors = tuple(colors[i] + weight * mixed[i] for i in range(3))
            return here_below, center_below, middle, kept, colors

        def step(block, carry):
            for u in range(UNROLL):
                carry = plane(block * UNROLL + u, carry)
            return carry

        here, center = cells(0)
        flat = jnp.zeros((strip, LANES), jnp.float32)
        carry = (here, center, center[:strip], jnp.ones_like(flat), (flat,) * 3)
        carry = lax.fori_loop(0, total_planes // UNROLL, step, carry)
        for channel in range(3):
            shifted[c, channel] = carry[4][channel]
        shifted[c, 3] = 1.0 - carry[3]

    @pl.loop(0, chunks)
    def _(c):
        for k in order:
            source = lax.rem(d + k, depth_count)
            landing(field.at[c, pl.ds(source * planes, planes)], recv.at[source, c]).wait()

        @pl.when(d == 0)
        def _():
            merge(c, jnp.logical_and(jnp.logical_not(upper), r > 0))

        @pl.when(d == depth_count - 1)
        def _():
            merge(c, jnp.logical_and(upper, r < rows_count - 1))

        field[c, total_planes] = field[c, total_planes - 1]
        for p in range(PASSES):
            diffuse(c, p)
        shade(c)

    ending = last_columns()
    early = lane[:strip] < LANES - HALO
    for c in range(chunks):
        for channel in range(4):
            beyond = roll(shifted[c + 1, channel], -HALO, 1) if c < chunks - 1 else ending[channel]
            picture[channel, :, c * LANES : (c + 1) * LANES] = jnp.where(
                early, roll(shifted[c, channel], -HALO, 1), beyond
            )

    for c in range(chunks):
        for k in order:
            parcel(peer_of(k), c, k).wait_send()
    for copy in edge_copies():
        copy.wait_send()


def in_one_kernel(depth_count, rows_count, density, transfer_table):
    planes, band, columns = density.shape
    strip = band // depth_count
    chunks = columns // LANES
    total_planes = planes * depth_count
    tall = strip + TILE
    return pl.pallas_call(
        functools.partial(volume_kernel, depth_count, rows_count),
        out_shape=jax.ShapeDtypeStruct((4, strip, columns), jnp.float32),
        in_specs=[pl.BlockSpec(memory_space=pltpu.HBM)] * 2,
        out_specs=pl.BlockSpec(memory_space=pltpu.VMEM),
        scratch_shapes=[
            pltpu.VMEM((planes, band, columns), jnp.float32),
            pltpu.SMEM(transfer_table.shape, jnp.float32),
            pltpu.VMEM((depth_count, chunks, planes, tall, LANES), jnp.float32),
            pltpu.VMEM((depth_count + 1, planes, chunks, TILE, LANES), jnp.float32),
            pltpu.VMEM((chunks, total_planes + 1, tall, LANES), jnp.float32),
            pltpu.VMEM((PASSES, total_planes + 1, tall, LANES), jnp.float32),
            pltpu.VMEM((PASSES + 1, total_planes + 1, tall, LANES), jnp.float32),
            pltpu.VMEM((PASSES + 1, total_planes + 1, tall, LANES), jnp.float32),
            pltpu.VMEM((8, TILE, LANES), jnp.float32),
            pltpu.VMEM((chunks, 4, strip, LANES), jnp.float32),
            pltpu.SemaphoreType.DMA,
            pltpu.SemaphoreType.DMA,
            pltpu.SemaphoreType.DMA((depth_count, chunks)),
            pltpu.SemaphoreType.DMA((depth_count, chunks)),
            pltpu.SemaphoreType.DMA((2,)),
            pltpu.SemaphoreType.DMA((depth_count,)),
        ],
        compiler_params=pltpu.CompilerParams(
            collective_id=0, has_side_effects=True, vmem_limit_bytes=24 * 2**20
        ),
    )(*[pltpu.with_memory_space_constraint(x, pltpu.HBM) for x in (density, transfer_table)])


def fits_one_kernel(depth_count, rows_count, density):
    planes, band, columns = density.shape
    strip = band // depth_count
    total_planes = planes * depth_count
    return (
        depth_count > 1
        and rows_count > 1
        and band % depth_count == 0
        and strip % TILE == 0
        and HALO * 2 == TILE
        and columns % LANES == 0
        and total_planes % UNROLL == 0
        and total_planes * 2 * HALO == LANES
        and planes * columns * band + 24 * (total_planes + 1) * (strip + TILE) * LANES < 2**22
    )


def choose(density, transfer_table):
    depth_count = lax.axis_size("depth")
    rows_count = lax.axis_size("rows")
    if fits_one_kernel(depth_count, rows_count, density):
        return in_one_kernel(depth_count, rows_count, density, transfer_table)
    return per_device(density, transfer_table)


def solution(mesh):
    placed = (P("depth", "rows", None), P())
    return jax.shard_map(
        choose,
        mesh=mesh,
        in_specs=placed,
        out_specs=P(None, ("rows", "depth"), None),
        check_vma=False,
    )
```

```python
import functools

import jax
import jax.numpy as jnp
from jax import lax
from jax.experimental import pallas as pl
from jax.experimental.pallas import tpu as pltpu
from jax.sharding import PartitionSpec as P

PASSES = 3
KNOTS = 16


TIME_STEP = 0.15
OPTICAL_DEPTH = 3.0
UPPER_DENSITY = 6.0
AMBIENT = 0.35


def extended(cells, sides, width):
    for axis, dim in sides:
        count = lax.axis_size(axis)
        ends = count - 1
        head = lax.slice_in_dim(cells, 0, width, axis=dim)
        tail = lax.slice_in_dim(cells, cells.shape[dim] - width, cells.shape[dim], axis=dim)
        cells = jnp.concatenate(
            [
                lax.ppermute(tail, axis, [(i, (i + 1) % count) for i in range(ends)]),
                cells,
                lax.ppermute(head, axis, [((i + 1) % count, i) for i in range(ends)]),
            ],
            axis=dim,
        )
    return cells


def partner(value, axis, stride):
    mask = 2**stride
    pairs = [(source, source ^ mask) for source in range(lax.axis_size(axis))]
    return lax.ppermute(value, axis, pairs)


def diffusion_flux(center, neighbours):
    summed = jnp.zeros_like(center)
    for other in neighbours:
        change = other - center
        summed = summed + change / (1.0 + change * change)
    return center + TIME_STEP * summed


def appearance(center, neighbours, transfer_table, depth_count):
    deeper, nearer, next_row, prev_row, next_col, prev_col = neighbours
    grad_depth = (deeper - nearer) * 0.5
    grad_row = (next_row - prev_row) * 0.5
    grad_col = (next_col - prev_col) * 0.5
    shading = AMBIENT + (1.0 - AMBIENT) * jnp.abs(
        0.64 * grad_depth + 0.6 * grad_row + 0.48 * grad_col
    ) / jnp.sqrt(grad_depth * grad_depth + grad_row * grad_row + grad_col * grad_col + 0.25)
    position = center * ((KNOTS - 1) / UPPER_DENSITY)
    mixed = [jnp.zeros_like(center) for channel in range(4)]
    for knot in range(KNOTS):
        hat_weight = jnp.maximum(0.0, 1.0 - jnp.abs(position - knot))
        mixed = [
            mixed[channel] + transfer_table[channel, knot] * hat_weight for channel in range(4)
        ]
    opacity = 1.0 - jnp.exp(-mixed[3] * (OPTICAL_DEPTH / depth_count))
    colors = jnp.stack([mixed[0] * shading, mixed[1] * shading, mixed[2] * shading])
    return (colors, opacity)


def neighbour_fields(field):
    padded = extended(field, (("depth", 0), ("rows", 1)), 1)
    depth_index = lax.axis_index("depth")
    depth_count = lax.axis_size("depth")
    rows_index = lax.axis_index("rows")
    rows_count = lax.axis_size("rows")
    above = jnp.where(depth_index == 0, field[:1], padded[:1, 1:-1])
    below = jnp.where(depth_index == depth_count - 1, field[-1:], padded[-1:, 1:-1])
    first_row = jnp.where(rows_index == 0, field[:, :1], padded[1:-1, :1])
    last_row = jnp.where(rows_index == rows_count - 1, field[:, -1:], padded[1:-1, -1:])
    deeper = jnp.concatenate([field[1:], below], axis=0)
    nearer = jnp.concatenate([above, field[:-1]], axis=0)
    next_row = jnp.concatenate([field[:, 1:], last_row], axis=1)
    prev_row = jnp.concatenate([first_row, field[:, :-1]], axis=1)
    next_col = jnp.concatenate([field[:, :, 1:], field[:, :, -1:]], axis=2)
    prev_col = jnp.concatenate([field[:, :, :1], field[:, :, :-1]], axis=2)
    return (deeper, nearer, next_row, prev_row, next_col, prev_col)


def composite(front_part, back_part):
    return front_part + (1.0 - front_part[3:4]) * back_part


def per_device(density, transfer_table):
    planes_here = density.shape[0]
    band_rows = density.shape[1]
    columns = density.shape[2]
    depth_count = lax.axis_size("depth")
    depth_index = lax.axis_index("depth")
    total_planes = planes_here * depth_count
    field = density
    for sweep in range(PASSES):
        field = diffusion_flux(field, neighbour_fields(field))
    colors, opacity = appearance(field, neighbour_fields(field), transfer_table, total_planes)
    color_sum = jnp.zeros((3, band_rows, columns), jnp.float32)
    remaining = jnp.ones((band_rows, columns), jnp.float32)
    for plane in range(planes_here):
        color_sum = color_sum + remaining * opacity[plane] * colors[:, plane]
        remaining = remaining * (1.0 - opacity[plane])
    partial_value = jnp.concatenate([color_sum, (1.0 - remaining)[None]], axis=0)
    strip_rows = band_rows // depth_count
    current = partial_value.reshape(4, depth_count, strip_rows, columns)
    levels = depth_count.bit_length() - 1
    for bit in range(levels):
        blocks = current.shape[1]
        paired = current.reshape(4, blocks // 2, 2, strip_rows, columns)
        own_bit = depth_index // 2**bit % 2
        kept_half = jnp.where(own_bit == 0, paired[:, :, 0], paired[:, :, 1])
        sent_half = jnp.where(own_bit == 0, paired[:, :, 1], paired[:, :, 0])
        received = partner(sent_half, "depth", bit)
        front_part = jnp.where(own_bit == 0, kept_half, received)
        back_part = jnp.where(own_bit == 0, received, kept_half)
        current = composite(front_part, back_part)
    return current.reshape(4, strip_rows, columns)


HALO = PASSES + 1
TILE = 8
LANES = 128
UNROLL = 16


def flux(change):
    denominator = 1.0 + change * change
    guess = pl.reciprocal(denominator, approx=True)
    return change * (guess * (2.0 - denominator * guess))


def roll(cells, shift, axis):
    return pltpu.roll(cells, shift % cells.shape[axis], axis)


def lookup(entries, index):
    return jnp.take_along_axis(entries, index, axis=1)


def volume_kernel(
    depth_count,
    rows_count,
    density,
    transfer_table,
    picture,
    local,
    table,
    parcels,
    edges,
    field,
    later,
    rolled,
    side,
    knots,
    shifted,
    ending,
    load_sem,
    table_sem,
    send,
    recv,
    edge_send,
    edge_recv,
):
    planes, band, columns = local.shape
    strip = band // depth_count
    chunks = columns // LANES
    total_planes = planes * depth_count
    tall = strip + TILE
    d = lax.axis_index("depth")
    r = lax.axis_index("rows")
    next_rows = lax.rem(r + 1, rows_count)
    prev_rows = lax.rem(r + rows_count - 1, rows_count)
    order = sorted(range(1, depth_count), key=lambda k: abs(k - depth_count // 2))
    odd = lax.rem(d, 2)

    def peer_of(k):
        return lax.rem(d + k + odd * (depth_count - 2 * k), depth_count)

    load = pltpu.make_async_copy(density, local, load_sem)
    load.start()
    load_table = pltpu.make_async_copy(transfer_table, table, table_sem)
    load_table.start()

    barrier = pltpu.get_barrier_semaphore()

    def greet(depth, rows):
        pl.semaphore_signal(
            barrier, inc=1, device_id=(depth, rows), device_id_type=pl.DeviceIdType.MESH
        )

    for k in order:
        greet(peer_of(k), r)

    @pl.when(d == 0)
    def _():
        for s in range(depth_count):
            greet(s, prev_rows)

    @pl.when(d == depth_count - 1)
    def _():
        for s in range(depth_count):
            greet(s, next_rows)

    def flipped(rows, first):
        return jnp.concatenate([rows[first - i : first - i + 1] for i in range(HALO)], axis=0)

    load.wait()
    for c in range(chunks):
        lanes = slice(c * LANES, (c + 1) * LANES)
        for p in range(planes):
            first = local[p, :TILE, lanes]
            final = local[p, band - TILE :, lanes]
            at = p % 2 * HALO
            edges[depth_count, p // 2, c, at : at + HALO, :] = first[:HALO]
            edges[depth_count + 1, p // 2, c, at : at + HALO, :] = final[HALO:]
            for s in range(depth_count):
                parcels[s, c, p, :strip, :] = local[p, s * strip : (s + 1) * strip, lanes]
                if s == 0:
                    before = flipped(first, HALO - 1)
                else:
                    before = local[p, s * strip - TILE : s * strip, lanes][HALO:]
                if s == depth_count - 1:
                    after = flipped(final, TILE - 1)
                else:
                    after = local[p, (s + 1) * strip : (s + 1) * strip + TILE, lanes][:HALO]
                parcels[s, c, p, strip:, :] = jnp.concatenate([after, before], axis=0)

    def parcel(peer, c, slot):
        return pltpu.make_async_remote_copy(
            src_ref=parcels.at[peer, c],
            dst_ref=field.at[c, pl.ds(d * planes, planes)],
            send_sem=send.at[slot, c],
            recv_sem=recv.at[d, c],
            device_id=(peer, r),
            device_id_type=pl.DeviceIdType.MESH,
        )

    def edge_copies():
        return [
            pltpu.make_async_remote_copy(
                src_ref=edges.at[depth_count + slot],
                dst_ref=edges.at[d],
                send_sem=edge_send.at[slot],
                recv_sem=edge_recv.at[d],
                device_id=(depth, rows),
                device_id_type=pl.DeviceIdType.MESH,
            )
            for slot, depth, rows in ((0, depth_count - 1, prev_rows), (1, 0, next_rows))
        ]

    def landing(ref, sem):
        return pltpu.make_async_copy(ref, ref, sem)

    pl.semaphore_wait(barrier, depth_count + 1)
    for copy in edge_copies():
        copy.start()
    for c in range(chunks):
        for k in order:
            parcel(peer_of(k), c, k).start()

    for c in range(chunks):
        for p in range(planes):
            field[c, d * planes + p] = parcels[d, c, p]
    dark = jnp.zeros((tall, LANES), jnp.float32)

    @pl.loop(0, total_planes + 1)
    def _(z):
        for p in range(PASSES + 1):
            rolled[p, z] = dark
            side[p, z] = dark

    load_table.wait()
    entry = lax.broadcasted_iota(jnp.int32, (TILE, LANES), 1)
    for channel in range(4):
        value = jnp.zeros((TILE, LANES), jnp.float32)
        slope = jnp.zeros((TILE, LANES), jnp.float32)
        for knot in range(KNOTS - 1):
            start = table[channel, knot]
            value = jnp.where(entry == knot, start, value)
            slope = jnp.where(entry == knot, table[channel, knot + 1] - start, slope)
        knots[channel] = value
        knots[4 + channel] = slope

    lane = lax.broadcasted_iota(jnp.int32, (tall, LANES), 1)
    lane_zero = lane == 0
    upper = lax.broadcasted_iota(jnp.int32, (TILE, LANES), 0) < HALO

    def merge(c, first_plane, replaced):
        for s in range(depth_count):
            for p in range(planes):
                z = s * planes + p
                pair = edges[s, p // 2, c]
                rows = pair if p % 2 == first_plane else roll(pair, HALO, 0)
                field[c, z, strip:, :] = jnp.where(replaced, rows, field[c, z, strip:, :])

    @pl.when((d == 0) | (d == depth_count - 1))
    def _():
        for s in range(depth_count):
            landing(edges.at[s], edge_recv.at[s]).wait()

    def stage(c, p):
        inner = lane > jnp.where(c == 0, p, -1)

        def cells(z):
            here = field[c, z] if p == 0 else later[p - 1, z]
            moved = roll(here, 1, 1)
            center = jnp.where(lane_zero, rolled[p, z], moved)
            rolled[p, z] = moved
            return here, center

        def sides(z, value):
            value = jnp.where(inner, value, 0.0)
            moved = roll(value, 1, 1)
            before = jnp.where(lane_zero, side[p, z], moved)
            side[p, z] = moved
            return value, before

        return cells, sides

    def diffuse(c, p):
        cells, sides = stage(c, p)

        def plane(z, carry):
            here, center, above = carry
            here_below, center_below = cells(z + 1)
            below = flux(center_below - center)
            down = flux(roll(center, -1, 0) - center)
            right, left = sides(z, flux(here - center))
            summed = (below - above) + (down - roll(down, 1, 0)) + (right - left)
            result = center + TIME_STEP * summed
            later[p, z] = result
            return (here_below, center_below, below), result

        def step(block, carry):
            for u in range(UNROLL):
                carry, result = plane(block * UNROLL + u, carry)

            later[p, total_planes] = result
            return carry

        here, center = cells(0)
        lax.fori_loop(0, total_planes // UNROLL, step, (here, center, dark))

    def transfer(cells):
        position = cells * ((KNOTS - 1) / UPPER_DENSITY)
        index = jnp.clip(position.astype(jnp.int32), 0, KNOTS - 2)
        part = position - index.astype(jnp.float32)
        tiles = [index[i : i + TILE] for i in range(0, strip, TILE)]
        mixed = []
        for channel in range(4):
            value = jnp.concatenate([lookup(knots[channel], tile) for tile in tiles], axis=0)
            slope = jnp.concatenate([lookup(knots[4 + channel], tile) for tile in tiles], axis=0)
            mixed.append(value + part * slope)
        return mixed

    def shading_of(grad_depth, grad_row, grad_col):
        return AMBIENT + (1.0 - AMBIENT) * jnp.abs(
            0.64 * grad_depth + 0.6 * grad_row + 0.48 * grad_col
        ) * lax.rsqrt(
            grad_depth * grad_depth + grad_row * grad_row + grad_col * grad_col + 0.25
        )

    def last_columns(c):
        group = LANES // total_planes
        first_lane = lane < group
        deepest = lane >= LANES - group
        rightmost = lane % group == group - 1
        cells = field[c, total_planes - 1]
        for z in range(total_planes - 1):
            other = roll(field[c, z], (z + 1) * group, 1)
            cells = jnp.where((lane >= z * group) & (lane < (z + 1) * group), other, cells)

        def changes(cells):
            return (
                roll(cells, -group, 1) - cells,
                roll(cells, -1, 0) - cells,
                roll(cells, -1, 1) - cells,
            )

        for sweep in range(PASSES):
            below, down, right = changes(cells)
            below = jnp.where(deepest, 0.0, flux(below))
            down = flux(down)
            right = jnp.where(rightmost, 0.0, flux(right))
            summed = (
                (below - roll(below, group, 1))
                + (down - roll(down, 1, 0))
                + (right - roll(right, 1, 1))
            )
            cells = cells + TIME_STEP * summed
        below, down, right = changes(cells)
        below = jnp.where(deepest, 0.0, below)
        right = jnp.where(rightmost, 0.0, right)
        shading = shading_of(
            (below + roll(below, group, 1))[:strip] * 0.5,
            (down + roll(down, 1, 0))[:strip] * 0.5,
            (right + roll(right, 1, 1))[:strip] * 0.5,
        )
        mixed = transfer(cells[:strip])
        through = jnp.exp(mixed[3] * (-OPTICAL_DEPTH / total_planes))
        ahead = [group * 2**i for i in range((total_planes - 1).bit_length())]
        for shift in ahead:
            through = through * jnp.where(lane[:strip] < shift, 1.0, roll(through, shift, 1))
        remaining = jnp.where(first_lane[:strip], 1.0, roll(through, group, 1))
        weight = (remaining - through) * shading
        for channel in range(3):
            color = weight * mixed[channel]
            for shift in ahead:
                color = color + roll(color, shift, 1)
            ending[channel] = color
        ending[3] = 1.0 - through

    def shade(c):
        cells, sides = stage(c, PASSES)

        def plane(z, carry):
            here, center, nearer, remaining, colors = carry
            here_below, center_below = cells(z + 1)
            down = roll(center, -1, 0) - center
            right, left = sides(z, here - center)
            middle = center[:strip]
            grad_depth = (center_below[:strip] - nearer) * 0.5
            grad_row = (down + roll(down, 1, 0))[:strip] * 0.5
            grad_col = (right + left)[:strip] * 0.5
            shading = shading_of(grad_depth, grad_row, grad_col)
            mixed = transfer(middle)
            through = jnp.exp(mixed[3] * (-OPTICAL_DEPTH / total_planes))
            kept = remaining * through
            weight = (remaining - kept) * shading
            colors = tuple(colors[i] + weight * mixed[i] for i in range(3))
            return here_below, center_below, middle, kept, colors

        def step(block, carry):
            for u in range(UNROLL):
                carry = plane(block * UNROLL + u, carry)
            return carry

        here, center = cells(0)
        flat = jnp.zeros((strip, LANES), jnp.float32)
        carry = (here, center, center[:strip], jnp.ones_like(flat), (flat,) * 3)
        carry = lax.fori_loop(0, total_planes // UNROLL, step, carry)
        for channel in range(3):
            shifted[c, channel] = carry[4][channel]
        shifted[c, 3] = 1.0 - carry[3]

    @pl.loop(0, chunks)
    def _(c):
        for k in order:
            source = lax.rem(d + k, depth_count)
            landing(field.at[c, pl.ds(source * planes, planes)], recv.at[source, c]).wait()

        @pl.when(d == 0)
        def _():
            merge(c, 1, jnp.logical_and(jnp.logical_not(upper), r > 0))

        @pl.when(d == depth_count - 1)
        def _():
            merge(c, 0, jnp.logical_and(upper, r < rows_count - 1))

        field[c, total_planes] = field[c, total_planes - 1]
        last_columns(c)
        for p in range(PASSES):
            diffuse(c, p)
        shade(c)

    early = lane[:strip] < LANES - HALO
    for c in range(chunks):
        for channel in range(4):
            beyond = roll(shifted[c + 1, channel], -HALO, 1) if c < chunks - 1 else ending[channel]
            picture[channel, :, c * LANES : (c + 1) * LANES] = jnp.where(
                early, roll(shifted[c, channel], -HALO, 1), beyond
            )

    for c in range(chunks):
        for k in order:
            parcel(peer_of(k), c, k).wait_send()
    for copy in edge_copies():
        copy.wait_send()


def in_one_kernel(depth_count, rows_count, density, transfer_table):
    planes, band, columns = density.shape
    strip = band // depth_count
    chunks = columns // LANES
    total_planes = planes * depth_count
    tall = strip + TILE
    return pl.pallas_call(
        functools.partial(volume_kernel, depth_count, rows_count),
        out_shape=jax.ShapeDtypeStruct((4, strip, columns), jnp.float32),
        in_specs=[pl.BlockSpec(memory_space=pltpu.HBM)] * 2,
        out_specs=pl.BlockSpec(memory_space=pltpu.VMEM),
        scratch_shapes=[
            pltpu.VMEM((planes, band, columns), jnp.float32),
            pltpu.SMEM(transfer_table.shape, jnp.float32),
            pltpu.VMEM((depth_count, chunks, planes, tall, LANES), jnp.float32),
            pltpu.VMEM((depth_count + 2, planes // 2, chunks, TILE, LANES), jnp.float32),
            pltpu.VMEM((chunks, total_planes + 1, tall, LANES), jnp.float32),
            pltpu.VMEM((PASSES, total_planes + 1, tall, LANES), jnp.float32),
            pltpu.VMEM((PASSES + 1, total_planes + 1, tall, LANES), jnp.float32),
            pltpu.VMEM((PASSES + 1, total_planes + 1, tall, LANES), jnp.float32),
            pltpu.VMEM((8, TILE, LANES), jnp.float32),
            pltpu.VMEM((chunks, 4, strip, LANES), jnp.float32),
            pltpu.VMEM((4, strip, LANES), jnp.float32),
            pltpu.SemaphoreType.DMA,
            pltpu.SemaphoreType.DMA,
            pltpu.SemaphoreType.DMA((depth_count, chunks)),
            pltpu.SemaphoreType.DMA((depth_count, chunks)),
            pltpu.SemaphoreType.DMA((2,)),
            pltpu.SemaphoreType.DMA((depth_count,)),
        ],
        compiler_params=pltpu.CompilerParams(
            collective_id=0, has_side_effects=True, vmem_limit_bytes=24 * 2**20
        ),
    )(*[pltpu.with_memory_space_constraint(x, pltpu.HBM) for x in (density, transfer_table)])


def fits_one_kernel(depth_count, rows_count, density):
    planes, band, columns = density.shape
    strip = band // depth_count
    total_planes = planes * depth_count
    return (
        depth_count > 1
        and rows_count > 1
        and band % depth_count == 0
        and strip % TILE == 0
        and HALO * 2 == TILE
        and columns % LANES == 0
        and planes % 2 == 0
        and total_planes % UNROLL == 0
        and total_planes * 2 * HALO == LANES
        and planes * columns * band + 24 * (total_planes + 1) * (strip + TILE) * LANES < 2**22
    )


def choose(density, transfer_table):
    depth_count = lax.axis_size("depth")
    rows_count = lax.axis_size("rows")
    if fits_one_kernel(depth_count, rows_count, density):
        return in_one_kernel(depth_count, rows_count, density, transfer_table)
    return per_device(density, transfer_table)


def solution(mesh):
    placed = (P("depth", "rows", None), P())
    return jax.shard_map(
        choose,
        mesh=mesh,
        in_specs=placed,
        out_specs=P(None, ("rows", "depth"), None),
        check_vma=False,
    )
```

```python
import functools

import jax
import jax.numpy as jnp
from jax import lax
from jax.experimental import pallas as pl
from jax.experimental.pallas import tpu as pltpu
from jax.sharding import PartitionSpec as P

PASSES = 3
KNOTS = 16


TIME_STEP = 0.15
OPTICAL_DEPTH = 3.0
UPPER_DENSITY = 6.0
AMBIENT = 0.35


def extended(cells, sides, width):
    for axis, dim in sides:
        count = lax.axis_size(axis)
        ends = count - 1
        head = lax.slice_in_dim(cells, 0, width, axis=dim)
        tail = lax.slice_in_dim(cells, cells.shape[dim] - width, cells.shape[dim], axis=dim)
        cells = jnp.concatenate(
            [
                lax.ppermute(tail, axis, [(i, (i + 1) % count) for i in range(ends)]),
                cells,
                lax.ppermute(head, axis, [((i + 1) % count, i) for i in range(ends)]),
            ],
            axis=dim,
        )
    return cells


def partner(value, axis, stride):
    mask = 2**stride
    pairs = [(source, source ^ mask) for source in range(lax.axis_size(axis))]
    return lax.ppermute(value, axis, pairs)


def diffusion_flux(center, neighbours):
    summed = jnp.zeros_like(center)
    for other in neighbours:
        change = other - center
        summed = summed + change / (1.0 + change * change)
    return center + TIME_STEP * summed


def appearance(center, neighbours, transfer_table, depth_count):
    deeper, nearer, next_row, prev_row, next_col, prev_col = neighbours
    grad_depth = (deeper - nearer) * 0.5
    grad_row = (next_row - prev_row) * 0.5
    grad_col = (next_col - prev_col) * 0.5
    shading = AMBIENT + (1.0 - AMBIENT) * jnp.abs(
        0.64 * grad_depth + 0.6 * grad_row + 0.48 * grad_col
    ) / jnp.sqrt(grad_depth * grad_depth + grad_row * grad_row + grad_col * grad_col + 0.25)
    position = center * ((KNOTS - 1) / UPPER_DENSITY)
    mixed = [jnp.zeros_like(center) for channel in range(4)]
    for knot in range(KNOTS):
        hat_weight = jnp.maximum(0.0, 1.0 - jnp.abs(position - knot))
        mixed = [
            mixed[channel] + transfer_table[channel, knot] * hat_weight for channel in range(4)
        ]
    opacity = 1.0 - jnp.exp(-mixed[3] * (OPTICAL_DEPTH / depth_count))
    colors = jnp.stack([mixed[0] * shading, mixed[1] * shading, mixed[2] * shading])
    return (colors, opacity)


def neighbour_fields(field):
    padded = extended(field, (("depth", 0), ("rows", 1)), 1)
    depth_index = lax.axis_index("depth")
    depth_count = lax.axis_size("depth")
    rows_index = lax.axis_index("rows")
    rows_count = lax.axis_size("rows")
    above = jnp.where(depth_index == 0, field[:1], padded[:1, 1:-1])
    below = jnp.where(depth_index == depth_count - 1, field[-1:], padded[-1:, 1:-1])
    first_row = jnp.where(rows_index == 0, field[:, :1], padded[1:-1, :1])
    last_row = jnp.where(rows_index == rows_count - 1, field[:, -1:], padded[1:-1, -1:])
    deeper = jnp.concatenate([field[1:], below], axis=0)
    nearer = jnp.concatenate([above, field[:-1]], axis=0)
    next_row = jnp.concatenate([field[:, 1:], last_row], axis=1)
    prev_row = jnp.concatenate([first_row, field[:, :-1]], axis=1)
    next_col = jnp.concatenate([field[:, :, 1:], field[:, :, -1:]], axis=2)
    prev_col = jnp.concatenate([field[:, :, :1], field[:, :, :-1]], axis=2)
    return (deeper, nearer, next_row, prev_row, next_col, prev_col)


def composite(front_part, back_part):
    return front_part + (1.0 - front_part[3:4]) * back_part


def per_device(density, transfer_table):
    planes_here = density.shape[0]
    band_rows = density.shape[1]
    columns = density.shape[2]
    depth_count = lax.axis_size("depth")
    depth_index = lax.axis_index("depth")
    total_planes = planes_here * depth_count
    field = density
    for sweep in range(PASSES):
        field = diffusion_flux(field, neighbour_fields(field))
    colors, opacity = appearance(field, neighbour_fields(field), transfer_table, total_planes)
    color_sum = jnp.zeros((3, band_rows, columns), jnp.float32)
    remaining = jnp.ones((band_rows, columns), jnp.float32)
    for plane in range(planes_here):
        color_sum = color_sum + remaining * opacity[plane] * colors[:, plane]
        remaining = remaining * (1.0 - opacity[plane])
    partial_value = jnp.concatenate([color_sum, (1.0 - remaining)[None]], axis=0)
    strip_rows = band_rows // depth_count
    current = partial_value.reshape(4, depth_count, strip_rows, columns)
    levels = depth_count.bit_length() - 1
    for bit in range(levels):
        blocks = current.shape[1]
        paired = current.reshape(4, blocks // 2, 2, strip_rows, columns)
        own_bit = depth_index // 2**bit % 2
        kept_half = jnp.where(own_bit == 0, paired[:, :, 0], paired[:, :, 1])
        sent_half = jnp.where(own_bit == 0, paired[:, :, 1], paired[:, :, 0])
        received = partner(sent_half, "depth", bit)
        front_part = jnp.where(own_bit == 0, kept_half, received)
        back_part = jnp.where(own_bit == 0, received, kept_half)
        current = composite(front_part, back_part)
    return current.reshape(4, strip_rows, columns)


HALO = PASSES + 1
TILE = 8
LANES = 128
UNROLL = 16


def flux(change):
    denominator = 1.0 + change * change
    guess = pl.reciprocal(denominator, approx=True)
    return change * (guess * (2.0 - denominator * guess))


def roll(cells, shift, axis):
    return pltpu.roll(cells, shift % cells.shape[axis], axis)


def lookup(entries, index):
    return jnp.take_along_axis(entries, index, axis=1)


def volume_kernel(
    depth_count,
    rows_count,
    density,
    transfer_table,
    picture,
    local,
    table,
    parcels,
    edges,
    field,
    later,
    rolled,
    side,
    knots,
    shifted,
    ending,
    load_sem,
    table_sem,
    send,
    recv,
    edge_send,
    edge_recv,
):
    planes, band, columns = local.shape
    strip = band // depth_count
    chunks = columns // LANES
    total_planes = planes * depth_count
    tall = strip + TILE
    d = lax.axis_index("depth")
    r = lax.axis_index("rows")
    next_rows = lax.rem(r + 1, rows_count)
    prev_rows = lax.rem(r + rows_count - 1, rows_count)
    order = sorted(range(1, depth_count), key=lambda k: abs(k - depth_count // 2))
    odd = lax.rem(d, 2)

    def peer_of(k):
        return lax.rem(d + k + odd * (depth_count - 2 * k), depth_count)

    def columns_of(c):
        return slice(c * LANES, (c + 1) * LANES)

    loads = [
        pltpu.make_async_copy(
            density.at[:, :, columns_of(c)], local.at[:, :, columns_of(c)], load_sem.at[c]
        )
        for c in range(chunks)
    ]
    for load in loads:
        load.start()
    load_table = pltpu.make_async_copy(transfer_table, table, table_sem)
    load_table.start()

    barrier = pltpu.get_barrier_semaphore()

    def greet(depth, rows):
        pl.semaphore_signal(
            barrier, inc=1, device_id=(depth, rows), device_id_type=pl.DeviceIdType.MESH
        )

    for k in order:
        greet(peer_of(k), r)

    @pl.when(d == 0)
    def _():
        for s in range(depth_count):
            greet(s, prev_rows)

    @pl.when(d == depth_count - 1)
    def _():
        for s in range(depth_count):
            greet(s, next_rows)

    def flipped(rows, first):
        return jnp.concatenate([rows[first - i : first - i + 1] for i in range(HALO)], axis=0)

    def parcel(peer, c, slot):
        return pltpu.make_async_remote_copy(
            src_ref=parcels.at[peer, c],
            dst_ref=field.at[c, pl.ds(d * planes, planes)],
            send_sem=send.at[slot, c],
            recv_sem=recv.at[d, c],
            device_id=(peer, r),
            device_id_type=pl.DeviceIdType.MESH,
        )

    def build(c):
        lanes = columns_of(c)
        for p in range(planes):
            first = local[p, :TILE, lanes]
            final = local[p, band - TILE :, lanes]
            at = p % 2 * HALO
            edges[depth_count, c, p // 2, at : at + HALO, :] = first[:HALO]
            edges[depth_count + 1, c, p // 2, at : at + HALO, :] = final[HALO:]
            for s in range(depth_count):
                parcels[s, c, p, :strip, :] = local[p, s * strip : (s + 1) * strip, lanes]
                if s == 0:
                    before = flipped(first, HALO - 1)
                else:
                    before = local[p, s * strip - TILE : s * strip, lanes][HALO:]
                if s == depth_count - 1:
                    after = flipped(final, TILE - 1)
                else:
                    after = local[p, (s + 1) * strip : (s + 1) * strip + TILE, lanes][:HALO]
                parcels[s, c, p, strip:, :] = jnp.concatenate([after, before], axis=0)

    def edge_copies(c):
        return [
            pltpu.make_async_remote_copy(
                src_ref=edges.at[depth_count + slot, c],
                dst_ref=edges.at[d, c],
                send_sem=edge_send.at[slot, c],
                recv_sem=edge_recv.at[d, c],
                device_id=(depth, rows),
                device_id_type=pl.DeviceIdType.MESH,
            )
            for slot, depth, rows in ((0, depth_count - 1, prev_rows), (1, 0, next_rows))
        ]

    def landing(ref, sem):
        return pltpu.make_async_copy(ref, ref, sem)

    for c in range(chunks):
        loads[c].wait()
        build(c)
        if c == 0:
            pl.semaphore_wait(barrier, depth_count + 1)
        for k in order:
            parcel(peer_of(k), c, k).start()
        for copy in edge_copies(c):
            copy.start()

    for c in range(chunks):
        for p in range(planes):
            field[c, d * planes + p] = parcels[d, c, p]
    dark = jnp.zeros((tall, LANES), jnp.float32)

    @pl.loop(0, total_planes + 1)
    def _(z):
        for p in range(PASSES + 1):
            rolled[p, z] = dark
            side[p, z] = dark

    load_table.wait()
    entry = lax.broadcasted_iota(jnp.int32, (TILE, LANES), 1)
    for channel in range(4):
        value = jnp.zeros((TILE, LANES), jnp.float32)
        slope = jnp.zeros((TILE, LANES), jnp.float32)
        for knot in range(KNOTS - 1):
            start = table[channel, knot]
            value = jnp.where(entry == knot, start, value)
            slope = jnp.where(entry == knot, table[channel, knot + 1] - start, slope)
        knots[channel] = value
        knots[4 + channel] = slope

    lane = lax.broadcasted_iota(jnp.int32, (tall, LANES), 1)
    lane_zero = lane == 0
    upper = lax.broadcasted_iota(jnp.int32, (TILE, LANES), 0) < HALO

    def merge(c, first_plane, replaced):
        for s in range(depth_count):
            landing(edges.at[s, c], edge_recv.at[s, c]).wait()
            for p in range(planes):
                z = s * planes + p
                pair = edges[s, c, p // 2]
                rows = pair if p % 2 == first_plane else roll(pair, HALO, 0)
                field[c, z, strip:, :] = jnp.where(replaced, rows, field[c, z, strip:, :])

    def stage(c, p):
        inner = lane > jnp.where(c == 0, p, -1)

        def cells(z):
            here = field[c, z] if p == 0 else later[p - 1, z]
            moved = roll(here, 1, 1)
            center = jnp.where(lane_zero, rolled[p, z], moved)
            rolled[p, z] = moved
            return here, center

        def sides(z, value):
            value = jnp.where(inner, value, 0.0)
            moved = roll(value, 1, 1)
            before = jnp.where(lane_zero, side[p, z], moved)
            side[p, z] = moved
            return value, before

        return cells, sides

    def diffuse(c, p):
        cells, sides = stage(c, p)

        def plane(z, carry):
            here, center, above = carry
            here_below, center_below = cells(z + 1)
            below = flux(center_below - center)
            down = flux(roll(center, -1, 0) - center)
            right, left = sides(z, flux(here - center))
            summed = (below - above) + (down - roll(down, 1, 0)) + (right - left)
            result = center + TIME_STEP * summed
            later[p, z] = result
            return (here_below, center_below, below), result

        def step(block, carry):
            for u in range(UNROLL):
                carry, result = plane(block * UNROLL + u, carry)

            later[p, total_planes] = result
            return carry

        here, center = cells(0)
        lax.fori_loop(0, total_planes // UNROLL, step, (here, center, dark))

    def transfer(cells):
        position = cells * ((KNOTS - 1) / UPPER_DENSITY)
        index = jnp.clip(position.astype(jnp.int32), 0, KNOTS - 2)
        part = position - index.astype(jnp.float32)
        tiles = [index[i : i + TILE] for i in range(0, strip, TILE)]
        mixed = []
        for channel in range(4):
            value = jnp.concatenate([lookup(knots[channel], tile) for tile in tiles], axis=0)
            slope = jnp.concatenate([lookup(knots[4 + channel], tile) for tile in tiles], axis=0)
            mixed.append(value + part * slope)
        return mixed

    def shading_of(grad_depth, grad_row, grad_col):
        return AMBIENT + (1.0 - AMBIENT) * jnp.abs(
            0.64 * grad_depth + 0.6 * grad_row + 0.48 * grad_col
        ) * lax.rsqrt(
            grad_depth * grad_depth + grad_row * grad_row + grad_col * grad_col + 0.25
        )

    def last_columns(c):
        group = LANES // total_planes
        first_lane = lane < group
        deepest = lane >= LANES - group
        rightmost = lane % group == group - 1
        cells = field[c, total_planes - 1]
        for z in range(total_planes - 1):
            other = roll(field[c, z], (z + 1) * group, 1)
            cells = jnp.where((lane >= z * group) & (lane < (z + 1) * group), other, cells)

        def changes(cells):
            return (
                roll(cells, -group, 1) - cells,
                roll(cells, -1, 0) - cells,
                roll(cells, -1, 1) - cells,
            )

        for sweep in range(PASSES):
            below, down, right = changes(cells)
            below = jnp.where(deepest, 0.0, flux(below))
            down = flux(down)
            right = jnp.where(rightmost, 0.0, flux(right))
            summed = (
                (below - roll(below, group, 1))
                + (down - roll(down, 1, 0))
                + (right - roll(right, 1, 1))
            )
            cells = cells + TIME_STEP * summed
        below, down, right = changes(cells)
        below = jnp.where(deepest, 0.0, below)
        right = jnp.where(rightmost, 0.0, right)
        shading = shading_of(
            (below + roll(below, group, 1))[:strip] * 0.5,
            (down + roll(down, 1, 0))[:strip] * 0.5,
            (right + roll(right, 1, 1))[:strip] * 0.5,
        )
        mixed = transfer(cells[:strip])
        through = jnp.exp(mixed[3] * (-OPTICAL_DEPTH / total_planes))
        ahead = [group * 2**i for i in range((total_planes - 1).bit_length())]
        for shift in ahead:
            through = through * jnp.where(lane[:strip] < shift, 1.0, roll(through, shift, 1))
        remaining = jnp.where(first_lane[:strip], 1.0, roll(through, group, 1))
        weight = (remaining - through) * shading
        for channel in range(3):
            color = weight * mixed[channel]
            for shift in ahead:
                color = color + roll(color, shift, 1)
            ending[channel] = color
        ending[3] = 1.0 - through

    def shade(c):
        cells, sides = stage(c, PASSES)

        def plane(z, carry):
            here, center, nearer, remaining, colors = carry
            here_below, center_below = cells(z + 1)
            down = roll(center, -1, 0) - center
            right, left = sides(z, here - center)
            middle = center[:strip]
            grad_depth = (center_below[:strip] - nearer) * 0.5
            grad_row = (down + roll(down, 1, 0))[:strip] * 0.5
            grad_col = (right + left)[:strip] * 0.5
            shading = shading_of(grad_depth, grad_row, grad_col)
            mixed = transfer(middle)
            through = jnp.exp(mixed[3] * (-OPTICAL_DEPTH / total_planes))
            kept = remaining * through
            weight = (remaining - kept) * shading
            colors = tuple(colors[i] + weight * mixed[i] for i in range(3))
            return here_below, center_below, middle, kept, colors

        def step(block, carry):
            for u in range(UNROLL):
                carry = plane(block * UNROLL + u, carry)
            return carry

        here, center = cells(0)
        flat = jnp.zeros((strip, LANES), jnp.float32)
        carry = (here, center, center[:strip], jnp.ones_like(flat), (flat,) * 3)
        carry = lax.fori_loop(0, total_planes // UNROLL, step, carry)
        for channel in range(3):
            shifted[c, channel] = carry[4][channel]
        shifted[c, 3] = 1.0 - carry[3]

    @pl.loop(0, chunks)
    def _(c):
        for k in order:
            source = lax.rem(d + k, depth_count)
            landing(field.at[c, pl.ds(source * planes, planes)], recv.at[source, c]).wait()

        @pl.when(d == 0)
        def _():
            merge(c, 1, jnp.logical_and(jnp.logical_not(upper), r > 0))

        @pl.when(d == depth_count - 1)
        def _():
            merge(c, 0, jnp.logical_and(upper, r < rows_count - 1))

        field[c, total_planes] = field[c, total_planes - 1]
        last_columns(c)
        for p in range(PASSES):
            diffuse(c, p)
        shade(c)

    early = lane[:strip] < LANES - HALO
    for c in range(chunks):
        for channel in range(4):
            beyond = roll(shifted[c + 1, channel], -HALO, 1) if c < chunks - 1 else ending[channel]
            picture[channel, :, c * LANES : (c + 1) * LANES] = jnp.where(
                early, roll(shifted[c, channel], -HALO, 1), beyond
            )

    for c in range(chunks):
        for k in order:
            parcel(peer_of(k), c, k).wait_send()
        for copy in edge_copies(c):
            copy.wait_send()


def in_one_kernel(depth_count, rows_count, density, transfer_table):
    planes, band, columns = density.shape
    strip = band // depth_count
    chunks = columns // LANES
    total_planes = planes * depth_count
    tall = strip + TILE
    return pl.pallas_call(
        functools.partial(volume_kernel, depth_count, rows_count),
        out_shape=jax.ShapeDtypeStruct((4, strip, columns), jnp.float32),
        in_specs=[pl.BlockSpec(memory_space=pltpu.HBM)] * 2,
        out_specs=pl.BlockSpec(memory_space=pltpu.VMEM),
        scratch_shapes=[
            pltpu.VMEM((planes, band, columns), jnp.float32),
            pltpu.SMEM(transfer_table.shape, jnp.float32),
            pltpu.VMEM((depth_count, chunks, planes, tall, LANES), jnp.float32),
            pltpu.VMEM((depth_count + 2, chunks, planes // 2, TILE, LANES), jnp.float32),
            pltpu.VMEM((chunks, total_planes + 1, tall, LANES), jnp.float32),
            pltpu.VMEM((PASSES, total_planes + 1, tall, LANES), jnp.float32),
            pltpu.VMEM((PASSES + 1, total_planes + 1, tall, LANES), jnp.float32),
            pltpu.VMEM((PASSES + 1, total_planes + 1, tall, LANES), jnp.float32),
            pltpu.VMEM((8, TILE, LANES), jnp.float32),
            pltpu.VMEM((chunks, 4, strip, LANES), jnp.float32),
            pltpu.VMEM((4, strip, LANES), jnp.float32),
            pltpu.SemaphoreType.DMA((chunks,)),
            pltpu.SemaphoreType.DMA,
            pltpu.SemaphoreType.DMA((depth_count, chunks)),
            pltpu.SemaphoreType.DMA((depth_count, chunks)),
            pltpu.SemaphoreType.DMA((2, chunks)),
            pltpu.SemaphoreType.DMA((depth_count, chunks)),
        ],
        compiler_params=pltpu.CompilerParams(
            collective_id=0, has_side_effects=True, vmem_limit_bytes=24 * 2**20
        ),
    )(*[pltpu.with_memory_space_constraint(x, pltpu.HBM) for x in (density, transfer_table)])


def fits_one_kernel(depth_count, rows_count, density):
    planes, band, columns = density.shape
    strip = band // depth_count
    total_planes = planes * depth_count
    return (
        depth_count > 1
        and rows_count > 1
        and band % depth_count == 0
        and strip % TILE == 0
        and HALO * 2 == TILE
        and columns % LANES == 0
        and planes % 2 == 0
        and total_planes % UNROLL == 0
        and total_planes * 2 * HALO == LANES
        and planes * columns * band + 24 * (total_planes + 1) * (strip + TILE) * LANES < 2**22
    )


def choose(density, transfer_table):
    depth_count = lax.axis_size("depth")
    rows_count = lax.axis_size("rows")
    if fits_one_kernel(depth_count, rows_count, density):
        return in_one_kernel(depth_count, rows_count, density, transfer_table)
    return per_device(density, transfer_table)


def solution(mesh):
    placed = (P("depth", "rows", None), P())
    return jax.shard_map(
        choose,
        mesh=mesh,
        in_specs=placed,
        out_specs=P(None, ("rows", "depth"), None),
        check_vma=False,
    )
```

```python
import functools

import jax
import jax.numpy as jnp
from jax import lax
from jax.experimental import pallas as pl
from jax.experimental.pallas import tpu as pltpu
from jax.sharding import PartitionSpec as P

PASSES = 3
KNOTS = 16


TIME_STEP = 0.15
OPTICAL_DEPTH = 3.0
UPPER_DENSITY = 6.0
AMBIENT = 0.35


def extended(cells, sides, width):
    for axis, dim in sides:
        count = lax.axis_size(axis)
        ends = count - 1
        head = lax.slice_in_dim(cells, 0, width, axis=dim)
        tail = lax.slice_in_dim(cells, cells.shape[dim] - width, cells.shape[dim], axis=dim)
        cells = jnp.concatenate(
            [
                lax.ppermute(tail, axis, [(i, (i + 1) % count) for i in range(ends)]),
                cells,
                lax.ppermute(head, axis, [((i + 1) % count, i) for i in range(ends)]),
            ],
            axis=dim,
        )
    return cells


def partner(value, axis, stride):
    mask = 2**stride
    pairs = [(source, source ^ mask) for source in range(lax.axis_size(axis))]
    return lax.ppermute(value, axis, pairs)


def diffusion_flux(center, neighbours):
    summed = jnp.zeros_like(center)
    for other in neighbours:
        change = other - center
        summed = summed + change / (1.0 + change * change)
    return center + TIME_STEP * summed


def appearance(center, neighbours, transfer_table, depth_count):
    deeper, nearer, next_row, prev_row, next_col, prev_col = neighbours
    grad_depth = (deeper - nearer) * 0.5
    grad_row = (next_row - prev_row) * 0.5
    grad_col = (next_col - prev_col) * 0.5
    shading = AMBIENT + (1.0 - AMBIENT) * jnp.abs(
        0.64 * grad_depth + 0.6 * grad_row + 0.48 * grad_col
    ) / jnp.sqrt(grad_depth * grad_depth + grad_row * grad_row + grad_col * grad_col + 0.25)
    position = center * ((KNOTS - 1) / UPPER_DENSITY)
    mixed = [jnp.zeros_like(center) for channel in range(4)]
    for knot in range(KNOTS):
        hat_weight = jnp.maximum(0.0, 1.0 - jnp.abs(position - knot))
        mixed = [
            mixed[channel] + transfer_table[channel, knot] * hat_weight for channel in range(4)
        ]
    opacity = 1.0 - jnp.exp(-mixed[3] * (OPTICAL_DEPTH / depth_count))
    colors = jnp.stack([mixed[0] * shading, mixed[1] * shading, mixed[2] * shading])
    return (colors, opacity)


def neighbour_fields(field):
    padded = extended(field, (("depth", 0), ("rows", 1)), 1)
    depth_index = lax.axis_index("depth")
    depth_count = lax.axis_size("depth")
    rows_index = lax.axis_index("rows")
    rows_count = lax.axis_size("rows")
    above = jnp.where(depth_index == 0, field[:1], padded[:1, 1:-1])
    below = jnp.where(depth_index == depth_count - 1, field[-1:], padded[-1:, 1:-1])
    first_row = jnp.where(rows_index == 0, field[:, :1], padded[1:-1, :1])
    last_row = jnp.where(rows_index == rows_count - 1, field[:, -1:], padded[1:-1, -1:])
    deeper = jnp.concatenate([field[1:], below], axis=0)
    nearer = jnp.concatenate([above, field[:-1]], axis=0)
    next_row = jnp.concatenate([field[:, 1:], last_row], axis=1)
    prev_row = jnp.concatenate([first_row, field[:, :-1]], axis=1)
    next_col = jnp.concatenate([field[:, :, 1:], field[:, :, -1:]], axis=2)
    prev_col = jnp.concatenate([field[:, :, :1], field[:, :, :-1]], axis=2)
    return (deeper, nearer, next_row, prev_row, next_col, prev_col)


def composite(front_part, back_part):
    return front_part + (1.0 - front_part[3:4]) * back_part


def per_device(density, transfer_table):
    planes_here = density.shape[0]
    band_rows = density.shape[1]
    columns = density.shape[2]
    depth_count = lax.axis_size("depth")
    depth_index = lax.axis_index("depth")
    total_planes = planes_here * depth_count
    field = density
    for sweep in range(PASSES):
        field = diffusion_flux(field, neighbour_fields(field))
    colors, opacity = appearance(field, neighbour_fields(field), transfer_table, total_planes)
    color_sum = jnp.zeros((3, band_rows, columns), jnp.float32)
    remaining = jnp.ones((band_rows, columns), jnp.float32)
    for plane in range(planes_here):
        color_sum = color_sum + remaining * opacity[plane] * colors[:, plane]
        remaining = remaining * (1.0 - opacity[plane])
    partial_value = jnp.concatenate([color_sum, (1.0 - remaining)[None]], axis=0)
    strip_rows = band_rows // depth_count
    current = partial_value.reshape(4, depth_count, strip_rows, columns)
    levels = depth_count.bit_length() - 1
    for bit in range(levels):
        blocks = current.shape[1]
        paired = current.reshape(4, blocks // 2, 2, strip_rows, columns)
        own_bit = depth_index // 2**bit % 2
        kept_half = jnp.where(own_bit == 0, paired[:, :, 0], paired[:, :, 1])
        sent_half = jnp.where(own_bit == 0, paired[:, :, 1], paired[:, :, 0])
        received = partner(sent_half, "depth", bit)
        front_part = jnp.where(own_bit == 0, kept_half, received)
        back_part = jnp.where(own_bit == 0, received, kept_half)
        current = composite(front_part, back_part)
    return current.reshape(4, strip_rows, columns)


HALO = PASSES + 1
TILE = 8
LANES = 128
UNROLL = 16
GROUP = 2


def flux(change):
    denominator = 1.0 + change * change
    guess = pl.reciprocal(denominator, approx=True)
    return change * (guess * (2.0 - denominator * guess))


def roll(cells, shift, axis):
    return pltpu.roll(cells, shift % cells.shape[axis], axis)


def lookup(entries, index):
    return jnp.take_along_axis(entries, index, axis=1)


def volume_kernel(
    depth_count,
    rows_count,
    density,
    transfer_table,
    picture,
    local,
    table,
    parcels,
    edges,
    field,
    later,
    rolled,
    side,
    knots,
    shifted,
    ending,
    load_sem,
    table_sem,
    send,
    recv,
    edge_send,
    edge_recv,
):
    planes, band, columns = local.shape
    strip = band // depth_count
    chunks = columns // LANES
    total_planes = planes * depth_count
    tall = strip + TILE
    d = lax.axis_index("depth")
    r = lax.axis_index("rows")
    next_rows = lax.rem(r + 1, rows_count)
    prev_rows = lax.rem(r + rows_count - 1, rows_count)
    order = sorted(range(1, depth_count), key=lambda k: abs(k - depth_count // 2))
    odd = lax.rem(d, 2)

    def peer_of(k):
        return lax.rem(d + k + odd * (depth_count - 2 * k), depth_count)

    load = pltpu.make_async_copy(density, local, load_sem)
    load.start()
    load_table = pltpu.make_async_copy(transfer_table, table, table_sem)
    load_table.start()

    barrier = pltpu.get_barrier_semaphore()

    def greet(depth, rows):
        pl.semaphore_signal(
            barrier, inc=1, device_id=(depth, rows), device_id_type=pl.DeviceIdType.MESH
        )

    for k in order:
        greet(peer_of(k), r)

    @pl.when(d == 0)
    def _():
        for s in range(depth_count):
            greet(s, prev_rows)

    @pl.when(d == depth_count - 1)
    def _():
        for s in range(depth_count):
            greet(s, next_rows)

    def flipped(rows, first):
        return jnp.concatenate([rows[first - i : first - i + 1] for i in range(HALO)], axis=0)

    load.wait()
    for c in range(chunks):
        lanes = slice(c * LANES, (c + 1) * LANES)
        for p in range(planes):
            first = local[p, :TILE, lanes]
            final = local[p, band - TILE :, lanes]
            at = p % 2 * HALO
            edges[depth_count, p // 2, c, at : at + HALO, :] = first[:HALO]
            edges[depth_count + 1, p // 2, c, at : at + HALO, :] = final[HALO:]
            for s in range(depth_count):
                parcels[s, c, p, :strip, :] = local[p, s * strip : (s + 1) * strip, lanes]
                if s == 0:
                    before = flipped(first, HALO - 1)
                else:
                    before = local[p, s * strip - TILE : s * strip, lanes][HALO:]
                if s == depth_count - 1:
                    after = flipped(final, TILE - 1)
                else:
                    after = local[p, (s + 1) * strip : (s + 1) * strip + TILE, lanes][:HALO]
                parcels[s, c, p, strip:, :] = jnp.concatenate([after, before], axis=0)

    def parcel(peer, g, slot):
        return pltpu.make_async_remote_copy(
            src_ref=parcels.at[peer, pl.ds(g * GROUP, GROUP)],
            dst_ref=field.at[pl.ds(g * GROUP, GROUP), pl.ds(d * planes, planes)],
            send_sem=send.at[slot, g],
            recv_sem=recv.at[d, g],
            device_id=(peer, r),
            device_id_type=pl.DeviceIdType.MESH,
        )

    def edge_copies():
        return [
            pltpu.make_async_remote_copy(
                src_ref=edges.at[depth_count + slot],
                dst_ref=edges.at[d],
                send_sem=edge_send.at[slot],
                recv_sem=edge_recv.at[d],
                device_id=(depth, rows),
                device_id_type=pl.DeviceIdType.MESH,
            )
            for slot, depth, rows in ((0, depth_count - 1, prev_rows), (1, 0, next_rows))
        ]

    def landing(ref, sem):
        return pltpu.make_async_copy(ref, ref, sem)

    pl.semaphore_wait(barrier, depth_count + 1)
    for copy in edge_copies():
        copy.start()
    for g in range(chunks // GROUP):
        for k in order:
            parcel(peer_of(k), g, k).start()

    for c in range(chunks):
        for p in range(planes):
            field[c, d * planes + p] = parcels[d, c, p]
    dark = jnp.zeros((tall, LANES), jnp.float32)

    @pl.loop(0, total_planes + 1)
    def _(z):
        for p in range(PASSES + 1):
            rolled[p, z] = dark
            side[p, z] = dark

    load_table.wait()
    entry = lax.broadcasted_iota(jnp.int32, (TILE, LANES), 1)
    for channel in range(4):
        value = jnp.zeros((TILE, LANES), jnp.float32)
        slope = jnp.zeros((TILE, LANES), jnp.float32)
        for knot in range(KNOTS - 1):
            start = table[channel, knot]
            value = jnp.where(entry == knot, start, value)
            slope = jnp.where(entry == knot, table[channel, knot + 1] - start, slope)
        knots[channel] = value
        knots[4 + channel] = slope

    lane = lax.broadcasted_iota(jnp.int32, (tall, LANES), 1)
    lane_zero = lane == 0
    upper = lax.broadcasted_iota(jnp.int32, (TILE, LANES), 0) < HALO

    def merge(c, first_plane, replaced):
        for s in range(depth_count):
            for p in range(planes):
                z = s * planes + p
                pair = edges[s, p // 2, c]
                rows = pair if p % 2 == first_plane else roll(pair, HALO, 0)
                field[c, z, strip:, :] = jnp.where(replaced, rows, field[c, z, strip:, :])

    @pl.when((d == 0) | (d == depth_count - 1))
    def _():
        for s in range(depth_count):
            landing(edges.at[s], edge_recv.at[s]).wait()

    def stage(c, p):
        inner = lane > jnp.where(c == 0, p, -1)

        def cells(z):
            here = field[c, z] if p == 0 else later[p - 1, z]
            moved = roll(here, 1, 1)
            center = jnp.where(lane_zero, rolled[p, z], moved)
            rolled[p, z] = moved
            return here, center

        def sides(z, value):
            value = jnp.where(inner, value, 0.0)
            moved = roll(value, 1, 1)
            before = jnp.where(lane_zero, side[p, z], moved)
            side[p, z] = moved
            return value, before

        return cells, sides

    def diffuse(c, p):
        cells, sides = stage(c, p)

        def plane(z, carry):
            here, center, above = carry
            here_below, center_below = cells(z + 1)
            below = flux(center_below - center)
            down = flux(roll(center, -1, 0) - center)
            right, left = sides(z, flux(here - center))
            summed = (below - above) + (down - roll(down, 1, 0)) + (right - left)
            result = center + TIME_STEP * summed
            later[p, z] = result
            return (here_below, center_below, below), result

        def step(block, carry):
            for u in range(UNROLL):
                carry, result = plane(block * UNROLL + u, carry)

            later[p, total_planes] = result
            return carry

        here, center = cells(0)
        lax.fori_loop(0, total_planes // UNROLL, step, (here, center, dark))

    def transfer(cells):
        position = cells * ((KNOTS - 1) / UPPER_DENSITY)
        index = jnp.clip(position.astype(jnp.int32), 0, KNOTS - 2)
        part = position - index.astype(jnp.float32)
        tiles = [index[i : i + TILE] for i in range(0, strip, TILE)]
        mixed = []
        for channel in range(4):
            value = jnp.concatenate([lookup(knots[channel], tile) for tile in tiles], axis=0)
            slope = jnp.concatenate([lookup(knots[4 + channel], tile) for tile in tiles], axis=0)
            mixed.append(value + part * slope)
        return mixed

    def shading_of(grad_depth, grad_row, grad_col):
        return AMBIENT + (1.0 - AMBIENT) * jnp.abs(
            0.64 * grad_depth + 0.6 * grad_row + 0.48 * grad_col
        ) * lax.rsqrt(
            grad_depth * grad_depth + grad_row * grad_row + grad_col * grad_col + 0.25
        )

    def last_columns(c):
        group = LANES // total_planes
        first_lane = lane < group
        deepest = lane >= LANES - group
        rightmost = lane % group == group - 1
        cells = field[c, total_planes - 1]
        for z in range(total_planes - 1):
            other = roll(field[c, z], (z + 1) * group, 1)
            cells = jnp.where((lane >= z * group) & (lane < (z + 1) * group), other, cells)

        def changes(cells):
            return (
                roll(cells, -group, 1) - cells,
                roll(cells, -1, 0) - cells,
                roll(cells, -1, 1) - cells,
            )

        for sweep in range(PASSES):
            below, down, right = changes(cells)
            below = jnp.where(deepest, 0.0, flux(below))
            down = flux(down)
            right = jnp.where(rightmost, 0.0, flux(right))
            summed = (
                (below - roll(below, group, 1))
                + (down - roll(down, 1, 0))
                + (right - roll(right, 1, 1))
            )
            cells = cells + TIME_STEP * summed
        below, down, right = changes(cells)
        below = jnp.where(deepest, 0.0, below)
        right = jnp.where(rightmost, 0.0, right)
        shading = shading_of(
            (below + roll(below, group, 1))[:strip] * 0.5,
            (down + roll(down, 1, 0))[:strip] * 0.5,
            (right + roll(right, 1, 1))[:strip] * 0.5,
        )
        mixed = transfer(cells[:strip])
        through = jnp.exp(mixed[3] * (-OPTICAL_DEPTH / total_planes))
        ahead = [group * 2**i for i in range((total_planes - 1).bit_length())]
        for shift in ahead:
            through = through * jnp.where(lane[:strip] < shift, 1.0, roll(through, shift, 1))
        remaining = jnp.where(first_lane[:strip], 1.0, roll(through, group, 1))
        weight = (remaining - through) * shading
        for channel in range(3):
            color = weight * mixed[channel]
            for shift in ahead:
                color = color + roll(color, shift, 1)
            ending[channel] = color
        ending[3] = 1.0 - through

    def shade(c):
        cells, sides = stage(c, PASSES)

        def plane(z, carry):
            here, center, nearer, remaining, colors = carry
            here_below, center_below = cells(z + 1)
            down = roll(center, -1, 0) - center
            right, left = sides(z, here - center)
            middle = center[:strip]
            grad_depth = (center_below[:strip] - nearer) * 0.5
            grad_row = (down + roll(down, 1, 0))[:strip] * 0.5
            grad_col = (right + left)[:strip] * 0.5
            shading = shading_of(grad_depth, grad_row, grad_col)
            mixed = transfer(middle)
            through = jnp.exp(mixed[3] * (-OPTICAL_DEPTH / total_planes))
            kept = remaining * through
            weight = (remaining - kept) * shading
            colors = tuple(colors[i] + weight * mixed[i] for i in range(3))
            return here_below, center_below, middle, kept, colors

        def step(block, carry):
            for u in range(UNROLL):
                carry = plane(block * UNROLL + u, carry)
            return carry

        here, center = cells(0)
        flat = jnp.zeros((strip, LANES), jnp.float32)
        carry = (here, center, center[:strip], jnp.ones_like(flat), (flat,) * 3)
        carry = lax.fori_loop(0, total_planes // UNROLL, step, carry)
        for channel in range(3):
            shifted[c, channel] = carry[4][channel]
        shifted[c, 3] = 1.0 - carry[3]

    @pl.loop(0, chunks)
    def _(c):
        @pl.when(lax.rem(c, GROUP) == 0)
        def _():
            for k in order:
                source = lax.rem(d + k, depth_count)
                landing(
                    field.at[pl.ds(c, GROUP), pl.ds(source * planes, planes)],
                    recv.at[source, lax.div(c, GROUP)],
                ).wait()

        @pl.when(d == 0)
        def _():
            merge(c, 1, jnp.logical_and(jnp.logical_not(upper), r > 0))

        @pl.when(d == depth_count - 1)
        def _():
            merge(c, 0, jnp.logical_and(upper, r < rows_count - 1))

        field[c, total_planes] = field[c, total_planes - 1]
        last_columns(c)
        for p in range(PASSES):
            diffuse(c, p)
        shade(c)

    early = lane[:strip] < LANES - HALO
    for c in range(chunks):
        for channel in range(4):
            beyond = roll(shifted[c + 1, channel], -HALO, 1) if c < chunks - 1 else ending[channel]
            picture[channel, :, c * LANES : (c + 1) * LANES] = jnp.where(
                early, roll(shifted[c, channel], -HALO, 1), beyond
            )

    for g in range(chunks // GROUP):
        for k in order:
            parcel(peer_of(k), g, k).wait_send()
    for copy in edge_copies():
        copy.wait_send()


def in_one_kernel(depth_count, rows_count, density, transfer_table):
    planes, band, columns = density.shape
    strip = band // depth_count
    chunks = columns // LANES
    total_planes = planes * depth_count
    tall = strip + TILE
    return pl.pallas_call(
        functools.partial(volume_kernel, depth_count, rows_count),
        out_shape=jax.ShapeDtypeStruct((4, strip, columns), jnp.float32),
        in_specs=[pl.BlockSpec(memory_space=pltpu.HBM)] * 2,
        out_specs=pl.BlockSpec(memory_space=pltpu.VMEM),
        scratch_shapes=[
            pltpu.VMEM((planes, band, columns), jnp.float32),
            pltpu.SMEM(transfer_table.shape, jnp.float32),
            pltpu.VMEM((depth_count, chunks, planes, tall, LANES), jnp.float32),
            pltpu.VMEM((depth_count + 2, planes // 2, chunks, TILE, LANES), jnp.float32),
            pltpu.VMEM((chunks, total_planes + 1, tall, LANES), jnp.float32),
            pltpu.VMEM((PASSES, total_planes + 1, tall, LANES), jnp.float32),
            pltpu.VMEM((PASSES + 1, total_planes + 1, tall, LANES), jnp.float32),
            pltpu.VMEM((PASSES + 1, total_planes + 1, tall, LANES), jnp.float32),
            pltpu.VMEM((8, TILE, LANES), jnp.float32),
            pltpu.VMEM((chunks, 4, strip, LANES), jnp.float32),
            pltpu.VMEM((4, strip, LANES), jnp.float32),
            pltpu.SemaphoreType.DMA,
            pltpu.SemaphoreType.DMA,
            pltpu.SemaphoreType.DMA((depth_count, chunks // GROUP)),
            pltpu.SemaphoreType.DMA((depth_count, chunks // GROUP)),
            pltpu.SemaphoreType.DMA((2,)),
            pltpu.SemaphoreType.DMA((depth_count,)),
        ],
        compiler_params=pltpu.CompilerParams(
            collective_id=0, has_side_effects=True, vmem_limit_bytes=24 * 2**20
        ),
    )(*[pltpu.with_memory_space_constraint(x, pltpu.HBM) for x in (density, transfer_table)])


def fits_one_kernel(depth_count, rows_count, density):
    planes, band, columns = density.shape
    strip = band // depth_count
    total_planes = planes * depth_count
    return (
        depth_count > 1
        and rows_count > 1
        and band % depth_count == 0
        and strip % TILE == 0
        and HALO * 2 == TILE
        and columns % (GROUP * LANES) == 0
        and planes % 2 == 0
        and total_planes % UNROLL == 0
        and total_planes * 2 * HALO == LANES
        and planes * columns * band + 24 * (total_planes + 1) * (strip + TILE) * LANES < 2**22
    )


def choose(density, transfer_table):
    depth_count = lax.axis_size("depth")
    rows_count = lax.axis_size("rows")
    if fits_one_kernel(depth_count, rows_count, density):
        return in_one_kernel(depth_count, rows_count, density, transfer_table)
    return per_device(density, transfer_table)


def solution(mesh):
    placed = (P("depth", "rows", None), P())
    return jax.shard_map(
        choose,
        mesh=mesh,
        in_specs=placed,
        out_specs=P(None, ("rows", "depth"), None),
        check_vma=False,
    )
```

```python
import functools

import jax
import jax.numpy as jnp
from jax import lax
from jax.experimental import pallas as pl
from jax.experimental.pallas import tpu as pltpu
from jax.sharding import PartitionSpec as P

PASSES = 3
KNOTS = 16


TIME_STEP = 0.15
OPTICAL_DEPTH = 3.0
UPPER_DENSITY = 6.0
AMBIENT = 0.35


def extended(cells, sides, width):
    for axis, dim in sides:
        count = lax.axis_size(axis)
        ends = count - 1
        head = lax.slice_in_dim(cells, 0, width, axis=dim)
        tail = lax.slice_in_dim(cells, cells.shape[dim] - width, cells.shape[dim], axis=dim)
        cells = jnp.concatenate(
            [
                lax.ppermute(tail, axis, [(i, (i + 1) % count) for i in range(ends)]),
                cells,
                lax.ppermute(head, axis, [((i + 1) % count, i) for i in range(ends)]),
            ],
            axis=dim,
        )
    return cells


def partner(value, axis, stride):
    mask = 2**stride
    pairs = [(source, source ^ mask) for source in range(lax.axis_size(axis))]
    return lax.ppermute(value, axis, pairs)


def diffusion_flux(center, neighbours):
    summed = jnp.zeros_like(center)
    for other in neighbours:
        change = other - center
        summed = summed + change / (1.0 + change * change)
    return center + TIME_STEP * summed


def appearance(center, neighbours, transfer_table, depth_count):
    deeper, nearer, next_row, prev_row, next_col, prev_col = neighbours
    grad_depth = (deeper - nearer) * 0.5
    grad_row = (next_row - prev_row) * 0.5
    grad_col = (next_col - prev_col) * 0.5
    shading = AMBIENT + (1.0 - AMBIENT) * jnp.abs(
        0.64 * grad_depth + 0.6 * grad_row + 0.48 * grad_col
    ) / jnp.sqrt(grad_depth * grad_depth + grad_row * grad_row + grad_col * grad_col + 0.25)
    position = center * ((KNOTS - 1) / UPPER_DENSITY)
    mixed = [jnp.zeros_like(center) for channel in range(4)]
    for knot in range(KNOTS):
        hat_weight = jnp.maximum(0.0, 1.0 - jnp.abs(position - knot))
        mixed = [
            mixed[channel] + transfer_table[channel, knot] * hat_weight for channel in range(4)
        ]
    opacity = 1.0 - jnp.exp(-mixed[3] * (OPTICAL_DEPTH / depth_count))
    colors = jnp.stack([mixed[0] * shading, mixed[1] * shading, mixed[2] * shading])
    return (colors, opacity)


def neighbour_fields(field):
    padded = extended(field, (("depth", 0), ("rows", 1)), 1)
    depth_index = lax.axis_index("depth")
    depth_count = lax.axis_size("depth")
    rows_index = lax.axis_index("rows")
    rows_count = lax.axis_size("rows")
    above = jnp.where(depth_index == 0, field[:1], padded[:1, 1:-1])
    below = jnp.where(depth_index == depth_count - 1, field[-1:], padded[-1:, 1:-1])
    first_row = jnp.where(rows_index == 0, field[:, :1], padded[1:-1, :1])
    last_row = jnp.where(rows_index == rows_count - 1, field[:, -1:], padded[1:-1, -1:])
    deeper = jnp.concatenate([field[1:], below], axis=0)
    nearer = jnp.concatenate([above, field[:-1]], axis=0)
    next_row = jnp.concatenate([field[:, 1:], last_row], axis=1)
    prev_row = jnp.concatenate([first_row, field[:, :-1]], axis=1)
    next_col = jnp.concatenate([field[:, :, 1:], field[:, :, -1:]], axis=2)
    prev_col = jnp.concatenate([field[:, :, :1], field[:, :, :-1]], axis=2)
    return (deeper, nearer, next_row, prev_row, next_col, prev_col)


def composite(front_part, back_part):
    return front_part + (1.0 - front_part[3:4]) * back_part


def per_device(density, transfer_table):
    planes_here = density.shape[0]
    band_rows = density.shape[1]
    columns = density.shape[2]
    depth_count = lax.axis_size("depth")
    depth_index = lax.axis_index("depth")
    total_planes = planes_here * depth_count
    field = density
    for sweep in range(PASSES):
        field = diffusion_flux(field, neighbour_fields(field))
    colors, opacity = appearance(field, neighbour_fields(field), transfer_table, total_planes)
    color_sum = jnp.zeros((3, band_rows, columns), jnp.float32)
    remaining = jnp.ones((band_rows, columns), jnp.float32)
    for plane in range(planes_here):
        color_sum = color_sum + remaining * opacity[plane] * colors[:, plane]
        remaining = remaining * (1.0 - opacity[plane])
    partial_value = jnp.concatenate([color_sum, (1.0 - remaining)[None]], axis=0)
    strip_rows = band_rows // depth_count
    current = partial_value.reshape(4, depth_count, strip_rows, columns)
    levels = depth_count.bit_length() - 1
    for bit in range(levels):
        blocks = current.shape[1]
        paired = current.reshape(4, blocks // 2, 2, strip_rows, columns)
        own_bit = depth_index // 2**bit % 2
        kept_half = jnp.where(own_bit == 0, paired[:, :, 0], paired[:, :, 1])
        sent_half = jnp.where(own_bit == 0, paired[:, :, 1], paired[:, :, 0])
        received = partner(sent_half, "depth", bit)
        front_part = jnp.where(own_bit == 0, kept_half, received)
        back_part = jnp.where(own_bit == 0, received, kept_half)
        current = composite(front_part, back_part)
    return current.reshape(4, strip_rows, columns)


HALO = PASSES + 1
TILE = 8
LANES = 128
UNROLL = 16


def flux(change):
    denominator = 1.0 + change * change
    guess = pl.reciprocal(denominator, approx=True)
    return change * (guess * (2.0 - denominator * guess))


def roll(cells, shift, axis):
    return pltpu.roll(cells, shift % cells.shape[axis], axis)


def lookup(entries, index):
    return jnp.take_along_axis(entries, index, axis=1)


def volume_kernel(
    depth_count,
    rows_count,
    density,
    transfer_table,
    picture,
    local,
    table,
    parcels,
    edges,
    field,
    later,
    rolled,
    side,
    knots,
    shifted,
    ending,
    load_sem,
    table_sem,
    send,
    recv,
    edge_send,
    edge_recv,
):
    planes, band, columns = local.shape
    strip = band // depth_count
    chunks = columns // LANES
    total_planes = planes * depth_count
    tall = strip + TILE
    d = lax.axis_index("depth")
    r = lax.axis_index("rows")
    next_rows = lax.rem(r + 1, rows_count)
    prev_rows = lax.rem(r + rows_count - 1, rows_count)
    order = sorted(range(1, depth_count), key=lambda k: abs(k - depth_count // 2))
    odd = lax.rem(d, 2)

    def peer_of(k):
        return lax.rem(d + k + odd * (depth_count - 2 * k), depth_count)

    load = pltpu.make_async_copy(density, local, load_sem)
    load.start()
    load_table = pltpu.make_async_copy(transfer_table, table, table_sem)
    load_table.start()

    barrier = pltpu.get_barrier_semaphore()

    def greet(depth, rows):
        pl.semaphore_signal(
            barrier, inc=1, device_id=(depth, rows), device_id_type=pl.DeviceIdType.MESH
        )

    for k in order:
        greet(peer_of(k), r)

    @pl.when(d == 0)
    def _():
        for s in range(depth_count):
            greet(s, prev_rows)

    @pl.when(d == depth_count - 1)
    def _():
        for s in range(depth_count):
            greet(s, next_rows)

    def flipped(rows, first):
        return jnp.concatenate([rows[first - i : first - i + 1] for i in range(HALO)], axis=0)

    load.wait()
    for c in range(chunks):
        lanes = slice(c * LANES, (c + 1) * LANES)
        for p in range(planes):
            first = local[p, :TILE, lanes]
            final = local[p, band - TILE :, lanes]
            at = p % 2 * HALO
            edges[depth_count, p // 2, c, at : at + HALO, :] = first[:HALO]
            edges[depth_count + 1, p // 2, c, at : at + HALO, :] = final[HALO:]
            for s in range(depth_count):
                parcels[s, c, p, :strip, :] = local[p, s * strip : (s + 1) * strip, lanes]
                if s == 0:
                    before = flipped(first, HALO - 1)
                else:
                    before = local[p, s * strip - TILE : s * strip, lanes][HALO:]
                if s == depth_count - 1:
                    after = flipped(final, TILE - 1)
                else:
                    after = local[p, (s + 1) * strip : (s + 1) * strip + TILE, lanes][:HALO]
                parcels[s, c, p, strip:, :] = jnp.concatenate([after, before], axis=0)

    def parcel(peer, c, slot):
        return pltpu.make_async_remote_copy(
            src_ref=parcels.at[peer, c],
            dst_ref=field.at[c, pl.ds(d * planes, planes)],
            send_sem=send.at[slot, c],
            recv_sem=recv.at[d, c],
            device_id=(peer, r),
            device_id_type=pl.DeviceIdType.MESH,
        )

    def edge_copies():
        return [
            pltpu.make_async_remote_copy(
                src_ref=edges.at[depth_count + slot],
                dst_ref=edges.at[d],
                send_sem=edge_send.at[slot],
                recv_sem=edge_recv.at[d],
                device_id=(depth, rows),
                device_id_type=pl.DeviceIdType.MESH,
            )
            for slot, depth, rows in ((0, depth_count - 1, prev_rows), (1, 0, next_rows))
        ]

    def landing(ref, sem):
        return pltpu.make_async_copy(ref, ref, sem)

    pl.semaphore_wait(barrier, depth_count + 1)
    for copy in edge_copies():
        copy.start()
    for c in range(chunks):
        for k in order:
            parcel(peer_of(k), c, k).start()

    for c in range(chunks):
        for p in range(planes):
            field[c, d * planes + p] = parcels[d, c, p]
    dark = jnp.zeros((tall, LANES), jnp.float32)

    @pl.loop(0, total_planes + 1)
    def _(z):
        for p in range(PASSES + 1):
            rolled[p, z] = dark
            side[p, z] = dark

    load_table.wait()
    entry = lax.broadcasted_iota(jnp.int32, (TILE, LANES), 1)
    for channel in range(4):
        value = jnp.zeros((TILE, LANES), jnp.float32)
        slope = jnp.zeros((TILE, LANES), jnp.float32)
        for knot in range(KNOTS - 1):
            start = table[channel, knot]
            value = jnp.where(entry == knot, start, value)
            slope = jnp.where(entry == knot, table[channel, knot + 1] - start, slope)
        knots[channel] = value
        knots[4 + channel] = slope

    lane = lax.broadcasted_iota(jnp.int32, (tall, LANES), 1)
    lane_zero = lane == 0
    upper = lax.broadcasted_iota(jnp.int32, (TILE, LANES), 0) < HALO

    def merge(c, first_plane, replaced):
        for s in range(depth_count):
            for p in range(planes):
                z = s * planes + p
                pair = edges[s, p // 2, c]
                rows = pair if p % 2 == first_plane else roll(pair, HALO, 0)
                field[c, z, strip:, :] = jnp.where(replaced, rows, field[c, z, strip:, :])

    @pl.when((d == 0) | (d == depth_count - 1))
    def _():
        for s in range(depth_count):
            landing(edges.at[s], edge_recv.at[s]).wait()

    def stage(c, p):
        inner = lane > jnp.where(c == 0, p, -1)

        def cells(z):
            here = field[c, z] if p == 0 else later[p - 1, z]
            moved = roll(here, 1, 1)
            center = jnp.where(lane_zero, rolled[p, z], moved)
            rolled[p, z] = moved
            return here, center

        def sides(z, value):
            value = jnp.where(inner, value, 0.0)
            moved = roll(value, 1, 1)
            before = jnp.where(lane_zero, side[p, z], moved)
            side[p, z] = moved
            return value, before

        return cells, sides

    def diffuse(c, p):
        cells, sides = stage(c, p)

        def plane(z, carry):
            here, center, above = carry
            here_below, center_below = cells(z + 1)
            below = flux(center_below - center)
            down = flux(roll(center, -1, 0) - center)
            right, left = sides(z, flux(here - center))
            summed = (below - above) + (down - roll(down, 1, 0)) + (right - left)
            result = center + TIME_STEP * summed
            later[p, z] = result
            return (here_below, center_below, below), result

        def step(block, carry):
            for u in range(UNROLL):
                carry, result = plane(block * UNROLL + u, carry)

            later[p, total_planes] = result
            return carry

        here, center = cells(0)
        lax.fori_loop(0, total_planes // UNROLL, step, (here, center, dark))

    def transfer(cells):
        position = cells * ((KNOTS - 1) / UPPER_DENSITY)
        index = jnp.clip(position.astype(jnp.int32), 0, KNOTS - 2)
        part = position - index.astype(jnp.float32)
        tiles = [index[i : i + TILE] for i in range(0, strip, TILE)]
        mixed = []
        for channel in range(4):
            value = jnp.concatenate([lookup(knots[channel], tile) for tile in tiles], axis=0)
            slope = jnp.concatenate([lookup(knots[4 + channel], tile) for tile in tiles], axis=0)
            mixed.append(value + part * slope)
        return mixed

    def shading_of(grad_depth, grad_row, grad_col):
        return AMBIENT + (1.0 - AMBIENT) * jnp.abs(
            0.64 * grad_depth + 0.6 * grad_row + 0.48 * grad_col
        ) * lax.rsqrt(
            grad_depth * grad_depth + grad_row * grad_row + grad_col * grad_col + 0.25
        )

    def last_columns(c):
        group = LANES // total_planes
        first_lane = lane < group
        deepest = lane >= LANES - group
        rightmost = lane % group == group - 1
        cells = field[c, total_planes - 1]
        for z in range(total_planes - 1):
            other = roll(field[c, z], (z + 1) * group, 1)
            cells = jnp.where((lane >= z * group) & (lane < (z + 1) * group), other, cells)

        def changes(cells):
            return (
                roll(cells, -group, 1) - cells,
                roll(cells, -1, 0) - cells,
                roll(cells, -1, 1) - cells,
            )

        for sweep in range(PASSES):
            below, down, right = changes(cells)
            below = jnp.where(deepest, 0.0, flux(below))
            down = flux(down)
            right = jnp.where(rightmost, 0.0, flux(right))
            summed = (
                (below - roll(below, group, 1))
                + (down - roll(down, 1, 0))
                + (right - roll(right, 1, 1))
            )
            cells = cells + TIME_STEP * summed
        below, down, right = changes(cells)
        below = jnp.where(deepest, 0.0, below)
        right = jnp.where(rightmost, 0.0, right)
        shading = shading_of(
            (below + roll(below, group, 1))[:strip] * 0.5,
            (down + roll(down, 1, 0))[:strip] * 0.5,
            (right + roll(right, 1, 1))[:strip] * 0.5,
        )
        mixed = transfer(cells[:strip])
        through = jnp.exp(mixed[3] * (-OPTICAL_DEPTH / total_planes))
        ahead = [group * 2**i for i in range((total_planes - 1).bit_length())]
        for shift in ahead:
            through = through * jnp.where(lane[:strip] < shift, 1.0, roll(through, shift, 1))
        remaining = jnp.where(first_lane[:strip], 1.0, roll(through, group, 1))
        weight = (remaining - through) * shading
        for channel in range(3):
            color = weight * mixed[channel]
            for shift in ahead:
                color = color + roll(color, shift, 1)
            ending[channel] = color
        ending[3] = 1.0 - through

    def shade(c):
        cells, sides = stage(c, PASSES)

        def plane(z, carry):
            here, center, nearer, remaining, colors = carry
            here_below, center_below = cells(z + 1)
            down = roll(center, -1, 0) - center
            right, left = sides(z, here - center)
            middle = center[:strip]
            grad_depth = (center_below[:strip] - nearer) * 0.5
            grad_row = (down + roll(down, 1, 0))[:strip] * 0.5
            grad_col = (right + left)[:strip] * 0.5
            shading = shading_of(grad_depth, grad_row, grad_col)
            mixed = transfer(middle)
            through = jnp.exp(mixed[3] * (-OPTICAL_DEPTH / total_planes))
            kept = remaining * through
            weight = (remaining - kept) * shading
            colors = tuple(colors[i] + weight * mixed[i] for i in range(3))
            return here_below, center_below, middle, kept, colors

        def step(block, carry):
            for u in range(UNROLL):
                carry = plane(block * UNROLL + u, carry)
            return carry

        here, center = cells(0)
        flat = jnp.zeros((strip, LANES), jnp.float32)
        carry = (here, center, center[:strip], jnp.ones_like(flat), (flat,) * 3)
        carry = lax.fori_loop(0, total_planes // UNROLL, step, carry)
        for channel in range(3):
            shifted[c, channel] = carry[4][channel]
        shifted[c, 3] = 1.0 - carry[3]

    early = lane[:strip] < LANES - HALO

    def write(c, channel, beyond):
        lanes = pl.ds(pl.multiple_of(c * LANES, LANES), LANES) if not isinstance(c, int) else slice(c * LANES, (c + 1) * LANES)
        own = roll(shifted[c, channel], -HALO, 1)
        picture[channel, :, lanes] = jnp.where(early, own, beyond)

    def finish_sends(c):
        for k in order:
            parcel(peer_of(k), c, k).wait_send()

    @pl.loop(0, chunks)
    def _(c):
        @pl.when(c > 0)
        def _():
            finish_sends(c - 1)

        for k in order:
            source = lax.rem(d + k, depth_count)
            landing(field.at[c, pl.ds(source * planes, planes)], recv.at[source, c]).wait()

        @pl.when(d == 0)
        def _():
            merge(c, 1, jnp.logical_and(jnp.logical_not(upper), r > 0))

        @pl.when(d == depth_count - 1)
        def _():
            merge(c, 0, jnp.logical_and(upper, r < rows_count - 1))

        field[c, total_planes] = field[c, total_planes - 1]
        last_columns(c)
        for p in range(PASSES):
            diffuse(c, p)
        shade(c)

        @pl.when(c > 0)
        def _():
            for channel in range(4):
                write(c - 1, channel, roll(shifted[c, channel], -HALO, 1))

    for channel in range(4):
        write(chunks - 1, channel, ending[channel])
    finish_sends(chunks - 1)
    for copy in edge_copies():
        copy.wait_send()


def in_one_kernel(depth_count, rows_count, density, transfer_table):
    planes, band, columns = density.shape
    strip = band // depth_count
    chunks = columns // LANES
    total_planes = planes * depth_count
    tall = strip + TILE
    return pl.pallas_call(
        functools.partial(volume_kernel, depth_count, rows_count),
        out_shape=jax.ShapeDtypeStruct((4, strip, columns), jnp.float32),
        in_specs=[pl.BlockSpec(memory_space=pltpu.HBM)] * 2,
        out_specs=pl.BlockSpec(memory_space=pltpu.VMEM),
        scratch_shapes=[
            pltpu.VMEM((planes, band, columns), jnp.float32),
            pltpu.SMEM(transfer_table.shape, jnp.float32),
            pltpu.VMEM((depth_count, chunks, planes, tall, LANES), jnp.float32),
            pltpu.VMEM((depth_count + 2, planes // 2, chunks, TILE, LANES), jnp.float32),
            pltpu.VMEM((chunks, total_planes + 1, tall, LANES), jnp.float32),
            pltpu.VMEM((PASSES, total_planes + 1, tall, LANES), jnp.float32),
            pltpu.VMEM((PASSES + 1, total_planes + 1, tall, LANES), jnp.float32),
            pltpu.VMEM((PASSES + 1, total_planes + 1, tall, LANES), jnp.float32),
            pltpu.VMEM((8, TILE, LANES), jnp.float32),
            pltpu.VMEM((chunks, 4, strip, LANES), jnp.float32),
            pltpu.VMEM((4, strip, LANES), jnp.float32),
            pltpu.SemaphoreType.DMA,
            pltpu.SemaphoreType.DMA,
            pltpu.SemaphoreType.DMA((depth_count, chunks)),
            pltpu.SemaphoreType.DMA((depth_count, chunks)),
            pltpu.SemaphoreType.DMA((2,)),
            pltpu.SemaphoreType.DMA((depth_count,)),
        ],
        compiler_params=pltpu.CompilerParams(
            collective_id=0, has_side_effects=True, vmem_limit_bytes=24 * 2**20
        ),
    )(*[pltpu.with_memory_space_constraint(x, pltpu.HBM) for x in (density, transfer_table)])


def fits_one_kernel(depth_count, rows_count, density):
    planes, band, columns = density.shape
    strip = band // depth_count
    total_planes = planes * depth_count
    return (
        depth_count > 1
        and rows_count > 1
        and band % depth_count == 0
        and strip % TILE == 0
        and HALO * 2 == TILE
        and columns % LANES == 0
        and planes % 2 == 0
        and total_planes % UNROLL == 0
        and total_planes * 2 * HALO == LANES
        and planes * columns * band + 24 * (total_planes + 1) * (strip + TILE) * LANES < 2**22
    )


def choose(density, transfer_table):
    depth_count = lax.axis_size("depth")
    rows_count = lax.axis_size("rows")
    if fits_one_kernel(depth_count, rows_count, density):
        return in_one_kernel(depth_count, rows_count, density, transfer_table)
    return per_device(density, transfer_table)


def solution(mesh):
    placed = (P("depth", "rows", None), P())
    return jax.shard_map(
        choose,
        mesh=mesh,
        in_specs=placed,
        out_specs=P(None, ("rows", "depth"), None),
        check_vma=False,
    )
```

```python
import functools

import jax
import jax.numpy as jnp
from jax import lax
from jax.experimental import pallas as pl
from jax.experimental.pallas import tpu as pltpu
from jax.sharding import PartitionSpec as P

PASSES = 3
KNOTS = 16


TIME_STEP = 0.15
OPTICAL_DEPTH = 3.0
UPPER_DENSITY = 6.0
AMBIENT = 0.35


def extended(cells, sides, width):
    for axis, dim in sides:
        count = lax.axis_size(axis)
        ends = count - 1
        head = lax.slice_in_dim(cells, 0, width, axis=dim)
        tail = lax.slice_in_dim(cells, cells.shape[dim] - width, cells.shape[dim], axis=dim)
        cells = jnp.concatenate(
            [
                lax.ppermute(tail, axis, [(i, (i + 1) % count) for i in range(ends)]),
                cells,
                lax.ppermute(head, axis, [((i + 1) % count, i) for i in range(ends)]),
            ],
            axis=dim,
        )
    return cells


def partner(value, axis, stride):
    mask = 2**stride
    pairs = [(source, source ^ mask) for source in range(lax.axis_size(axis))]
    return lax.ppermute(value, axis, pairs)


def diffusion_flux(center, neighbours):
    summed = jnp.zeros_like(center)
    for other in neighbours:
        change = other - center
        summed = summed + change / (1.0 + change * change)
    return center + TIME_STEP * summed


def appearance(center, neighbours, transfer_table, depth_count):
    deeper, nearer, next_row, prev_row, next_col, prev_col = neighbours
    grad_depth = (deeper - nearer) * 0.5
    grad_row = (next_row - prev_row) * 0.5
    grad_col = (next_col - prev_col) * 0.5
    shading = AMBIENT + (1.0 - AMBIENT) * jnp.abs(
        0.64 * grad_depth + 0.6 * grad_row + 0.48 * grad_col
    ) / jnp.sqrt(grad_depth * grad_depth + grad_row * grad_row + grad_col * grad_col + 0.25)
    position = center * ((KNOTS - 1) / UPPER_DENSITY)
    mixed = [jnp.zeros_like(center) for channel in range(4)]
    for knot in range(KNOTS):
        hat_weight = jnp.maximum(0.0, 1.0 - jnp.abs(position - knot))
        mixed = [
            mixed[channel] + transfer_table[channel, knot] * hat_weight for channel in range(4)
        ]
    opacity = 1.0 - jnp.exp(-mixed[3] * (OPTICAL_DEPTH / depth_count))
    colors = jnp.stack([mixed[0] * shading, mixed[1] * shading, mixed[2] * shading])
    return (colors, opacity)


def neighbour_fields(field):
    padded = extended(field, (("depth", 0), ("rows", 1)), 1)
    depth_index = lax.axis_index("depth")
    depth_count = lax.axis_size("depth")
    rows_index = lax.axis_index("rows")
    rows_count = lax.axis_size("rows")
    above = jnp.where(depth_index == 0, field[:1], padded[:1, 1:-1])
    below = jnp.where(depth_index == depth_count - 1, field[-1:], padded[-1:, 1:-1])
    first_row = jnp.where(rows_index == 0, field[:, :1], padded[1:-1, :1])
    last_row = jnp.where(rows_index == rows_count - 1, field[:, -1:], padded[1:-1, -1:])
    deeper = jnp.concatenate([field[1:], below], axis=0)
    nearer = jnp.concatenate([above, field[:-1]], axis=0)
    next_row = jnp.concatenate([field[:, 1:], last_row], axis=1)
    prev_row = jnp.concatenate([first_row, field[:, :-1]], axis=1)
    next_col = jnp.concatenate([field[:, :, 1:], field[:, :, -1:]], axis=2)
    prev_col = jnp.concatenate([field[:, :, :1], field[:, :, :-1]], axis=2)
    return (deeper, nearer, next_row, prev_row, next_col, prev_col)


def composite(front_part, back_part):
    return front_part + (1.0 - front_part[3:4]) * back_part


def per_device(density, transfer_table):
    planes_here = density.shape[0]
    band_rows = density.shape[1]
    columns = density.shape[2]
    depth_count = lax.axis_size("depth")
    depth_index = lax.axis_index("depth")
    total_planes = planes_here * depth_count
    field = density
    for sweep in range(PASSES):
        field = diffusion_flux(field, neighbour_fields(field))
    colors, opacity = appearance(field, neighbour_fields(field), transfer_table, total_planes)
    color_sum = jnp.zeros((3, band_rows, columns), jnp.float32)
    remaining = jnp.ones((band_rows, columns), jnp.float32)
    for plane in range(planes_here):
        color_sum = color_sum + remaining * opacity[plane] * colors[:, plane]
        remaining = remaining * (1.0 - opacity[plane])
    partial_value = jnp.concatenate([color_sum, (1.0 - remaining)[None]], axis=0)
    strip_rows = band_rows // depth_count
    current = partial_value.reshape(4, depth_count, strip_rows, columns)
    levels = depth_count.bit_length() - 1
    for bit in range(levels):
        blocks = current.shape[1]
        paired = current.reshape(4, blocks // 2, 2, strip_rows, columns)
        own_bit = depth_index // 2**bit % 2
        kept_half = jnp.where(own_bit == 0, paired[:, :, 0], paired[:, :, 1])
        sent_half = jnp.where(own_bit == 0, paired[:, :, 1], paired[:, :, 0])
        received = partner(sent_half, "depth", bit)
        front_part = jnp.where(own_bit == 0, kept_half, received)
        back_part = jnp.where(own_bit == 0, received, kept_half)
        current = composite(front_part, back_part)
    return current.reshape(4, strip_rows, columns)


HALO = PASSES + 1
TILE = 8
LANES = 128
UNROLL = 16


def flux(change):
    denominator = 1.0 + change * change
    guess = pl.reciprocal(denominator, approx=True)
    return change * (guess * (2.0 - denominator * guess))


def roll(cells, shift, axis):
    return pltpu.roll(cells, shift % cells.shape[axis], axis)


def lookup(entries, index):
    return jnp.take_along_axis(entries, index, axis=1)


def volume_kernel(
    depth_count,
    rows_count,
    density,
    transfer_table,
    picture,
    local,
    rim,
    table,
    parcels,
    edges,
    field,
    later,
    rolled,
    side,
    knots,
    shifted,
    ending,
    load_sem,
    table_sem,
    send,
    recv,
    edge_send,
    edge_recv,
):
    planes, band, columns = local.shape
    strip = band // depth_count
    chunks = columns // LANES
    total_planes = planes * depth_count
    tall = strip + TILE
    d = lax.axis_index("depth")
    r = lax.axis_index("rows")
    next_rows = lax.rem(r + 1, rows_count)
    prev_rows = lax.rem(r + rows_count - 1, rows_count)
    order = sorted(range(1, depth_count), key=lambda k: abs(k - depth_count // 2))
    odd = lax.rem(d, 2)

    def peer_of(k):
        return lax.rem(d + k + odd * (depth_count - 2 * k), depth_count)

    rims = [
        pltpu.make_async_copy(density.at[:, :TILE, :], rim.at[0], load_sem.at[chunks]),
        pltpu.make_async_copy(density.at[:, band - TILE :, :], rim.at[1], load_sem.at[chunks + 1]),
    ]
    loads = [
        pltpu.make_async_copy(
            density.at[:, :, c * LANES : (c + 1) * LANES],
            local.at[:, :, c * LANES : (c + 1) * LANES],
            load_sem.at[c],
        )
        for c in range(chunks)
    ]
    for load in rims + loads:
        load.start()
    load_table = pltpu.make_async_copy(transfer_table, table, table_sem)
    load_table.start()

    barrier = pltpu.get_barrier_semaphore()

    def greet(depth, rows):
        pl.semaphore_signal(
            barrier, inc=1, device_id=(depth, rows), device_id_type=pl.DeviceIdType.MESH
        )

    for k in order:
        greet(peer_of(k), r)

    @pl.when(d == 0)
    def _():
        for s in range(depth_count):
            greet(s, prev_rows)

    @pl.when(d == depth_count - 1)
    def _():
        for s in range(depth_count):
            greet(s, next_rows)

    def flipped(rows, first):
        return jnp.concatenate([rows[first - i : first - i + 1] for i in range(HALO)], axis=0)

    def parcel(peer, c, slot):
        return pltpu.make_async_remote_copy(
            src_ref=parcels.at[peer, c],
            dst_ref=field.at[c, pl.ds(d * planes, planes)],
            send_sem=send.at[slot, c],
            recv_sem=recv.at[d, c],
            device_id=(peer, r),
            device_id_type=pl.DeviceIdType.MESH,
        )

    def build(c):
        lanes = slice(c * LANES, (c + 1) * LANES)
        for p in range(planes):
            first = local[p, :TILE, lanes]
            final = local[p, band - TILE :, lanes]
            for s in range(depth_count):
                parcels[s, c, p, :strip, :] = local[p, s * strip : (s + 1) * strip, lanes]
                if s == 0:
                    before = flipped(first, HALO - 1)
                else:
                    before = local[p, s * strip - TILE : s * strip, lanes][HALO:]
                if s == depth_count - 1:
                    after = flipped(final, TILE - 1)
                else:
                    after = local[p, (s + 1) * strip : (s + 1) * strip + TILE, lanes][:HALO]
                parcels[s, c, p, strip:, :] = jnp.concatenate([after, before], axis=0)

    def edge_copies():
        return [
            pltpu.make_async_remote_copy(
                src_ref=edges.at[depth_count + slot],
                dst_ref=edges.at[d],
                send_sem=edge_send.at[slot],
                recv_sem=edge_recv.at[d],
                device_id=(depth, rows),
                device_id_type=pl.DeviceIdType.MESH,
            )
            for slot, depth, rows in ((0, depth_count - 1, prev_rows), (1, 0, next_rows))
        ]

    def landing(ref, sem):
        return pltpu.make_async_copy(ref, ref, sem)

    for load in rims:
        load.wait()
    for p in range(planes):
        at = p % 2 * HALO
        for c in range(chunks):
            lanes = slice(c * LANES, (c + 1) * LANES)
            edges[depth_count, p // 2, c, at : at + HALO, :] = rim[0, p, :, lanes][:HALO]
            edges[depth_count + 1, p // 2, c, at : at + HALO, :] = rim[1, p, :, lanes][HALO:]
    for c in range(chunks):
        loads[c].wait()
        build(c)
        if c == 0:
            pl.semaphore_wait(barrier, depth_count + 1)
            for copy in edge_copies():
                copy.start()
        for k in order:
            parcel(peer_of(k), c, k).start()

    for c in range(chunks):
        for p in range(planes):
            field[c, d * planes + p] = parcels[d, c, p]
    dark = jnp.zeros((tall, LANES), jnp.float32)

    @pl.loop(0, total_planes + 1)
    def _(z):
        for p in range(PASSES + 1):
            rolled[p, z] = dark
            side[p, z] = dark

    load_table.wait()
    entry = lax.broadcasted_iota(jnp.int32, (TILE, LANES), 1)
    for channel in range(4):
        value = jnp.zeros((TILE, LANES), jnp.float32)
        slope = jnp.zeros((TILE, LANES), jnp.float32)
        for knot in range(KNOTS - 1):
            start = table[channel, knot]
            value = jnp.where(entry == knot, start, value)
            slope = jnp.where(entry == knot, table[channel, knot + 1] - start, slope)
        knots[channel] = value
        knots[4 + channel] = slope

    lane = lax.broadcasted_iota(jnp.int32, (tall, LANES), 1)
    lane_zero = lane == 0
    upper = lax.broadcasted_iota(jnp.int32, (TILE, LANES), 0) < HALO

    def merge(c, first_plane, replaced):
        for s in range(depth_count):
            for p in range(planes):
                z = s * planes + p
                pair = edges[s, p // 2, c]
                rows = pair if p % 2 == first_plane else roll(pair, HALO, 0)
                field[c, z, strip:, :] = jnp.where(replaced, rows, field[c, z, strip:, :])

    @pl.when((d == 0) | (d == depth_count - 1))
    def _():
        for s in range(depth_count):
            landing(edges.at[s], edge_recv.at[s]).wait()

    def stage(c, p):
        inner = lane > jnp.where(c == 0, p, -1)

        def cells(z):
            here = field[c, z] if p == 0 else later[p - 1, z]
            moved = roll(here, 1, 1)
            center = jnp.where(lane_zero, rolled[p, z], moved)
            rolled[p, z] = moved
            return here, center

        def sides(z, value):
            value = jnp.where(inner, value, 0.0)
            moved = roll(value, 1, 1)
            before = jnp.where(lane_zero, side[p, z], moved)
            side[p, z] = moved
            return value, before

        return cells, sides

    def diffuse(c, p):
        cells, sides = stage(c, p)

        def plane(z, carry):
            here, center, above = carry
            here_below, center_below = cells(z + 1)
            below = flux(center_below - center)
            down = flux(roll(center, -1, 0) - center)
            right, left = sides(z, flux(here - center))
            summed = (below - above) + (down - roll(down, 1, 0)) + (right - left)
            result = center + TIME_STEP * summed
            later[p, z] = result
            return (here_below, center_below, below), result

        def step(block, carry):
            for u in range(UNROLL):
                carry, result = plane(block * UNROLL + u, carry)

            later[p, total_planes] = result
            return carry

        here, center = cells(0)
        lax.fori_loop(0, total_planes // UNROLL, step, (here, center, dark))

    def transfer(cells):
        position = cells * ((KNOTS - 1) / UPPER_DENSITY)
        index = jnp.clip(position.astype(jnp.int32), 0, KNOTS - 2)
        part = position - index.astype(jnp.float32)
        tiles = [index[i : i + TILE] for i in range(0, strip, TILE)]
        mixed = []
        for channel in range(4):
            value = jnp.concatenate([lookup(knots[channel], tile) for tile in tiles], axis=0)
            slope = jnp.concatenate([lookup(knots[4 + channel], tile) for tile in tiles], axis=0)
            mixed.append(value + part * slope)
        return mixed

    def shading_of(grad_depth, grad_row, grad_col):
        return AMBIENT + (1.0 - AMBIENT) * jnp.abs(
            0.64 * grad_depth + 0.6 * grad_row + 0.48 * grad_col
        ) * lax.rsqrt(
            grad_depth * grad_depth + grad_row * grad_row + grad_col * grad_col + 0.25
        )

    def last_columns(c):
        group = LANES // total_planes
        first_lane = lane < group
        deepest = lane >= LANES - group
        rightmost = lane % group == group - 1
        cells = field[c, total_planes - 1]
        for z in range(total_planes - 1):
            other = roll(field[c, z], (z + 1) * group, 1)
            cells = jnp.where((lane >= z * group) & (lane < (z + 1) * group), other, cells)

        def changes(cells):
            return (
                roll(cells, -group, 1) - cells,
                roll(cells, -1, 0) - cells,
                roll(cells, -1, 1) - cells,
            )

        for sweep in range(PASSES):
            below, down, right = changes(cells)
            below = jnp.where(deepest, 0.0, flux(below))
            down = flux(down)
            right = jnp.where(rightmost, 0.0, flux(right))
            summed = (
                (below - roll(below, group, 1))
                + (down - roll(down, 1, 0))
                + (right - roll(right, 1, 1))
            )
            cells = cells + TIME_STEP * summed
        below, down, right = changes(cells)
        below = jnp.where(deepest, 0.0, below)
        right = jnp.where(rightmost, 0.0, right)
        shading = shading_of(
            (below + roll(below, group, 1))[:strip] * 0.5,
            (down + roll(down, 1, 0))[:strip] * 0.5,
            (right + roll(right, 1, 1))[:strip] * 0.5,
        )
        mixed = transfer(cells[:strip])
        through = jnp.exp(mixed[3] * (-OPTICAL_DEPTH / total_planes))
        ahead = [group * 2**i for i in range((total_planes - 1).bit_length())]
        for shift in ahead:
            through = through * jnp.where(lane[:strip] < shift, 1.0, roll(through, shift, 1))
        remaining = jnp.where(first_lane[:strip], 1.0, roll(through, group, 1))
        weight = (remaining - through) * shading
        for channel in range(3):
            color = weight * mixed[channel]
            for shift in ahead:
                color = color + roll(color, shift, 1)
            ending[channel] = color
        ending[3] = 1.0 - through

    def shade(c):
        cells, sides = stage(c, PASSES)

        def plane(z, carry):
            here, center, nearer, remaining, colors = carry
            here_below, center_below = cells(z + 1)
            down = roll(center, -1, 0) - center
            right, left = sides(z, here - center)
            middle = center[:strip]
            grad_depth = (center_below[:strip] - nearer) * 0.5
            grad_row = (down + roll(down, 1, 0))[:strip] * 0.5
            grad_col = (right + left)[:strip] * 0.5
            shading = shading_of(grad_depth, grad_row, grad_col)
            mixed = transfer(middle)
            through = jnp.exp(mixed[3] * (-OPTICAL_DEPTH / total_planes))
            kept = remaining * through
            weight = (remaining - kept) * shading
            colors = tuple(colors[i] + weight * mixed[i] for i in range(3))
            return here_below, center_below, middle, kept, colors

        def step(block, carry):
            for u in range(UNROLL):
                carry = plane(block * UNROLL + u, carry)
            return carry

        here, center = cells(0)
        flat = jnp.zeros((strip, LANES), jnp.float32)
        carry = (here, center, center[:strip], jnp.ones_like(flat), (flat,) * 3)
        carry = lax.fori_loop(0, total_planes // UNROLL, step, carry)
        for channel in range(3):
            shifted[c, channel] = carry[4][channel]
        shifted[c, 3] = 1.0 - carry[3]

    early = lane[:strip] < LANES - HALO

    def write(c, channel, beyond):
        lanes = pl.ds(pl.multiple_of(c * LANES, LANES), LANES) if not isinstance(c, int) else slice(c * LANES, (c + 1) * LANES)
        own = roll(shifted[c, channel], -HALO, 1)
        picture[channel, :, lanes] = jnp.where(early, own, beyond)

    def finish_sends(c):
        for k in order:
            parcel(peer_of(k), c, k).wait_send()

    @pl.loop(0, chunks)
    def _(c):
        @pl.when(c > 0)
        def _():
            finish_sends(c - 1)

        for k in order:
            source = lax.rem(d + k, depth_count)
            landing(field.at[c, pl.ds(source * planes, planes)], recv.at[source, c]).wait()

        @pl.when(d == 0)
        def _():
            merge(c, 1, jnp.logical_and(jnp.logical_not(upper), r > 0))

        @pl.when(d == depth_count - 1)
        def _():
            merge(c, 0, jnp.logical_and(upper, r < rows_count - 1))

        field[c, total_planes] = field[c, total_planes - 1]
        last_columns(c)
        for p in range(PASSES):
            diffuse(c, p)
        shade(c)

        @pl.when(c > 0)
        def _():
            for channel in range(4):
                write(c - 1, channel, roll(shifted[c, channel], -HALO, 1))

    for channel in range(4):
        write(chunks - 1, channel, ending[channel])
    finish_sends(chunks - 1)
    for copy in edge_copies():
        copy.wait_send()


def in_one_kernel(depth_count, rows_count, density, transfer_table):
    planes, band, columns = density.shape
    strip = band // depth_count
    chunks = columns // LANES
    total_planes = planes * depth_count
    tall = strip + TILE
    return pl.pallas_call(
        functools.partial(volume_kernel, depth_count, rows_count),
        out_shape=jax.ShapeDtypeStruct((4, strip, columns), jnp.float32),
        in_specs=[pl.BlockSpec(memory_space=pltpu.HBM)] * 2,
        out_specs=pl.BlockSpec(memory_space=pltpu.VMEM),
        scratch_shapes=[
            pltpu.VMEM((planes, band, columns), jnp.float32),
            pltpu.VMEM((2, planes, TILE, columns), jnp.float32),
            pltpu.SMEM(transfer_table.shape, jnp.float32),
            pltpu.VMEM((depth_count, chunks, planes, tall, LANES), jnp.float32),
            pltpu.VMEM((depth_count + 2, planes // 2, chunks, TILE, LANES), jnp.float32),
            pltpu.VMEM((chunks, total_planes + 1, tall, LANES), jnp.float32),
            pltpu.VMEM((PASSES, total_planes + 1, tall, LANES), jnp.float32),
            pltpu.VMEM((PASSES + 1, total_planes + 1, tall, LANES), jnp.float32),
            pltpu.VMEM((PASSES + 1, total_planes + 1, tall, LANES), jnp.float32),
            pltpu.VMEM((8, TILE, LANES), jnp.float32),
            pltpu.VMEM((chunks, 4, strip, LANES), jnp.float32),
            pltpu.VMEM((4, strip, LANES), jnp.float32),
            pltpu.SemaphoreType.DMA((chunks + 2,)),
            pltpu.SemaphoreType.DMA,
            pltpu.SemaphoreType.DMA((depth_count, chunks)),
            pltpu.SemaphoreType.DMA((depth_count, chunks)),
            pltpu.SemaphoreType.DMA((2,)),
            pltpu.SemaphoreType.DMA((depth_count,)),
        ],
        compiler_params=pltpu.CompilerParams(
            collective_id=0, has_side_effects=True, vmem_limit_bytes=24 * 2**20
        ),
    )(*[pltpu.with_memory_space_constraint(x, pltpu.HBM) for x in (density, transfer_table)])


def fits_one_kernel(depth_count, rows_count, density):
    planes, band, columns = density.shape
    strip = band // depth_count
    total_planes = planes * depth_count
    return (
        depth_count > 1
        and rows_count > 1
        and band % depth_count == 0
        and strip % TILE == 0
        and HALO * 2 == TILE
        and columns % LANES == 0
        and planes % 2 == 0
        and total_planes % UNROLL == 0
        and total_planes * 2 * HALO == LANES
        and planes * columns * band + 24 * (total_planes + 1) * (strip + TILE) * LANES < 2**22
    )


def choose(density, transfer_table):
    depth_count = lax.axis_size("depth")
    rows_count = lax.axis_size("rows")
    if fits_one_kernel(depth_count, rows_count, density):
        return in_one_kernel(depth_count, rows_count, density, transfer_table)
    return per_device(density, transfer_table)


def solution(mesh):
    placed = (P("depth", "rows", None), P())
    return jax.shard_map(
        choose,
        mesh=mesh,
        in_specs=placed,
        out_specs=P(None, ("rows", "depth"), None),
        check_vma=False,
    )
```

```python
import functools

import jax
import jax.numpy as jnp
from jax import lax
from jax.experimental import pallas as pl
from jax.experimental.pallas import tpu as pltpu
from jax.sharding import PartitionSpec as P

PASSES = 3
KNOTS = 16


TIME_STEP = 0.15
OPTICAL_DEPTH = 3.0
UPPER_DENSITY = 6.0
AMBIENT = 0.35


def extended(cells, sides, width):
    for axis, dim in sides:
        count = lax.axis_size(axis)
        ends = count - 1
        head = lax.slice_in_dim(cells, 0, width, axis=dim)
        tail = lax.slice_in_dim(cells, cells.shape[dim] - width, cells.shape[dim], axis=dim)
        cells = jnp.concatenate(
            [
                lax.ppermute(tail, axis, [(i, (i + 1) % count) for i in range(ends)]),
                cells,
                lax.ppermute(head, axis, [((i + 1) % count, i) for i in range(ends)]),
            ],
            axis=dim,
        )
    return cells


def partner(value, axis, stride):
    mask = 2**stride
    pairs = [(source, source ^ mask) for source in range(lax.axis_size(axis))]
    return lax.ppermute(value, axis, pairs)


def diffusion_flux(center, neighbours):
    summed = jnp.zeros_like(center)
    for other in neighbours:
        change = other - center
        summed = summed + change / (1.0 + change * change)
    return center + TIME_STEP * summed


def appearance(center, neighbours, transfer_table, depth_count):
    deeper, nearer, next_row, prev_row, next_col, prev_col = neighbours
    grad_depth = (deeper - nearer) * 0.5
    grad_row = (next_row - prev_row) * 0.5
    grad_col = (next_col - prev_col) * 0.5
    shading = AMBIENT + (1.0 - AMBIENT) * jnp.abs(
        0.64 * grad_depth + 0.6 * grad_row + 0.48 * grad_col
    ) / jnp.sqrt(grad_depth * grad_depth + grad_row * grad_row + grad_col * grad_col + 0.25)
    position = center * ((KNOTS - 1) / UPPER_DENSITY)
    mixed = [jnp.zeros_like(center) for channel in range(4)]
    for knot in range(KNOTS):
        hat_weight = jnp.maximum(0.0, 1.0 - jnp.abs(position - knot))
        mixed = [
            mixed[channel] + transfer_table[channel, knot] * hat_weight for channel in range(4)
        ]
    opacity = 1.0 - jnp.exp(-mixed[3] * (OPTICAL_DEPTH / depth_count))
    colors = jnp.stack([mixed[0] * shading, mixed[1] * shading, mixed[2] * shading])
    return (colors, opacity)


def neighbour_fields(field):
    padded = extended(field, (("depth", 0), ("rows", 1)), 1)
    depth_index = lax.axis_index("depth")
    depth_count = lax.axis_size("depth")
    rows_index = lax.axis_index("rows")
    rows_count = lax.axis_size("rows")
    above = jnp.where(depth_index == 0, field[:1], padded[:1, 1:-1])
    below = jnp.where(depth_index == depth_count - 1, field[-1:], padded[-1:, 1:-1])
    first_row = jnp.where(rows_index == 0, field[:, :1], padded[1:-1, :1])
    last_row = jnp.where(rows_index == rows_count - 1, field[:, -1:], padded[1:-1, -1:])
    deeper = jnp.concatenate([field[1:], below], axis=0)
    nearer = jnp.concatenate([above, field[:-1]], axis=0)
    next_row = jnp.concatenate([field[:, 1:], last_row], axis=1)
    prev_row = jnp.concatenate([first_row, field[:, :-1]], axis=1)
    next_col = jnp.concatenate([field[:, :, 1:], field[:, :, -1:]], axis=2)
    prev_col = jnp.concatenate([field[:, :, :1], field[:, :, :-1]], axis=2)
    return (deeper, nearer, next_row, prev_row, next_col, prev_col)


def composite(front_part, back_part):
    return front_part + (1.0 - front_part[3:4]) * back_part


def per_device(density, transfer_table):
    planes_here = density.shape[0]
    band_rows = density.shape[1]
    columns = density.shape[2]
    depth_count = lax.axis_size("depth")
    depth_index = lax.axis_index("depth")
    total_planes = planes_here * depth_count
    field = density
    for sweep in range(PASSES):
        field = diffusion_flux(field, neighbour_fields(field))
    colors, opacity = appearance(field, neighbour_fields(field), transfer_table, total_planes)
    color_sum = jnp.zeros((3, band_rows, columns), jnp.float32)
    remaining = jnp.ones((band_rows, columns), jnp.float32)
    for plane in range(planes_here):
        color_sum = color_sum + remaining * opacity[plane] * colors[:, plane]
        remaining = remaining * (1.0 - opacity[plane])
    partial_value = jnp.concatenate([color_sum, (1.0 - remaining)[None]], axis=0)
    strip_rows = band_rows // depth_count
    current = partial_value.reshape(4, depth_count, strip_rows, columns)
    levels = depth_count.bit_length() - 1
    for bit in range(levels):
        blocks = current.shape[1]
        paired = current.reshape(4, blocks // 2, 2, strip_rows, columns)
        own_bit = depth_index // 2**bit % 2
        kept_half = jnp.where(own_bit == 0, paired[:, :, 0], paired[:, :, 1])
        sent_half = jnp.where(own_bit == 0, paired[:, :, 1], paired[:, :, 0])
        received = partner(sent_half, "depth", bit)
        front_part = jnp.where(own_bit == 0, kept_half, received)
        back_part = jnp.where(own_bit == 0, received, kept_half)
        current = composite(front_part, back_part)
    return current.reshape(4, strip_rows, columns)


HALO = PASSES + 1
TILE = 8
LANES = 128
UNROLL = 16


def flux(change):
    denominator = 1.0 + change * change
    guess = pl.reciprocal(denominator, approx=True)
    return change * (guess * (2.0 - denominator * guess))


def roll(cells, shift, axis):
    return pltpu.roll(cells, shift % cells.shape[axis], axis)


def lookup(entries, index):
    return jnp.take_along_axis(entries, index, axis=1)


def volume_kernel(
    depth_count,
    rows_count,
    density,
    transfer_table,
    picture,
    local,
    table,
    parcels,
    edges,
    field,
    later,
    rolled,
    side,
    knots,
    shifted,
    ending,
    load_sem,
    table_sem,
    send,
    recv,
    edge_send,
    edge_recv,
):
    planes, band, columns = local.shape
    strip = band // depth_count
    chunks = columns // LANES
    total_planes = planes * depth_count
    tall = strip + TILE
    d = lax.axis_index("depth")
    r = lax.axis_index("rows")
    next_rows = lax.rem(r + 1, rows_count)
    prev_rows = lax.rem(r + rows_count - 1, rows_count)
    far = sorted(range(1, depth_count), key=lambda k: abs(k - depth_count // 2))
    order = [far[i // 2] if i % 2 == 0 else far[-1 - i // 2] for i in range(depth_count - 1)]
    odd = lax.rem(d, 2)

    def peer_of(k):
        return lax.rem(d + k + odd * (depth_count - 2 * k), depth_count)

    load = pltpu.make_async_copy(density, local, load_sem)
    load.start()
    load_table = pltpu.make_async_copy(transfer_table, table, table_sem)
    load_table.start()

    barrier = pltpu.get_barrier_semaphore()

    def greet(depth, rows):
        pl.semaphore_signal(
            barrier, inc=1, device_id=(depth, rows), device_id_type=pl.DeviceIdType.MESH
        )

    for k in order:
        greet(peer_of(k), r)

    @pl.when(d == 0)
    def _():
        for s in range(depth_count):
            greet(s, prev_rows)

    @pl.when(d == depth_count - 1)
    def _():
        for s in range(depth_count):
            greet(s, next_rows)

    def flipped(rows, first):
        return jnp.concatenate([rows[first - i : first - i + 1] for i in range(HALO)], axis=0)

    load.wait()
    for c in range(chunks):
        lanes = slice(c * LANES, (c + 1) * LANES)
        for p in range(planes):
            first = local[p, :TILE, lanes]
            final = local[p, band - TILE :, lanes]
            at = p % 2 * HALO
            edges[depth_count, p // 2, c, at : at + HALO, :] = first[:HALO]
            edges[depth_count + 1, p // 2, c, at : at + HALO, :] = final[HALO:]
            for s in range(depth_count):
                parcels[s, c, p, :strip, :] = local[p, s * strip : (s + 1) * strip, lanes]
                if s == 0:
                    before = flipped(first, HALO - 1)
                else:
                    before = local[p, s * strip - TILE : s * strip, lanes][HALO:]
                if s == depth_count - 1:
                    after = flipped(final, TILE - 1)
                else:
                    after = local[p, (s + 1) * strip : (s + 1) * strip + TILE, lanes][:HALO]
                parcels[s, c, p, strip:, :] = jnp.concatenate([after, before], axis=0)

    def parcel(peer, c, slot):
        return pltpu.make_async_remote_copy(
            src_ref=parcels.at[peer, c],
            dst_ref=field.at[c, pl.ds(d * planes, planes)],
            send_sem=send.at[slot, c],
            recv_sem=recv.at[d, c],
            device_id=(peer, r),
            device_id_type=pl.DeviceIdType.MESH,
        )

    def edge_copies():
        return [
            pltpu.make_async_remote_copy(
                src_ref=edges.at[depth_count + slot],
                dst_ref=edges.at[d],
                send_sem=edge_send.at[slot],
                recv_sem=edge_recv.at[d],
                device_id=(depth, rows),
                device_id_type=pl.DeviceIdType.MESH,
            )
            for slot, depth, rows in ((0, depth_count - 1, prev_rows), (1, 0, next_rows))
        ]

    def landing(ref, sem):
        return pltpu.make_async_copy(ref, ref, sem)

    pl.semaphore_wait(barrier, depth_count + 1)
    for copy in edge_copies():
        copy.start()
    for c in range(chunks):
        for k in order:
            parcel(peer_of(k), c, k).start()

    for c in range(chunks):
        for p in range(planes):
            field[c, d * planes + p] = parcels[d, c, p]
    dark = jnp.zeros((tall, LANES), jnp.float32)

    @pl.loop(0, total_planes + 1)
    def _(z):
        for p in range(PASSES + 1):
            rolled[p, z] = dark
            side[p, z] = dark

    load_table.wait()
    entry = lax.broadcasted_iota(jnp.int32, (TILE, LANES), 1)
    for channel in range(4):
        value = jnp.zeros((TILE, LANES), jnp.float32)
        slope = jnp.zeros((TILE, LANES), jnp.float32)
        for knot in range(KNOTS - 1):
            start = table[channel, knot]
            value = jnp.where(entry == knot, start, value)
            slope = jnp.where(entry == knot, table[channel, knot + 1] - start, slope)
        knots[channel] = value
        knots[4 + channel] = slope

    lane = lax.broadcasted_iota(jnp.int32, (tall, LANES), 1)
    lane_zero = lane == 0
    upper = lax.broadcasted_iota(jnp.int32, (TILE, LANES), 0) < HALO

    def merge(c, first_plane, replaced):
        for s in range(depth_count):
            for p in range(planes):
                z = s * planes + p
                pair = edges[s, p // 2, c]
                rows = pair if p % 2 == first_plane else roll(pair, HALO, 0)
                field[c, z, strip:, :] = jnp.where(replaced, rows, field[c, z, strip:, :])

    @pl.when((d == 0) | (d == depth_count - 1))
    def _():
        for s in range(depth_count):
            landing(edges.at[s], edge_recv.at[s]).wait()

    def stage(c, p):
        inner = lane > jnp.where(c == 0, p, -1)

        def cells(z):
            here = field[c, z] if p == 0 else later[p - 1, z]
            moved = roll(here, 1, 1)
            center = jnp.where(lane_zero, rolled[p, z], moved)
            rolled[p, z] = moved
            return here, center

        def sides(z, value):
            value = jnp.where(inner, value, 0.0)
            moved = roll(value, 1, 1)
            before = jnp.where(lane_zero, side[p, z], moved)
            side[p, z] = moved
            return value, before

        return cells, sides

    def diffuse(c, p):
        cells, sides = stage(c, p)

        def plane(z, carry):
            here, center, above = carry
            here_below, center_below = cells(z + 1)
            below = flux(center_below - center)
            down = flux(roll(center, -1, 0) - center)
            right, left = sides(z, flux(here - center))
            summed = (below - above) + (down - roll(down, 1, 0)) + (right - left)
            result = center + TIME_STEP * summed
            later[p, z] = result
            return (here_below, center_below, below), result

        def step(block, carry):
            for u in range(UNROLL):
                carry, result = plane(block * UNROLL + u, carry)

            later[p, total_planes] = result
            return carry

        here, center = cells(0)
        lax.fori_loop(0, total_planes // UNROLL, step, (here, center, dark))

    def transfer(cells):
        position = cells * ((KNOTS - 1) / UPPER_DENSITY)
        index = jnp.clip(position.astype(jnp.int32), 0, KNOTS - 2)
        part = position - index.astype(jnp.float32)
        tiles = [index[i : i + TILE] for i in range(0, strip, TILE)]
        mixed = []
        for channel in range(4):
            value = jnp.concatenate([lookup(knots[channel], tile) for tile in tiles], axis=0)
            slope = jnp.concatenate([lookup(knots[4 + channel], tile) for tile in tiles], axis=0)
            mixed.append(value + part * slope)
        return mixed

    def shading_of(grad_depth, grad_row, grad_col):
        return AMBIENT + (1.0 - AMBIENT) * jnp.abs(
            0.64 * grad_depth + 0.6 * grad_row + 0.48 * grad_col
        ) * lax.rsqrt(
            grad_depth * grad_depth + grad_row * grad_row + grad_col * grad_col + 0.25
        )

    def last_columns(c):
        group = LANES // total_planes
        first_lane = lane < group
        deepest = lane >= LANES - group
        rightmost = lane % group == group - 1
        cells = field[c, total_planes - 1]
        for z in range(total_planes - 1):
            other = roll(field[c, z], (z + 1) * group, 1)
            cells = jnp.where((lane >= z * group) & (lane < (z + 1) * group), other, cells)

        def changes(cells):
            return (
                roll(cells, -group, 1) - cells,
                roll(cells, -1, 0) - cells,
                roll(cells, -1, 1) - cells,
            )

        for sweep in range(PASSES):
            below, down, right = changes(cells)
            below = jnp.where(deepest, 0.0, flux(below))
            down = flux(down)
            right = jnp.where(rightmost, 0.0, flux(right))
            summed = (
                (below - roll(below, group, 1))
                + (down - roll(down, 1, 0))
                + (right - roll(right, 1, 1))
            )
            cells = cells + TIME_STEP * summed
        below, down, right = changes(cells)
        below = jnp.where(deepest, 0.0, below)
        right = jnp.where(rightmost, 0.0, right)
        shading = shading_of(
            (below + roll(below, group, 1))[:strip] * 0.5,
            (down + roll(down, 1, 0))[:strip] * 0.5,
            (right + roll(right, 1, 1))[:strip] * 0.5,
        )
        mixed = transfer(cells[:strip])
        through = jnp.exp(mixed[3] * (-OPTICAL_DEPTH / total_planes))
        ahead = [group * 2**i for i in range((total_planes - 1).bit_length())]
        for shift in ahead:
            through = through * jnp.where(lane[:strip] < shift, 1.0, roll(through, shift, 1))
        remaining = jnp.where(first_lane[:strip], 1.0, roll(through, group, 1))
        weight = (remaining - through) * shading
        for channel in range(3):
            color = weight * mixed[channel]
            for shift in ahead:
                color = color + roll(color, shift, 1)
            ending[channel] = color
        ending[3] = 1.0 - through

    def shade(c):
        cells, sides = stage(c, PASSES)

        def plane(z, carry):
            here, center, nearer, remaining, colors = carry
            here_below, center_below = cells(z + 1)
            down = roll(center, -1, 0) - center
            right, left = sides(z, here - center)
            middle = center[:strip]
            grad_depth = (center_below[:strip] - nearer) * 0.5
            grad_row = (down + roll(down, 1, 0))[:strip] * 0.5
            grad_col = (right + left)[:strip] * 0.5
            shading = shading_of(grad_depth, grad_row, grad_col)
            mixed = transfer(middle)
            through = jnp.exp(mixed[3] * (-OPTICAL_DEPTH / total_planes))
            kept = remaining * through
            weight = (remaining - kept) * shading
            colors = tuple(colors[i] + weight * mixed[i] for i in range(3))
            return here_below, center_below, middle, kept, colors

        def step(block, carry):
            for u in range(UNROLL):
                carry = plane(block * UNROLL + u, carry)
            return carry

        here, center = cells(0)
        flat = jnp.zeros((strip, LANES), jnp.float32)
        carry = (here, center, center[:strip], jnp.ones_like(flat), (flat,) * 3)
        carry = lax.fori_loop(0, total_planes // UNROLL, step, carry)
        for channel in range(3):
            shifted[c, channel] = carry[4][channel]
        shifted[c, 3] = 1.0 - carry[3]

    early = lane[:strip] < LANES - HALO

    def write(c, channel, beyond):
        lanes = pl.ds(pl.multiple_of(c * LANES, LANES), LANES) if not isinstance(c, int) else slice(c * LANES, (c + 1) * LANES)
        own = roll(shifted[c, channel], -HALO, 1)
        picture[channel, :, lanes] = jnp.where(early, own, beyond)

    def finish_sends(c):
        for k in order:
            parcel(peer_of(k), c, k).wait_send()

    @pl.loop(0, chunks)
    def _(c):
        @pl.when(c > 0)
        def _():
            finish_sends(c - 1)

        for k in order:
            source = lax.rem(d + k, depth_count)
            landing(field.at[c, pl.ds(source * planes, planes)], recv.at[source, c]).wait()

        @pl.when(d == 0)
        def _():
            merge(c, 1, jnp.logical_and(jnp.logical_not(upper), r > 0))

        @pl.when(d == depth_count - 1)
        def _():
            merge(c, 0, jnp.logical_and(upper, r < rows_count - 1))

        field[c, total_planes] = field[c, total_planes - 1]
        last_columns(c)
        for p in range(PASSES):
            diffuse(c, p)
        shade(c)

        @pl.when(c > 0)
        def _():
            for channel in range(4):
                write(c - 1, channel, roll(shifted[c, channel], -HALO, 1))

    for channel in range(4):
        write(chunks - 1, channel, ending[channel])
    finish_sends(chunks - 1)
    for copy in edge_copies():
        copy.wait_send()


def in_one_kernel(depth_count, rows_count, density, transfer_table):
    planes, band, columns = density.shape
    strip = band // depth_count
    chunks = columns // LANES
    total_planes = planes * depth_count
    tall = strip + TILE
    return pl.pallas_call(
        functools.partial(volume_kernel, depth_count, rows_count),
        out_shape=jax.ShapeDtypeStruct((4, strip, columns), jnp.float32),
        in_specs=[pl.BlockSpec(memory_space=pltpu.HBM)] * 2,
        out_specs=pl.BlockSpec(memory_space=pltpu.VMEM),
        scratch_shapes=[
            pltpu.VMEM((planes, band, columns), jnp.float32),
            pltpu.SMEM(transfer_table.shape, jnp.float32),
            pltpu.VMEM((depth_count, chunks, planes, tall, LANES), jnp.float32),
            pltpu.VMEM((depth_count + 2, planes // 2, chunks, TILE, LANES), jnp.float32),
            pltpu.VMEM((chunks, total_planes + 1, tall, LANES), jnp.float32),
            pltpu.VMEM((PASSES, total_planes + 1, tall, LANES), jnp.float32),
            pltpu.VMEM((PASSES + 1, total_planes + 1, tall, LANES), jnp.float32),
            pltpu.VMEM((PASSES + 1, total_planes + 1, tall, LANES), jnp.float32),
            pltpu.VMEM((8, TILE, LANES), jnp.float32),
            pltpu.VMEM((chunks, 4, strip, LANES), jnp.float32),
            pltpu.VMEM((4, strip, LANES), jnp.float32),
            pltpu.SemaphoreType.DMA,
            pltpu.SemaphoreType.DMA,
            pltpu.SemaphoreType.DMA((depth_count, chunks)),
            pltpu.SemaphoreType.DMA((depth_count, chunks)),
            pltpu.SemaphoreType.DMA((2,)),
            pltpu.SemaphoreType.DMA((depth_count,)),
        ],
        compiler_params=pltpu.CompilerParams(
            collective_id=0, has_side_effects=True, vmem_limit_bytes=24 * 2**20
        ),
    )(*[pltpu.with_memory_space_constraint(x, pltpu.HBM) for x in (density, transfer_table)])


def fits_one_kernel(depth_count, rows_count, density):
    planes, band, columns = density.shape
    strip = band // depth_count
    total_planes = planes * depth_count
    return (
        depth_count > 1
        and rows_count > 1
        and band % depth_count == 0
        and strip % TILE == 0
        and HALO * 2 == TILE
        and columns % LANES == 0
        and planes % 2 == 0
        and total_planes % UNROLL == 0
        and total_planes * 2 * HALO == LANES
        and planes * columns * band + 24 * (total_planes + 1) * (strip + TILE) * LANES < 2**22
    )


def choose(density, transfer_table):
    depth_count = lax.axis_size("depth")
    rows_count = lax.axis_size("rows")
    if fits_one_kernel(depth_count, rows_count, density):
        return in_one_kernel(depth_count, rows_count, density, transfer_table)
    return per_device(density, transfer_table)


def solution(mesh):
    placed = (P("depth", "rows", None), P())
    return jax.shard_map(
        choose,
        mesh=mesh,
        in_specs=placed,
        out_specs=P(None, ("rows", "depth"), None),
        check_vma=False,
    )
```
